512 devices in a mesh: mem: 16 (over y, core), reg: 32 (over z, x).
Axes of the slice: x: 4, y: 8, z: 8, core: 2. Of those that a mesh axis runs over, the one named last changes fastest.
Arguments:
- background: bfloat16 [256, 16, 65536], P('mem', None, 'reg'), may hold values from -6 to 6
- observations: float32 [32, 32, 384], P('reg', 'mem'), may hold values from -6 to 6
- obs_coef: float32 [32, 32, 384], P('reg', 'mem'), may hold values from 0.5 to 1.5
- obs_rinv: float32 [32, 32, 384], P('reg', 'mem'), may hold values from 0.1 to 2
- obs_site: int32 [32, 32, 384], P('reg', 'mem'), may hold values from 0 to 1023
- obs_count: int32 [32, 32], P('reg', 'mem'), may hold values from 1 to 384, as said below
- neighbours: int32 [32, 32, 5], P('reg', 'mem'), may hold values from 0 to 8, as said below
Outputs:
- analysis: bfloat16 [256, 16, 65536], P('mem', None, 'reg')
The draws below stay inside these ranges and needn't reach their ends.
Inputs may be any that keep to these rules, and one draw needn't show every extreme that they name: `obs_count`: block counts are uneven across regions; some block has all 384 slots live in every draw. `neighbours`: each row holds distinct codes, never 4; codes 0 and 8 appear in every draw.
All inputs are finite; a program needn't handle non-finite values. Where the reference program divides by a largest or mean magnitude, that divisor is 1e-20 or more.
Results may differ from the reference program's by a relative error of at most 0.009.
Values may be sent and summed in bfloat16 or wider, within the bound.
A program may use at most 64 MiB of HBM per device.

```python
import math
import jax
import jax.numpy as jnp
from jax import lax

K = 256
V = 16
BCOL = 64
OBS = 384
NNB = 5
NS_ITERS = 4
BLK_REG = 32
NREG = 32
NCOL = 65536


def draw_obs_count(key, part):
    key = jax.random.fold_in(key, 11)
    first_key, second_key = jax.random.split(key)
    factor = jax.random.randint(first_key, (NREG, 1), 1, 5)
    raw_draw = jax.random.randint(second_key, (NREG, BLK_REG), 0, OBS)
    counted = jnp.minimum(OBS, OBS // 8 + raw_draw * factor // 4)
    counted = jnp.maximum(counted, 1)
    return counted.at[0, 0].set(OBS).astype(jnp.int32)


def draw_neighbours(key, part):
    key = jax.random.fold_in(key, 23)
    scores = jax.random.randint(key, (NREG, BLK_REG, 8), 0, 1 << 20) * 8 + jnp.arange(8, dtype=jnp.int32)
    picked = jnp.argsort(scores, axis=-1)[..., :NNB].astype(jnp.int32)
    codes = picked + (picked >= 4).astype(jnp.int32)
    return codes.at[0, 0].set(jnp.array([0, 8, 1, 2, 3], jnp.int32)).astype(jnp.int32)


def set_ends(values, rng, low, high):
    index_at = [jax.random.randint(jax.random.fold_in(rng, axis), (), 0, length) for axis, length in enumerate(values.shape)]
    longest = values.shape.index(max(values.shape))
    neighbour = index_at[:longest] + [(index_at[longest] + 1) % values.shape[longest]] + index_at[longest + 1:]
    return values.at[tuple(index_at)].set(low).at[tuple(neighbour)].set(high)


def shard_levels(key, extent, cuts, least, high):
    gain = 1.0
    for position, shards_of in cuts:
        steps = jax.random.uniform(jax.random.fold_in(jax.random.fold_in(key, 6), position), (shards_of,), jnp.float32, least / len(cuts), high / len(cuts))
        gain = gain * jnp.repeat(jnp.exp(steps), extent[position] // shards_of).reshape((-1,) + (1,) * (len(extent) - 1 - position))
    return gain


def gaussian(rng, extent, scale, bound, cuts=(), kind=jnp.bfloat16):
    entries = jax.random.normal(rng, extent, jnp.float32) * scale
    if len(cuts) > 0:
        entries = shard_levels(rng, extent, cuts, -0.22, 0.18) * entries
    return jnp.clip(entries, min=-bound, max=bound).astype(kind)


def setup_inputs(seed: int = 0) -> dict:
    key_of = jax.random.split(jax.random.key(seed), 8)
    background = gaussian(key_of[0], (K, V, NCOL), 1.0, 6.0, ((0, 16), (2, 32)))
    observations = gaussian(key_of[1], (NREG, BLK_REG, OBS), 1.0, 6.0, ((0, 32), (1, 16)), jnp.float32)
    obs_coef = jnp.clip(0.5 + 1.0 * jax.random.uniform(key_of[2], (NREG, BLK_REG, OBS), jnp.float32) ** shard_levels(key_of[2], (NREG, BLK_REG, OBS), ((0, 32), (1, 16)), -0.2, 0.2), 0.5, 1.5)
    obs_rinv = jnp.clip(jnp.exp(math.log(2.0) - 2.9957323 * jax.random.uniform(key_of[3], (NREG, BLK_REG, OBS), jnp.float32) ** shard_levels(key_of[3], (NREG, BLK_REG, OBS), ((0, 32), (1, 16)), -0.2, 0.2)), 0.1, 2.0)
    obs_site = set_ends(jax.random.randint(key_of[4], (NREG, BLK_REG, OBS), 0, V * BCOL), jax.random.fold_in(key_of[4], 1), 0, (V * BCOL) - 1).astype(jnp.int32)
    obs_count = draw_obs_count(jax.random.fold_in(key_of[7], 71), 0)
    neighbours = draw_neighbours(jax.random.fold_in(key_of[7], 71), 0)
    return dict(background=background, observations=observations, obs_coef=obs_coef, obs_rinv=obs_rinv, obs_site=obs_site, obs_count=obs_count, neighbours=neighbours)


def local_obs(block, obs_site, obs_coef, obs_rinv, obs_count, observed):
    widened = block.astype(jnp.float32)
    mean_state = lax.optimization_barrier(jnp.mean(widened, axis=0))
    spread = (widened - mean_state).astype(jnp.bfloat16)
    predicted = obs_coef * jnp.take(widened, obs_site, axis=1)
    mean_pred = lax.optimization_barrier(jnp.mean(predicted, axis=0))
    keep = (jnp.arange(obs_site.shape[0], dtype=jnp.int32) < obs_count).astype(jnp.float32)
    weight_root = jnp.sqrt(obs_rinv) * keep
    scaled = (weight_root * (predicted - mean_pred)).astype(jnp.bfloat16)
    misfit = weight_root * (observed - mean_pred)
    return (mean_state, spread, scaled, misfit)

def newton_root(matrix):
    identity = jnp.eye(matrix.shape[-1], dtype=jnp.float32)
    current = matrix
    inverse = jnp.broadcast_to(identity, matrix.shape)
    for _ in range(NS_ITERS):
        middle = 1.5 * identity - 0.5 * jnp.matmul(inverse, current, precision=lax.Precision.HIGHEST)
        current = jnp.matmul(current, middle, precision=lax.Precision.HIGHEST)
        inverse = jnp.matmul(middle, inverse, precision=lax.Precision.HIGHEST)
    return inverse

def transform(system, drive, ensemble):
    row_scale = lax.optimization_barrier(jnp.max(lax.optimization_barrier(jnp.sum(jnp.abs(system), axis=-1)), axis=-1))
    half = newton_root(system / row_scale[..., None, None]) / jnp.sqrt(row_scale)[..., None, None]
    inner_part = jnp.matmul(half, drive[..., None], precision=lax.Precision.HIGHEST)
    mean_weight = jnp.matmul(half, inner_part, precision=lax.Precision.HIGHEST)[..., 0]
    weights = jnp.sqrt(jnp.float32(ensemble - 1)) * half + mean_weight[..., :, None]
    return weights.astype(jnp.bfloat16)

def reference(background, observations, obs_coef, obs_rinv, obs_site, obs_count, neighbours):
    ensemble = background.shape[0]
    blocks = background.reshape(ensemble, V, NREG, BLK_REG, BCOL).transpose(2, 3, 0, 1, 4).reshape(NREG, BLK_REG, ensemble, V * BCOL)

    def first_pass(packed):
        return jax.vmap(local_obs)(*packed)
    mean_state, spread, scaled, misfit = lax.map(first_pass, (blocks, obs_site, obs_coef, obs_rinv, obs_count, observations))

    def block_gram(packed):
        wide_z = packed[0].astype(jnp.float32)
        gram = jnp.einsum('bko,blo->bkl', wide_z, wide_z, precision=lax.Precision.HIGHEST)
        drive_part = jnp.einsum('bko,bo->bk', wide_z, packed[1], precision=lax.Precision.HIGHEST)
        return (gram, drive_part)
    grams, drive_parts = lax.map(block_gram, (scaled, misfit))
    codes = jnp.concatenate([jnp.full((NREG, BLK_REG, 1), 4, jnp.int32), neighbours.astype(jnp.int32)], axis=-1)
    step_r = codes // 3 - 1
    step_s = codes % 3 - 1
    taper = jnp.exp2(-(jnp.abs(step_r) + jnp.abs(step_s)).astype(jnp.float32))
    identity = jnp.eye(ensemble, dtype=jnp.float32)

    def second_pass(region):
        region_rows = (region + step_r[region]) % NREG
        block_cols = (jnp.arange(BLK_REG, dtype=jnp.int32)[:, None] + step_s[region]) % BLK_REG
        near_gram = grams[region_rows, block_cols]
        near_drive = drive_parts[region_rows, block_cols]
        system = (ensemble - 1.0) * identity + lax.optimization_barrier(jnp.sum(taper[region][..., None, None] * near_gram, axis=1))
        drive = lax.optimization_barrier(jnp.sum(taper[region][..., None] * near_drive, axis=1))
        weights = transform(system, drive, ensemble)
        update = jnp.einsum('bkj,bkf->bjf', weights.astype(jnp.float32), spread[region].astype(jnp.float32), precision=lax.Precision.HIGHEST)
        return (mean_state[region][:, None, :] + update).astype(jnp.bfloat16)
    result = lax.map(second_pass, jnp.arange(NREG, dtype=jnp.int32))
    return result.reshape(NREG, BLK_REG, ensemble, V, BCOL).transpose(2, 3, 0, 1, 4).reshape(ensemble, V, NREG * BLK_REG * BCOL)
```

```python
import jax
import jax.numpy as jnp
from jax import lax
from jax.experimental import pallas as pl
from jax.experimental.pallas import tpu as pltpu
from jax.sharding import PartitionSpec as P

MESH = pl.DeviceIdType.MESH
F32 = jnp.float32
BF16 = jnp.bfloat16
NS_ITERS = 4
NMEM = 16
NREG = 32
K = 256
OBS = 384
CHUNKS = 8
PACK = 384
MSG = 400
CODE_ROW = 5
SENDS = (8, 7, 9, 6, 10, 5, 11, 4, 12, 3, 13, 2, 14, 1, 15)
EARLY = 5


def split2(x):
    high = x.astype(BF16)
    low = (x - high.astype(F32)).astype(BF16)
    return high, low


def dot(a, b):
    return jnp.dot(a, b, preferred_element_type=F32)


def dot_nt(a, b):
    return lax.dot_general(a, b, (((1,), (1,)), ((), ())), preferred_element_type=F32)


def dot3(a, b):
    return dot(a[0], b[0]) + (dot(a[0], b[1]) + dot(a[1], b[0]))


def rows_of(parts, rows):
    width = parts[0].shape[1]
    index = lax.broadcasted_iota(jnp.int32, (rows, width), 0)
    block = jnp.zeros((rows, width), F32)
    for i, part in enumerate(parts):
        block = jnp.where(index == i, part, block)
    return block


def drive_rows(low_half, high_half):
    a, b = low_half.astype(BF16).astype(F32), high_half.astype(BF16).astype(F32)
    return rows_of([a, b, low_half - a, high_half - b], MSG - PACK).astype(BF16)


def newton_root(matrix):
    n = matrix.shape[0]
    diagonal = lax.broadcasted_iota(jnp.int32, (n, n), 0) == lax.broadcasted_iota(jnp.int32, (n, n), 1)
    eye15 = jnp.where(diagonal, 1.5, 0.0).astype(F32)
    middle = eye15 - 0.5 * matrix
    inverse = split2(middle)
    current = split2(dot3(split2(matrix), inverse))
    for step in range(1, NS_ITERS):
        middle = split2(eye15 - 0.5 * dot3(inverse, current))
        if step < NS_ITERS - 1:
            current = split2(dot3(current, middle))
        product = dot3(middle, inverse)
        inverse = split2(product)
    return product


def kernel(
    x_ref, obs_ref, coef_ref, rinv_ref, site_ref, count_ref, near_ref, out_ref,
    flat, packed, recv, obs_send, obs_recv, code_recv, onehot, own, gmsg, yrecv, center, xsend, xrecv,
    spread, mean, update,
    in_s, in_r, obs_s, obs_r, code_s, code_r, y_s, y_r, x_s, x_r, out_s, out_r, own_s,
):
    me = lax.axis_index("mem")
    reg = lax.axis_index("reg")
    left, right = lax.rem(me + NMEM - 1, NMEM), lax.rem(me + 1, NMEM)
    below, above = lax.rem(reg + NREG - 1, NREG), lax.rem(reg + 1, NREG)
    edge = jnp.logical_or(me == 0, me == NMEM - 1)

    barrier = pltpu.get_barrier_semaphore()
    for i in range(1, NMEM):
        pl.semaphore_signal(
            barrier, inc=1, device_id={"mem": lax.rem(me + i, NMEM)}, device_id_type=MESH
        )
    for side in (below, above):
        pl.semaphore_signal(barrier, inc=1, device_id={"reg": side}, device_id_type=MESH)

    for j in range(2):
        for row, ref in enumerate((obs_ref, coef_ref, rinv_ref)):
            obs_send[j, row : row + 1, :] = ref[0, j : j + 1, :]
        obs_send[j, 3:4, :] = site_ref[0, j : j + 1, :].astype(F32)
        obs_send[j, 4:5, :] = jnp.full((1, OBS), count_ref[0, j].astype(F32))
        for code in range(9):
            value = jnp.float32(1.0 if code == 4 else 0.0)
            taper = 0.5 ** (abs(code // 3 - 1) + abs(code % 3 - 1))
            if code != 4:
                for i in range(5):
                    value = value + jnp.where(near_ref[0, j, i] == code, jnp.float32(taper), jnp.float32(0.0))
            obs_send[j, CODE_ROW + code : CODE_ROW + code + 1, :] = jnp.full((1, OBS), value)

    lane = lax.broadcasted_iota(jnp.int32, (16, 128), 1)
    first = lane < 64

    def reorder(slab, carry):
        columns = pl.ds(pl.multiple_of(slab * 128, 128), 128)
        flat[...] = x_ref[:, :, columns].astype(F32).reshape(256, 128)
        for c in range(CHUNKS):
            even = flat[pl.ds(2 * c, 16, stride=16), :]
            odd = flat[pl.ds(2 * c + 1, 16, stride=16), :]
            packed[2 * slab, c] = jnp.where(first, even, pltpu.roll(odd, 64, 1)).astype(BF16)
            packed[2 * slab + 1, c] = jnp.where(first, pltpu.roll(even, 64, 1), odd).astype(BF16)
        return carry

    lax.fori_loop(0, 16, reorder, 0)
    mine = pl.ds(pl.multiple_of(me * 16, 16), 16)
    for phase in range(2):
        recv[phase, :, mine, :] = packed[phase * NMEM + me]

    pl.semaphore_wait(barrier, NMEM + 1)

    def in_copy(phase, target):
        return pltpu.make_async_remote_copy(
            src_ref=packed.at[phase * NMEM + target],
            dst_ref=recv.at[phase, :, mine, :],
            send_sem=in_s.at[phase, target],
            recv_sem=in_r.at[phase, me],
            device_id={"mem": target},
            device_id_type=MESH,
        )

    def in_wait(phase):
        def one(i, carry):
            source = lax.rem(me + i, NMEM)
            rows = pl.ds(pl.multiple_of(source * 16, 16), 16)
            pltpu.make_async_remote_copy(
                src_ref=packed.at[phase * NMEM + me],
                dst_ref=recv.at[phase, :, rows, :],
                send_sem=in_s.at[phase, me],
                recv_sem=in_r.at[phase, source],
                device_id={"mem": source},
                device_id_type=MESH,
            ).wait_recv()
            return carry

        lax.fori_loop(1, NMEM, one, 0)

    half = me // 8

    def obs_copy(j):
        return pltpu.make_async_remote_copy(
            src_ref=obs_send.at[j],
            dst_ref=obs_recv.at[half],
            send_sem=obs_s.at[j],
            recv_sem=obs_r.at[half],
            device_id={"mem": lax.rem(2 * me + j, NMEM)},
            device_id_type=MESH,
        )

    def obs_far(j):
        return lax.rem(2 * me + j, NMEM) != me

    for j in range(2):
        pl.when(obs_far(j))(lambda j=j: obs_copy(j).start())

        @pl.when(jnp.logical_not(obs_far(j)))
        def _(j=j):
            obs_recv[half] = obs_send[j]

    def second_in(i, wanted):
        target = lax.rem(me + i, NMEM)
        at_edge = jnp.logical_or(target == 0, target == NMEM - 1)
        pl.when(at_edge if wanted else jnp.logical_not(at_edge))(lambda: in_copy(1, target).start())

    for i in SENDS:
        second_in(i, True)
    for i in SENDS:
        in_copy(0, lax.rem(me + i, NMEM)).start()
    for i in SENDS[:EARLY]:
        second_in(i, False)

    def code_copy(phase, side):
        return pltpu.make_async_remote_copy(
            src_ref=obs_recv.at[phase, :, 0:128],
            dst_ref=code_recv.at[phase, side],
            send_sem=code_s.at[phase, side],
            recv_sem=code_r.at[phase, side],
            device_id={"reg": above if side == 0 else below},
            device_id_type=MESH,
        )

    for phase in range(2):
        source = phase * 8 + me // 2

        @pl.when(source != me)
        def _(phase=phase):
            pltpu.make_async_remote_copy(
                src_ref=obs_send.at[0],
                dst_ref=obs_recv.at[phase],
                send_sem=obs_s.at[0],
                recv_sem=obs_r.at[phase],
                device_id={"mem": phase * 8 + me // 2},
                device_id_type=MESH,
            ).wait_recv()

        for side in range(2):
            code_copy(phase, side).start()
        site = obs_recv[phase, 3:4, :].astype(jnp.int32)
        for c in range(CHUNKS):
            place = lax.broadcasted_iota(jnp.int32, (128, OBS), 0) + c * 128
            onehot[phase, c * 128 : (c + 1) * 128, :] = jnp.where(place == site, 1.0, 0.0).astype(BF16)

    def observe(phase):
        values = jnp.concatenate([recv[phase, c] for c in range(CHUNKS)], axis=1)
        predicted = dot(values, onehot[phase]) * obs_recv[phase, 1:2, :]
        mean_pred = jnp.sum(predicted, axis=0, keepdims=True) * (1.0 / K)
        slot = lax.broadcasted_iota(jnp.int32, (1, OBS), 1).astype(F32)
        root = jnp.where(slot < obs_recv[phase, 4:5, :], jnp.sqrt(obs_recv[phase, 2:3, :]), 0.0)
        scaled = (root * (predicted - mean_pred)).astype(BF16)
        misfit = root * (obs_recv[phase, 0:1, :] - mean_pred)
        gram = dot_nt(scaled, scaled)
        a = misfit.astype(BF16).astype(F32)
        b = (misfit - a).astype(BF16).astype(F32)
        parts = rows_of([a, b, misfit - a - b], 16).astype(BF16)
        drive = jnp.sum(dot_nt(parts, scaled), axis=0, keepdims=True)
        for i, block in enumerate((gram[:128, :128], gram[:128, 128:], gram[128:, 128:])):
            own[phase, i * 128 : (i + 1) * 128, :] = block
            gmsg[phase, i * 128 : (i + 1) * 128, :] = block.astype(BF16)
        own[phase, PACK:MSG, :] = rows_of([drive[:, :128], drive[:, 128:]], MSG - PACK)
        gmsg[phase, PACK:MSG, :] = drive_rows(drive[:, :128], drive[:, 128:])

    def y_copy(phase, side):
        wraps = me == (NMEM - 1 if side == 0 else 0)
        return pltpu.make_async_remote_copy(
            src_ref=gmsg.at[jnp.where(wraps, 1 - phase, phase)],
            dst_ref=yrecv.at[phase, side],
            send_sem=y_s.at[phase, side],
            recv_sem=y_r.at[phase, side],
            device_id={"mem": right if side == 0 else left},
            device_id_type=MESH,
        )

    def x_copy(phase, side):
        return pltpu.make_async_remote_copy(
            src_ref=xsend.at[phase, side],
            dst_ref=xrecv.at[phase, side],
            send_sem=x_s.at[phase, side],
            recv_sem=x_r.at[phase, side],
            device_id={"reg": above if side == 0 else below},
            device_id_type=MESH,
        )

    def center_state(phase):
        for c in range(CHUNKS):
            values = recv[phase, c].astype(F32)
            average = jnp.sum(values, axis=0, keepdims=True) * (1.0 / K)
            mean[phase, :, c * 128 : (c + 1) * 128] = jnp.broadcast_to(average, (8, 128))
            spread[phase, :, c * 128 : (c + 1) * 128] = (values - average).astype(BF16)

    def sum_row(phase):
        for side in range(2):
            y_copy(phase, side).wait_recv()
            code_copy(phase, side).wait_recv()

        def weighted(weights, first_code, rows):
            w = [weights[CODE_ROW + first_code + i : CODE_ROW + first_code + i + 1, :] for i in range(3)]
            return (
                w[0] * yrecv[phase, 0, rows, :].astype(F32)
                + w[1] * own[phase, rows, :]
                + w[2] * yrecv[phase, 1, rows, :].astype(F32)
            )

        for side in range(2):
            weights = code_recv[phase, 1 - side]
            first_code = 0 if side == 0 else 6
            for i in range(3):
                rows = slice(i * 128, (i + 1) * 128)
                xsend[phase, side, rows, :] = weighted(weights, first_code, rows).astype(BF16)
            tail = weighted(weights, first_code, slice(PACK, MSG))
            xsend[phase, side, PACK:MSG, :] = drive_rows(
                tail[0:1] + tail[2:3], tail[1:2] + tail[3:4]
            )
            x_copy(phase, side).start()
        center[phase] = weighted(obs_recv[phase, :, 0:128], 3, slice(0, MSG))

    def transform(phase):
        for side in range(2):
            x_copy(phase, side).wait_recv()
        total = center[phase] + xrecv[phase, 0].astype(F32) + xrecv[phase, 1].astype(F32)
        tail = total[PACK:MSG]
        drive = jnp.concatenate([tail[0:1] + tail[2:3], tail[1:2] + tail[3:4]], axis=1)
        corner = total[128:256]
        system = jnp.concatenate(
            [
                jnp.concatenate([total[0:128], corner], axis=1),
                jnp.concatenate([corner.T, total[256:384]], axis=1),
            ],
            axis=0,
        )
        diagonal = lax.broadcasted_iota(jnp.int32, (K, K), 0) == lax.broadcasted_iota(jnp.int32, (K, K), 1)
        system = system + jnp.where(diagonal, K - 1.0, 0.0)
        scale = jnp.max(jnp.sum(jnp.abs(system), axis=0, keepdims=True), axis=1, keepdims=True)
        half = newton_root(system / scale) / jnp.sqrt(scale)
        halves = split2(half)
        vector = jnp.broadcast_to(drive, (16, K))
        vector = dot3(split2(vector), halves)
        vector = dot3(split2(vector), halves)[0:1]
        return (jnp.float32(K - 1.0) ** 0.5 * half + vector).astype(BF16)

    def apply(phase, weights):
        for c in range(0, CHUNKS, 2):
            columns = slice(c * 128, (c + 2) * 128)
            result = dot(weights, spread[phase, :, columns]) + mean[phase, 0:1, columns]
            update[phase, c] = result[:, :128].astype(BF16)
            update[phase, c + 1] = result[:, 128:].astype(BF16)

    def out_copy(phase, target):
        rows = pl.ds(pl.multiple_of(target * 16, 16), 16)
        return pltpu.make_async_remote_copy(
            src_ref=update.at[phase, :, rows, :],
            dst_ref=out_ref.at[phase, me],
            send_sem=out_s.at[phase, target],
            recv_sem=out_r.at[phase, me],
            device_id={"mem": target},
            device_id_type=MESH,
        )

    def own_copy(phase):
        return pltpu.make_async_copy(update.at[phase, :, mine, :], out_ref.at[phase, me], own_s.at[phase])

    def send_out(phase):
        for i in SENDS:
            out_copy(phase, lax.rem(me + i, NMEM)).start()
        own_copy(phase).start()

    in_wait(0)
    observe(0)

    @pl.when(edge)
    def _():
        in_wait(1)
        observe(1)

    for side in range(2):
        y_copy(0, side).start()
    for i in SENDS[EARLY:]:
        second_in(i, False)
    center_state(0)
    sum_row(0)

    @pl.when(jnp.logical_not(edge))
    def _():
        in_wait(1)
        observe(1)

    for side in range(2):
        y_copy(1, side).start()
    center_state(1)
    apply(0, transform(0))
    send_out(0)
    sum_row(1)
    apply(1, transform(1))
    send_out(1)

    for phase in range(2):
        own_copy(phase).wait()

        def finish(i, carry, phase=phase):
            other = lax.rem(me + i, NMEM)
            in_copy(phase, other).wait_send()
            out_copy(phase, other).wait_send()
            pltpu.make_async_remote_copy(
                src_ref=update.at[phase, :, mine, :],
                dst_ref=out_ref.at[phase, other],
                send_sem=out_s.at[phase, me],
                recv_sem=out_r.at[phase, other],
                device_id={"mem": other},
                device_id_type=MESH,
            ).wait_recv()
            return carry

        lax.fori_loop(1, NMEM, finish, 0)
        for side in range(2):
            code_copy(phase, side).wait_send()
            y_copy(phase, side).wait_send()
            x_copy(phase, side).wait_send()
    for j in range(2):
        pl.when(obs_far(j))(lambda j=j: obs_copy(j).wait_send())


def order_back(in_ref, out_ref, flat):
    first = lax.broadcasted_iota(jnp.int32, (16, 128), 1) < 64
    for p in range(in_ref.shape[0] // 2):
        for c in range(CHUNKS):
            a = in_ref[2 * p, c].astype(F32)
            b = in_ref[2 * p + 1, c].astype(F32)
            flat[p, pl.ds(2 * c, 16, stride=16), :] = jnp.where(first, a, pltpu.roll(b, 64, 1))
            flat[p, pl.ds(2 * c + 1, 16, stride=16), :] = jnp.where(first, pltpu.roll(a, 64, 1), b)
        out_ref[:, :, p * 128 : (p + 1) * 128] = flat[p].reshape(16, 16, 128).astype(BF16)


def per_device(background, observations, obs_coef, obs_rinv, obs_site, obs_count, neighbours):
    vmem = pl.BlockSpec(memory_space=pltpu.VMEM)
    smem = pl.BlockSpec(memory_space=pltpu.SMEM)
    dma = pltpu.SemaphoreType.DMA
    moved = pl.pallas_call(
        kernel,
        out_shape=jax.ShapeDtypeStruct((2, NMEM, CHUNKS, 16, 128), BF16),
        in_specs=[vmem] * 5 + [smem] * 2,
        out_specs=pl.BlockSpec(memory_space=pl.ANY),
        scratch_shapes=[
            pltpu.VMEM((256, 128), F32),
            pltpu.VMEM((2 * NMEM, CHUNKS, 16, 128), BF16),
            pltpu.VMEM((2, CHUNKS, K, 128), BF16),
            pltpu.VMEM((2, 16, OBS), F32),
            pltpu.VMEM((2, 16, OBS), F32),
            pltpu.VMEM((2, 2, 16, 128), F32),
            pltpu.VMEM((2, CHUNKS * 128, OBS), BF16),
            pltpu.VMEM((2, MSG, 128), F32),
            pltpu.VMEM((2, MSG, 128), BF16),
            pltpu.VMEM((2, 2, MSG, 128), BF16),
            pltpu.VMEM((2, MSG, 128), F32),
            pltpu.VMEM((2, 2, MSG, 128), BF16),
            pltpu.VMEM((2, 2, MSG, 128), BF16),
            pltpu.VMEM((2, K, CHUNKS * 128), BF16),
            pltpu.VMEM((2, 8, CHUNKS * 128), F32),
            pltpu.VMEM((2, CHUNKS, K, 128), BF16),
            dma((2, NMEM)), dma((2, NMEM)),
            dma((2,)), dma((2,)),
            dma((2, 2)), dma((2, 2)),
            dma((2, 2)), dma((2, 2)),
            dma((2, 2)), dma((2, 2)),
            dma((2, NMEM)), dma((2, NMEM)),
            dma((2,)),
        ],
        compiler_params=pltpu.CompilerParams(
            collective_id=0, has_side_effects=True, vmem_limit_bytes=40 << 20
        ),
        name="analysis",
    )(background, observations, obs_coef, obs_rinv, obs_site, obs_count, neighbours)
    steps = 4
    blocks = 2 * NMEM // steps
    width = background.shape[2] // steps
    return pl.pallas_call(
        order_back,
        grid=(steps,),
        out_shape=jax.ShapeDtypeStruct(background.shape, BF16),
        in_specs=[pl.BlockSpec((blocks, CHUNKS, 16, 128), lambda i: (i, 0, 0, 0))],
        out_specs=pl.BlockSpec((16, 16, width), lambda i: (0, 0, i)),
        scratch_shapes=[pltpu.VMEM((blocks // 2, 256, 128), F32)],
        name="order_back",
    )(moved.reshape(2 * NMEM, CHUNKS, 16, 128))


def solution(mesh):
    in_specs = (
        P("mem", None, "reg"),
        P("reg", "mem", None),
        P("reg", "mem", None),
        P("reg", "mem", None),
        P("reg", "mem", None),
        P("reg", "mem"),
        P("reg", "mem", None),
    )
    out_specs = P("mem", None, "reg")
    return jax.shard_map(
        per_device, mesh=mesh, in_specs=in_specs, out_specs=out_specs, check_vma=False
    )
```

```python
import contextlib

import jax
import jax.numpy as jnp
from jax import lax
from jax.experimental import pallas as pl
from jax.experimental.pallas import tpu as pltpu
from jax.sharding import PartitionSpec as P

MESH = pl.DeviceIdType.MESH
F32 = jnp.float32
BF16 = jnp.bfloat16
NS_ITERS = 4
NMEM = 16
NREG = 32
K = 256
OBS = 384
CHUNKS = 8
PACK = 384
MSG = 400
PARTS = ((0, 128), (128, 256), (256, MSG))
CODE_ROW = 5
SENDS = tuple((away, core) for away in (3, 2, 1, 4, -3, -2, -1) for core in range(2)) + ((0, 0),)
EARLY = 6
EARLY_OUT = 6


def split2(x):
    high = x.astype(BF16)
    low = (x - high.astype(F32)).astype(BF16)
    return high, low


def dot(a, b):
    return jnp.dot(a, b, preferred_element_type=F32)


def dot_nt(a, b):
    return lax.dot_general(a, b, (((1,), (1,)), ((), ())), preferred_element_type=F32)


def dot3(a, b):
    return dot(a[0], b[0]) + (dot(a[0], b[1]) + dot(a[1], b[0]))


def rows_of(parts, rows):
    width = parts[0].shape[1]
    index = lax.broadcasted_iota(jnp.int32, (rows, width), 0)
    block = jnp.zeros((rows, width), F32)
    for i, part in enumerate(parts):
        block = jnp.where(index == i, part, block)
    return block


def drive_rows(low_half, high_half):
    a, b = low_half.astype(BF16).astype(F32), high_half.astype(BF16).astype(F32)
    return rows_of([a, b, low_half - a, high_half - b], MSG - PACK).astype(BF16)


def newton_root(matrix):
    n = matrix.shape[0]
    diagonal = lax.broadcasted_iota(jnp.int32, (n, n), 0) == lax.broadcasted_iota(jnp.int32, (n, n), 1)
    eye15 = jnp.where(diagonal, 1.5, 0.0).astype(F32)
    middle = eye15 - 0.5 * matrix
    inverse = split2(middle)
    current = split2(dot3(split2(matrix), inverse))
    for step in range(1, NS_ITERS):
        middle = split2(eye15 - 0.5 * dot3(inverse, current))
        if step < NS_ITERS - 1:
            current = split2(dot3(current, middle))
        product = dot3(middle, inverse)
        inverse = split2(product)
    return product


def stage(name):
    return contextlib.nullcontext()


def kernel(
    x_hbm, obs_hbm, coef_hbm, rinv_hbm, site_hbm, count_hbm, near_hbm, out_hbm,
    state, obs_in, coef_in, rinv_in, site_in, count_in, near_in,
    flat, packed, recv, obs_send, obs_recv, code_recv, onehot, own, gmsg, yrecv, center, xsend, xrecv,
    spread, mean, update, returned, ordered,
    region_in, adjacent_in, state_s, small_s, in_s, in_r, obs_s, obs_r, code_s, code_r, y_s, y_r, x_s, x_r, out_s, out_r, result_s,
):
    me = lax.axis_index("mem")
    reg = lax.axis_index("reg")
    chip = me // 2
    left, right = lax.rem(me + NMEM - 1, NMEM), lax.rem(me + 1, NMEM)
    below, above = lax.rem(reg + NREG - 1, NREG), lax.rem(reg + 1, NREG)
    edge = jnp.logical_or(me == 0, me == NMEM - 1)

    core = lax.rem(me, 2)
    sibling = me + 1 - 2 * core
    barrier = pltpu.get_barrier_semaphore()

    def greet(target):
        pl.semaphore_signal(barrier, inc=1, device_id={"mem": target}, device_id_type=MESH)

    pl.when(core == 1)(lambda: greet(sibling))
    for i in range(1, 8):
        greet(2 * lax.rem(chip + i, 8))
    for side in (below, above):
        pl.semaphore_signal(
            barrier, inc=1, device_id={"mem": 2 * chip + 1, "reg": side}, device_id_type=MESH
        )

    def pass_barrier(hearer, count, passed):
        @pl.when(core == hearer)
        def _():
            pl.semaphore_wait(barrier, count)
            pl.semaphore_signal(passed, inc=1, device_id={"mem": sibling}, device_id_type=MESH)

        pl.when(core != hearer)(lambda: pl.semaphore_wait(passed, 1))

    def slab_of(step):
        away = 4 + lax.div(step + 1, 2) * (1 - 2 * lax.rem(step, 2))
        return lax.rem(chip + away, 8)

    def lanes(slab):
        return pl.ds(pl.multiple_of(slab * 128, 128), 128)

    def state_copy(phase):
        columns = pl.ds(phase * 1024, 1024)
        return pltpu.make_async_copy(
            x_hbm.at[:, :, columns], state.at[:, :, columns], state_s.at[phase]
        )

    small = [
        pltpu.make_async_copy(source, target, small_s.at[i])
        for i, (source, target) in enumerate(
            (
                (obs_hbm, obs_in), (coef_hbm, coef_in), (rinv_hbm, rinv_in), (site_hbm, site_in),
                (count_hbm, count_in), (near_hbm, near_in),
            )
        )
    ]

    state_copy(0).start()
    for copy in small:
        copy.start()
    state_copy(1).start()

    first = lax.broadcasted_iota(jnp.int32, (16, 128), 1) < 64
    mine = pl.ds(pl.multiple_of(me * 16, 16), 16)

    def reorder(slab):
        flat[...] = state[:, :, lanes(slab)].astype(F32).reshape(256, 128)
        for c in range(CHUNKS):
            even = flat[pl.ds(2 * c, 16, stride=16), :]
            odd = flat[pl.ds(2 * c + 1, 16, stride=16), :]
            packed[2 * slab, c] = jnp.where(first, even, pltpu.roll(odd, 64, 1)).astype(BF16)
            packed[2 * slab + 1, c] = jnp.where(first, pltpu.roll(even, 64, 1), odd).astype(BF16)

    def in_copy(phase, target):
        return pltpu.make_async_remote_copy(
            src_ref=packed.at[phase * NMEM + target],
            dst_ref=recv.at[phase, :, mine, :],
            send_sem=in_s.at[phase],
            recv_sem=in_r.at[phase],
            device_id={"mem": target},
            device_id_type=MESH,
        )

    def in_all(phase):
        others = recv.at[phase, :, pl.ds(0, K - 16), :]
        return pltpu.make_async_remote_copy(
            src_ref=others,
            dst_ref=others,
            send_sem=in_s.at[phase],
            recv_sem=in_r.at[phase],
            device_id={"mem": sibling},
            device_id_type=MESH,
        )

    def in_wait(phase):
        in_all(phase).wait_recv()

    half = me // 8

    def obs_copy(j):
        return pltpu.make_async_remote_copy(
            src_ref=obs_send.at[j],
            dst_ref=obs_recv.at[half],
            send_sem=obs_s.at[j],
            recv_sem=obs_r.at[half],
            device_id={"mem": lax.rem(2 * me + j, NMEM)},
            device_id_type=MESH,
        )

    def obs_far(j):
        return lax.rem(2 * me + j, NMEM) != me

    def first_in(step, carry):
        slab = slab_of(step)
        reorder(slab)
        for core in range(2):
            target = 2 * slab + core
            pl.when(target != me)(lambda target=target: in_copy(0, target).start())
        return carry

    with stage("barrier"):
        state_copy(0).wait()
        pass_barrier(0, NMEM - 1, region_in)
    with stage("first_in_a"):
        lax.fori_loop(0, 2, first_in, 0)

    with stage("obs_send"):
        for copy in small:
            copy.wait()
        row = lax.broadcasted_iota(jnp.int32, (16, OBS), 0)
        code = row - CODE_ROW
        away = jnp.abs(code // 3 - 1) + jnp.abs(lax.rem(code + 15, 3) - 1)
        taper = jnp.where(away == 0, 1.0, jnp.where(away == 1, 0.5, 0.25))
        for j in range(2):
            block = jnp.where(code == 4, 1.0, 0.0)
            for i in range(5):
                block = block + jnp.where(code == near_in[0, j : j + 1, i : i + 1], taper, 0.0)
            count = jnp.broadcast_to(count_in[0:1, j : j + 1].astype(F32), (16, OBS))
            obs_send[j] = jnp.where(row == 4, count, block)
            for i, ref in enumerate((obs_in, coef_in, rinv_in)):
                obs_send[j, i : i + 1, :] = ref[0, j : j + 1, :]
            obs_send[j, 3:4, :] = site_in[0, j : j + 1, :].astype(F32)
        for j in range(2):
            pl.when(obs_far(j))(lambda j=j: obs_copy(j).start())

            @pl.when(jnp.logical_not(obs_far(j)))
            def _(j=j):
                obs_recv[half] = obs_send[j]

    def partner(away, core):
        if away == 0:
            return 2 * chip + 1 - lax.rem(me, 2)
        turned = away * (1 - 2 * lax.rem(me, 2))
        return 2 * lax.rem(chip + 8 + turned, 8) + core

    def second_in(i, wanted):
        target = partner(*i)
        at_edge = jnp.logical_or(target == 0, target == NMEM - 1)
        pl.when(at_edge if wanted else jnp.logical_not(at_edge))(lambda: in_copy(1, target).start())

    def reorder_step(slab, carry):
        reorder(slab)
        return carry

    with stage("first_in_b"):
        lax.fori_loop(2, 8, first_in, 0)
    with stage("second_in"):
        state_copy(1).wait()
        reorder(8)
        reorder(15)
        for i in SENDS:
            second_in(i, True)
        lax.fori_loop(9, 15, reorder_step, 0)
        for i in SENDS[:EARLY]:
            second_in(i, False)
        recv[0, :, mine, :] = packed[me]
        recv[1, :, mine, :] = packed[NMEM + me]

    def code_copy(phase, side):
        return pltpu.make_async_remote_copy(
            src_ref=obs_recv.at[phase, :, 0:128],
            dst_ref=code_recv.at[phase, side],
            send_sem=code_s,
            recv_sem=code_r,
            device_id={"reg": above if side == 0 else below},
            device_id_type=MESH,
        )

    def codes_all():
        return pltpu.make_async_remote_copy(
            src_ref=code_recv,
            dst_ref=code_recv,
            send_sem=code_s,
            recv_sem=code_r,
            device_id={"reg": above},
            device_id_type=MESH,
        )

    with stage("onehot"):
        for phase in range(2):
            @pl.when(phase * 8 + chip != me)
            def _(phase=phase):
                pltpu.make_async_remote_copy(
                    src_ref=obs_send.at[0],
                    dst_ref=obs_recv.at[phase],
                    send_sem=obs_s.at[0],
                    recv_sem=obs_r.at[phase],
                    device_id={"mem": phase * 8 + chip},
                    device_id_type=MESH,
                ).wait_recv()

            site = obs_recv[phase, 3:4, :].astype(jnp.int32)
            for c in range(CHUNKS):
                place = lax.broadcasted_iota(jnp.int32, (128, OBS), 0) + c * 128
                onehot[phase, c * 128 : (c + 1) * 128, :] = jnp.where(place == site, 1.0, 0.0).astype(BF16)

    def observe(phase):
        values = jnp.concatenate([recv[phase, c] for c in range(CHUNKS)], axis=1)
        predicted = dot(values, onehot[phase]) * obs_recv[phase, 1:2, :]
        mean_pred = jnp.sum(predicted, axis=0, keepdims=True) * (1.0 / K)
        slot = lax.broadcasted_iota(jnp.int32, (1, OBS), 1).astype(F32)
        root = jnp.where(slot < obs_recv[phase, 4:5, :], jnp.sqrt(obs_recv[phase, 2:3, :]), 0.0)
        scaled = (root * (predicted - mean_pred)).astype(BF16)
        misfit = root * (obs_recv[phase, 0:1, :] - mean_pred)
        gram = dot_nt(scaled, scaled)
        a = misfit.astype(BF16).astype(F32)
        b = (misfit - a).astype(BF16).astype(F32)
        parts = rows_of([a, b, misfit - a - b], 16).astype(BF16)
        drive = jnp.sum(dot_nt(parts, scaled), axis=0, keepdims=True)
        for i, block in enumerate((gram[:128, :128], gram[:128, 128:], gram[128:, 128:])):
            own[phase, i * 128 : (i + 1) * 128, :] = block
            gmsg[phase, i * 128 : (i + 1) * 128, :] = block.astype(BF16)
        own[phase, PACK:MSG, :] = rows_of([drive[:, :128], drive[:, 128:]], MSG - PACK)
        gmsg[phase, PACK:MSG, :] = drive_rows(drive[:, :128], drive[:, 128:])

    def y_wraps(side):
        return me == (NMEM - 1 if side == 0 else 0)

    def y_copy(phase, side, part):
        rows = slice(*PARTS[part])
        return pltpu.make_async_remote_copy(
            src_ref=gmsg.at[jnp.where(y_wraps(side), 1 - phase, phase), rows],
            dst_ref=yrecv.at[phase, side, rows],
            send_sem=y_s.at[phase],
            recv_sem=y_r.at[phase, part],
            device_id={"mem": right if side == 0 else left},
            device_id_type=MESH,
        )

    def y_start(phase, side):
        for part in range(len(PARTS)):
            y_copy(phase, side, part).start()

    def x_copy(phase, side, part):
        rows = slice(*PARTS[part])
        return pltpu.make_async_remote_copy(
            src_ref=xsend.at[phase, side, rows],
            dst_ref=xrecv.at[phase, side, rows],
            send_sem=x_s.at[phase],
            recv_sem=x_r.at[phase],
            device_id={"reg": above if side == 0 else below},
            device_id_type=MESH,
        )

    def y_all(phase, rows, part=0):
        both = yrecv.at[phase, :, rows]
        return pltpu.make_async_remote_copy(
            src_ref=both,
            dst_ref=both,
            send_sem=y_s.at[phase],
            recv_sem=y_r.at[phase, part],
            device_id={"mem": sibling},
            device_id_type=MESH,
        )

    def x_all(phase):
        return pltpu.make_async_remote_copy(
            src_ref=xsend.at[phase],
            dst_ref=xrecv.at[phase],
            send_sem=x_s.at[phase],
            recv_sem=x_r.at[phase],
            device_id={"reg": above},
            device_id_type=MESH,
        )

    def x_wait(phase):
        x_all(phase).wait_recv()

    def center_state(phase):
        for c in range(CHUNKS):
            values = recv[phase, c].astype(F32)
            average = jnp.sum(values, axis=0, keepdims=True) * (1.0 / K)
            mean[phase, :, c * 128 : (c + 1) * 128] = jnp.broadcast_to(average, (8, 128))
            spread[phase, :, c * 128 : (c + 1) * 128] = (values - average).astype(BF16)

    def sum_row(phase):
        def weighted(weights, first_code, rows):
            w = [weights[CODE_ROW + first_code + i : CODE_ROW + first_code + i + 1, :] for i in range(3)]
            return (
                w[0] * yrecv[phase, 0, rows, :].astype(F32)
                + w[1] * own[phase, rows, :]
                + w[2] * yrecv[phase, 1, rows, :].astype(F32)
            )

        for part in range(len(PARTS)):
            rows = slice(part * 128, (part + 1) * 128)
            y_all(phase, slice(*PARTS[part]), part).wait_recv()
            for side in range(2):
                weights = code_recv[phase, 1 - side]
                first_code = 0 if side == 0 else 6
                xsend[phase, side, rows, :] = weighted(weights, first_code, rows).astype(BF16)
                if part == len(PARTS) - 1:
                    tail = weighted(weights, first_code, slice(PACK, MSG))
                    xsend[phase, side, PACK:MSG, :] = drive_rows(
                        tail[0:1] + tail[2:3], tail[1:2] + tail[3:4]
                    )
                x_copy(phase, side, part).start()
        center[phase] = weighted(obs_recv[phase, :, 0:128], 3, slice(0, MSG))

    def transform(phase):
        total = center[phase] + xrecv[phase, 0].astype(F32) + xrecv[phase, 1].astype(F32)
        tail = total[PACK:MSG]
        drive = jnp.concatenate([tail[0:1] + tail[2:3], tail[1:2] + tail[3:4]], axis=1)
        corner = total[128:256]
        system = jnp.concatenate(
            [
                jnp.concatenate([total[0:128], corner], axis=1),
                jnp.concatenate([corner.T, total[256:384]], axis=1),
            ],
            axis=0,
        )
        diagonal = lax.broadcasted_iota(jnp.int32, (K, K), 0) == lax.broadcasted_iota(jnp.int32, (K, K), 1)
        system = system + jnp.where(diagonal, K - 1.0, 0.0)
        scale = jnp.max(jnp.sum(jnp.abs(system), axis=0, keepdims=True), axis=1, keepdims=True)
        half_root = newton_root(system / scale) / jnp.sqrt(scale)
        halves = split2(half_root)
        vector = jnp.broadcast_to(drive, (16, K))
        vector = dot3(split2(vector), halves)
        vector = dot3(split2(vector), halves)[0:1]
        return (jnp.float32(K - 1.0) ** 0.5 * half_root + vector).astype(BF16)

    def apply(phase, weights):
        for c in range(0, CHUNKS, 2):
            columns = slice(c * 128, (c + 2) * 128)
            result = dot(weights, spread[phase, :, columns]) + mean[phase, 0:1, columns]
            update[phase, c] = result[:, :128].astype(BF16)
            update[phase, c + 1] = result[:, 128:].astype(BF16)

    def out_copy(phase, target):
        rows = pl.ds(pl.multiple_of(target * 16, 16), 16)
        return pltpu.make_async_remote_copy(
            src_ref=update.at[phase, :, rows, :],
            dst_ref=returned.at[phase, me],
            send_sem=out_s.at[phase],
            recv_sem=out_r.at[phase, chip],
            device_id={"mem": target},
            device_id_type=MESH,
        )

    def send_out(phase, offsets):
        for i in offsets:
            out_copy(phase, partner(*i)).start()

    def keep_own(phase):
        returned[phase, me] = update[phase, :, mine, :]

    def result_copy(slab):
        return pltpu.make_async_copy(
            ordered.at[:, :, lanes(slab)], out_hbm.at[:, :, lanes(slab)], result_s
        )

    def order_back(phase):
        def one(step, carry):
            source_chip = lax.rem(16 - slab_of(step) + 2 * chip, 8)
            def arrived(blocks):
                pltpu.make_async_remote_copy(
                    src_ref=returned.at[phase, blocks],
                    dst_ref=returned.at[phase, blocks],
                    send_sem=out_s.at[phase],
                    recv_sem=out_r.at[phase, source_chip],
                    device_id={"mem": sibling},
                    device_id_type=MESH,
                ).wait_recv()

            pl.when(source_chip != chip)(lambda: arrived(pl.ds(2 * source_chip, 2)))
            pl.when(source_chip == chip)(lambda: arrived(pl.ds(sibling, 1)))
            for c in range(CHUNKS):
                a = returned[phase, 2 * source_chip, c].astype(F32)
                b = returned[phase, 2 * source_chip + 1, c].astype(F32)
                flat[pl.ds(2 * c, 16, stride=16), :] = jnp.where(first, a, pltpu.roll(b, 64, 1))
                flat[pl.ds(2 * c + 1, 16, stride=16), :] = jnp.where(first, pltpu.roll(a, 64, 1), b)
            ordered[:, :, lanes(phase * 8 + source_chip)] = flat[...].reshape(16, 16, 128).astype(BF16)
            result_copy(phase * 8 + source_chip).start()
            return carry

        lax.fori_loop(0, 8, one, 0)

    with stage("adjacent"):
        pass_barrier(1, 4, adjacent_in)
        for phase in range(2):
            for side in range(2):
                code_copy(phase, side).start()
    with stage("in_wait0"):
        in_wait(0)
    with stage("observe0"):
        observe(0)
    for side in range(2):
        pl.when(jnp.logical_not(y_wraps(side)))(lambda side=side: y_start(0, side))
    def second_in_rest():
        for i in SENDS[EARLY:]:
            second_in(i, False)

    with stage("second_in_b"):
        pl.when(jnp.logical_not(edge))(second_in_rest)
    with stage("edge"):

        @pl.when(edge)
        def _():
            in_wait(1)
            observe(1)
            for side in range(2):
                pl.when(y_wraps(side))(lambda side=side: y_start(0, side))
            second_in_rest()
            for side in range(2):
                y_start(1, side)

    with stage("center0"):
        center_state(0)
    with stage("sum_row0"):
        codes_all().wait_recv()
        sum_row(0)
    with stage("in_wait1"):
        pl.when(jnp.logical_not(edge))(lambda: in_wait(1))
    with stage("observe1"):

        @pl.when(jnp.logical_not(edge))
        def _():
            observe(1)
            for side in range(2):
                y_start(1, side)

    with stage("x_wait0"):
        x_wait(0)
    with stage("transform0"):
        weights = transform(0)
    with stage("apply0"):
        apply(0, weights)
    send_out(0, SENDS)
    with stage("center1"):
        keep_own(0)
        center_state(1)
    with stage("sum_row1"):
        sum_row(1)
    with stage("x_wait1"):
        x_wait(1)
    with stage("transform1"):
        weights = transform(1)
    with stage("apply1"):
        apply(1, weights)
    send_out(1, SENDS)
    keep_own(1)
    with stage("sent"):
        for phase in range(2):
            in_all(phase).wait_send()
            y_all(phase, slice(0, MSG)).wait_send()
            x_all(phase).wait_send()
        codes_all().wait_send()
        for j in range(2):
            pl.when(obs_far(j))(lambda j=j: obs_copy(j).wait_send())
    with stage("back0"):
        order_back(0)
    with stage("back1"):
        order_back(1)

    with stage("drain"):
        for phase in range(2):
            others = update.at[phase, :, pl.ds(0, K - 16), :]
            pltpu.make_async_remote_copy(
                src_ref=others,
                dst_ref=others,
                send_sem=out_s.at[phase],
                recv_sem=out_r.at[phase, chip],
                device_id={"mem": sibling},
                device_id_type=MESH,
            ).wait_send()
        pltpu.make_async_copy(ordered, out_hbm, result_s).wait()


def per_device(background, observations, obs_coef, obs_rinv, obs_site, obs_count, neighbours):
    dma = pltpu.SemaphoreType.DMA
    small = (observations, obs_coef, obs_rinv, obs_site, obs_count, neighbours)
    return pl.pallas_call(
        kernel,
        out_shape=jax.ShapeDtypeStruct(background.shape, BF16),
        in_specs=[pl.BlockSpec(memory_space=pltpu.HBM)] * 7,
        out_specs=pl.BlockSpec(memory_space=pl.ANY),
        scratch_shapes=[
            pltpu.VMEM(background.shape, BF16),
            *(pltpu.VMEM(array.shape, array.dtype) for array in small),
            pltpu.VMEM((256, 128), F32),
            pltpu.VMEM((2 * NMEM, CHUNKS, 16, 128), BF16),
            pltpu.VMEM((2, CHUNKS, K, 128), BF16),
            pltpu.VMEM((2, 16, OBS), F32),
            pltpu.VMEM((2, 16, OBS), F32),
            pltpu.VMEM((2, 2, 16, 128), F32),
            pltpu.VMEM((2, CHUNKS * 128, OBS), BF16),
            pltpu.VMEM((2, MSG, 128), F32),
            pltpu.VMEM((2, MSG, 128), BF16),
            pltpu.VMEM((2, 2, MSG, 128), BF16),
            pltpu.VMEM((2, MSG, 128), F32),
            pltpu.VMEM((2, 2, MSG, 128), BF16),
            pltpu.VMEM((2, 2, MSG, 128), BF16),
            pltpu.VMEM((2, K, CHUNKS * 128), BF16),
            pltpu.VMEM((2, 8, CHUNKS * 128), F32),
            pltpu.VMEM((2, CHUNKS, K, 128), BF16),
            pltpu.VMEM((2, NMEM, CHUNKS, 16, 128), BF16),
            pltpu.VMEM(background.shape, BF16),
            pltpu.SemaphoreType.REGULAR, pltpu.SemaphoreType.REGULAR,
            dma((2,)), dma((6,)),
            dma((2,)), dma((2,)),
            dma((2,)), dma((2,)),
            dma, dma,
            dma((2,)), dma((2, len(PARTS))),
            dma((2,)), dma((2,)),
            dma((2,)), dma((2, 8)),
            dma,
        ],
        compiler_params=pltpu.CompilerParams(
            collective_id=0, has_side_effects=True, vmem_limit_bytes=62 << 20
        ),
        name="analysis",
    )(background, *small)


def solution(mesh):
    in_specs = (
        P("mem", None, "reg"),
        P("reg", "mem", None),
        P("reg", "mem", None),
        P("reg", "mem", None),
        P("reg", "mem", None),
        P("reg", "mem"),
        P("reg", "mem", None),
    )
    out_specs = P("mem", None, "reg")
    return jax.shard_map(
        per_device, mesh=mesh, in_specs=in_specs, out_specs=out_specs, check_vma=False
    )
```

```python
import contextlib

import jax
import jax.numpy as jnp
from jax import lax
from jax.experimental import pallas as pl
from jax.experimental.pallas import tpu as pltpu
from jax.sharding import PartitionSpec as P

MESH = pl.DeviceIdType.MESH
F32 = jnp.float32
BF16 = jnp.bfloat16
NS_ITERS = 4
NMEM = 16
NREG = 32
K = 256
OBS = 384
CHUNKS = 8
PACK = 256
MSG = 272
PARTS = ((0, 128), (128, MSG))
CODE_ROW = 5
SENDS = tuple((away, core) for away in (3, 2, 1, 4, -3, -2, -1) for core in range(2)) + ((0, 0),)
EARLY = 6
EARLY_OUT = 6


def split2(x):
    high = x.astype(BF16)
    low = (x - high.astype(F32)).astype(BF16)
    return high, low


def dot(a, b):
    return jnp.dot(a, b, preferred_element_type=F32)


def dot_nt(a, b):
    return lax.dot_general(a, b, (((1,), (1,)), ((), ())), preferred_element_type=F32)


def dot3(a, b):
    return dot(a[0], b[0]) + (dot(a[0], b[1]) + dot(a[1], b[0]))


def rows_of(parts, rows):
    width = parts[0].shape[1]
    index = lax.broadcasted_iota(jnp.int32, (rows, width), 0)
    block = jnp.zeros((rows, width), F32)
    for i, part in enumerate(parts):
        block = jnp.where(index == i, part, block)
    return block


def tail_rows(tail):
    low_half, high_half = tail[0:1] + tail[2:3], tail[1:2] + tail[3:4]
    a, b = low_half.astype(BF16).astype(F32), high_half.astype(BF16).astype(F32)
    return rows_of([a, b, low_half - a, high_half - b, tail[4:5]], MSG - PACK).astype(BF16)


def square_indices(n):
    return lax.broadcasted_iota(jnp.int32, (n, n), 0), lax.broadcasted_iota(jnp.int32, (n, n), 1)


def newton_root(matrix):
    row, column = square_indices(matrix.shape[0])
    level = jnp.sum(jnp.where(row == column, matrix, 0.0), axis=0, keepdims=True)
    level = jnp.sum(level, axis=1, keepdims=True) * (1.0 / matrix.shape[0])

    def product(left, right):
        inner = dot(left[2], right[2])
        return left[0] * right[0], left[0] * right[1] + (right[0] * left[1] + inner)

    def rounded(value, rest):
        return value, rest, rest.astype(BF16)

    def middle_of(value, rest):
        return rounded(1.5 - 0.5 * value, -0.5 * rest)

    current = rounded(level, jnp.where(row == column, matrix - level, matrix))
    middle = middle_of(*current[:2])
    inverse = middle
    current = rounded(*product(current, inverse))
    for step in range(1, NS_ITERS):
        middle = middle_of(*product(inverse, current))
        if step < NS_ITERS - 1:
            current = rounded(*product(current, middle))
        inverse = rounded(*product(middle, inverse))
    return jnp.where(row == column, inverse[0] + inverse[1], inverse[1])


def stage(name):
    return contextlib.nullcontext()


def kernel(
    x_hbm, obs_hbm, coef_hbm, rinv_hbm, site_hbm, count_hbm, near_hbm, out_hbm,
    state, obs_in, coef_in, rinv_in, site_in, count_in, near_in,
    flat, packed, recv, obs_send, obs_recv, code_recv, onehot, own, gmsg, yrecv, center, xsend, xrecv,
    spread, mean, update, returned, ordered,
    region_in, adjacent_in, state_s, small_s, in_s, in_r, obs_s, obs_r, code_s, code_r, y_s, y_r, x_s, x_r, out_s, out_r, result_s,
):
    me = lax.axis_index("mem")
    reg = lax.axis_index("reg")
    chip = me // 2
    left, right = lax.rem(me + NMEM - 1, NMEM), lax.rem(me + 1, NMEM)
    below, above = lax.rem(reg + NREG - 1, NREG), lax.rem(reg + 1, NREG)
    ends = (me == 0, me == NMEM - 1)
    edge = jnp.logical_or(*ends)

    def block_of(phase, owner):
        return owner if phase == 0 else 2 * NMEM - 1 - owner

    core = lax.rem(me, 2)
    sibling = me + 1 - 2 * core
    barrier = pltpu.get_barrier_semaphore()

    def greet(target):
        pl.semaphore_signal(barrier, inc=1, device_id={"mem": target}, device_id_type=MESH)

    pl.when(core == 1)(lambda: greet(sibling))
    for i in range(1, 8):
        greet(2 * lax.rem(chip + i, 8))
    for side in (below, above):
        pl.semaphore_signal(
            barrier, inc=1, device_id={"mem": 2 * chip + 1, "reg": side}, device_id_type=MESH
        )

    def pass_barrier(hearer, count, passed):
        @pl.when(core == hearer)
        def _():
            pl.semaphore_wait(barrier, count)
            pl.semaphore_signal(passed, inc=1, device_id={"mem": sibling}, device_id_type=MESH)

        pl.when(core != hearer)(lambda: pl.semaphore_wait(passed, 1))

    def slab_of(step):
        away = 4 + lax.div(step + 1, 2) * (1 - 2 * lax.rem(step, 2))
        return lax.rem(chip + away, 8)

    def lanes(slab):
        return pl.ds(pl.multiple_of(slab * 128, 128), 128)

    def state_copy(phase):
        columns = pl.ds(phase * 1024, 1024)
        return pltpu.make_async_copy(
            x_hbm.at[:, :, columns], state.at[:, :, columns], state_s.at[phase]
        )

    small = [
        pltpu.make_async_copy(source, target, small_s.at[i])
        for i, (source, target) in enumerate(
            (
                (obs_hbm, obs_in), (coef_hbm, coef_in), (rinv_hbm, rinv_in), (site_hbm, site_in),
                (count_hbm, count_in), (near_hbm, near_in),
            )
        )
    ]

    state_copy(0).start()
    for copy in small:
        copy.start()
    state_copy(1).start()

    first = lax.broadcasted_iota(jnp.int32, (16, 128), 1) < 64
    mine = pl.ds(pl.multiple_of(me * 16, 16), 16)

    def reorder(slab):
        flat[...] = state[:, :, lanes(slab)].astype(F32).reshape(256, 128)
        for c in range(CHUNKS):
            even = flat[pl.ds(2 * c, 16, stride=16), :]
            odd = flat[pl.ds(2 * c + 1, 16, stride=16), :]
            packed[2 * slab, c] = jnp.where(first, even, pltpu.roll(odd, 64, 1)).astype(BF16)
            packed[2 * slab + 1, c] = jnp.where(first, pltpu.roll(even, 64, 1), odd).astype(BF16)

    def in_copy(phase, target):
        return pltpu.make_async_remote_copy(
            src_ref=packed.at[block_of(phase, target)],
            dst_ref=recv.at[phase, :, mine, :],
            send_sem=in_s.at[phase],
            recv_sem=in_r.at[phase],
            device_id={"mem": target},
            device_id_type=MESH,
        )

    def in_all(phase):
        others = recv.at[phase, :, pl.ds(0, K - 16), :]
        return pltpu.make_async_remote_copy(
            src_ref=others,
            dst_ref=others,
            send_sem=in_s.at[phase],
            recv_sem=in_r.at[phase],
            device_id={"mem": sibling},
            device_id_type=MESH,
        )

    def in_wait(phase):
        in_all(phase).wait_recv()

    half = me // 8

    def obs_target(j):
        block = 2 * me + j
        return jnp.where(half == 0, block, 2 * NMEM - 1 - block)

    def obs_copy(j):
        return pltpu.make_async_remote_copy(
            src_ref=obs_send.at[j],
            dst_ref=obs_recv.at[half],
            send_sem=obs_s.at[j],
            recv_sem=obs_r.at[half],
            device_id={"mem": obs_target(j)},
            device_id_type=MESH,
        )

    def obs_far(j):
        return obs_target(j) != me

    def first_in(step, carry):
        slab = slab_of(step)
        reorder(slab)
        for core in range(2):
            target = 2 * slab + core
            pl.when(target != me)(lambda target=target: in_copy(0, target).start())
        return carry

    with stage("barrier"):
        state_copy(0).wait()
        pass_barrier(0, NMEM - 1, region_in)
    with stage("first_in_a"):
        lax.fori_loop(0, 2, first_in, 0)

    with stage("obs_send"):
        for copy in small:
            copy.wait()
        row = lax.broadcasted_iota(jnp.int32, (16, OBS), 0)
        code = row - CODE_ROW
        away = jnp.abs(code // 3 - 1) + jnp.abs(lax.rem(code + 15, 3) - 1)
        taper = jnp.where(away == 0, 1.0, jnp.where(away == 1, 0.5, 0.25))
        for j in range(2):
            block = jnp.where(code == 4, 1.0, 0.0)
            for i in range(5):
                block = block + jnp.where(code == near_in[0, j : j + 1, i : i + 1], taper, 0.0)
            count = jnp.broadcast_to(count_in[0:1, j : j + 1].astype(F32), (16, OBS))
            obs_send[j] = jnp.where(row == 4, count, block)
            for i, ref in enumerate((obs_in, coef_in, rinv_in)):
                obs_send[j, i : i + 1, :] = ref[0, j : j + 1, :]
            obs_send[j, 3:4, :] = site_in[0, j : j + 1, :].astype(F32)
        for j in range(2):
            pl.when(obs_far(j))(lambda j=j: obs_copy(j).start())

            @pl.when(jnp.logical_not(obs_far(j)))
            def _(j=j):
                obs_recv[half] = obs_send[j]

    def partner(away, core):
        if away == 0:
            return 2 * chip + 1 - lax.rem(me, 2)
        turned = away * (1 - 2 * lax.rem(me, 2))
        return 2 * lax.rem(chip + 8 + turned, 8) + core

    def second_in(i, wanted):
        target = partner(*i)
        at_edge = jnp.logical_or(target == 0, target == NMEM - 1)
        pl.when(at_edge if wanted else jnp.logical_not(at_edge))(lambda: in_copy(1, target).start())

    def reorder_step(slab, carry):
        reorder(slab)
        return carry

    with stage("first_in_b"):
        lax.fori_loop(2, 8, first_in, 0)
    with stage("second_in"):
        state_copy(1).wait()
        reorder(8)
        reorder(15)
        for i in SENDS:
            second_in(i, True)
        lax.fori_loop(9, 15, reorder_step, 0)
        for i in SENDS[:EARLY]:
            second_in(i, False)
        recv[0, :, mine, :] = packed[me]
        recv[1, :, mine, :] = packed[block_of(1, me)]

    def code_copy(phase, side):
        return pltpu.make_async_remote_copy(
            src_ref=obs_recv.at[phase, :, 0:128],
            dst_ref=code_recv.at[phase, side],
            send_sem=code_s,
            recv_sem=code_r,
            device_id={"reg": above if side == 0 else below},
            device_id_type=MESH,
        )

    def codes_all():
        return pltpu.make_async_remote_copy(
            src_ref=code_recv,
            dst_ref=code_recv,
            send_sem=code_s,
            recv_sem=code_r,
            device_id={"reg": above},
            device_id_type=MESH,
        )

    with stage("onehot"):
        for phase in range(2):
            source = block_of(phase, me) // 2

            @pl.when(source != me)
            def _(phase=phase, source=source):
                pltpu.make_async_remote_copy(
                    src_ref=obs_send.at[0],
                    dst_ref=obs_recv.at[phase],
                    send_sem=obs_s.at[0],
                    recv_sem=obs_r.at[phase],
                    device_id={"mem": source},
                    device_id_type=MESH,
                ).wait_recv()

            site = obs_recv[phase, 3:4, :].astype(jnp.int32)
            for c in range(CHUNKS):
                place = lax.broadcasted_iota(jnp.int32, (128, OBS), 0) + c * 128
                onehot[phase, c * 128 : (c + 1) * 128, :] = jnp.where(place == site, 1.0, 0.0).astype(BF16)

    def observe(phase):
        values = jnp.concatenate([recv[phase, c] for c in range(CHUNKS)], axis=1)
        predicted = dot(values, onehot[phase]) * obs_recv[phase, 1:2, :]
        mean_pred = jnp.sum(predicted, axis=0, keepdims=True) * (1.0 / K)
        slot = lax.broadcasted_iota(jnp.int32, (1, OBS), 1).astype(F32)
        root = jnp.where(slot < obs_recv[phase, 4:5, :], jnp.sqrt(obs_recv[phase, 2:3, :]), 0.0)
        scaled = (root * (predicted - mean_pred)).astype(BF16)
        misfit = root * (obs_recv[phase, 0:1, :] - mean_pred)
        gram = dot_nt(scaled, scaled)
        a = misfit.astype(BF16).astype(F32)
        b = (misfit - a).astype(BF16).astype(F32)
        parts = rows_of([a, b, misfit - a - b], 16).astype(BF16)
        drive = jnp.sum(dot_nt(parts, scaled), axis=0, keepdims=True)
        row, column = square_indices(128)
        upper, lower = gram[:128, :128], gram[128:, 128:]
        diagonal = jnp.sum(jnp.where(row == column, lower, 0.0), axis=0, keepdims=True)
        for i, block in enumerate((jnp.where(row <= column, upper, lower), gram[:128, 128:])):
            own[phase, i * 128 : (i + 1) * 128, :] = block
            gmsg[phase, i * 128 : (i + 1) * 128, :] = block.astype(BF16)
        zero = jnp.zeros((1, 128), F32)
        tail = rows_of([drive[:, :128], drive[:, 128:], zero, zero, diagonal], MSG - PACK)
        own[phase, PACK:MSG, :] = tail
        gmsg[phase, PACK:MSG, :] = tail_rows(tail)

    def y_copy(phase, side, part):
        rows = slice(*PARTS[part])
        return pltpu.make_async_remote_copy(
            src_ref=gmsg.at[phase, rows],
            dst_ref=yrecv.at[phase, side, rows],
            send_sem=y_s.at[phase],
            recv_sem=y_r.at[phase, part],
            device_id={"mem": right if side == 0 else left},
            device_id_type=MESH,
        )

    def y_start(phase):
        for side in range(2):

            @pl.when(jnp.logical_not(ends[1 - side]))
            def _(side=side):
                for part in range(len(PARTS)):
                    y_copy(phase, side, part).start()

    def y_turn():
        for side in range(2):

            @pl.when(ends[side])
            def _(side=side):
                for phase in range(2):
                    yrecv[phase, side] = gmsg[1 - phase]

    def x_copy(phase, side, part):
        rows = slice(*PARTS[part])
        return pltpu.make_async_remote_copy(
            src_ref=xsend.at[phase, side, rows],
            dst_ref=xrecv.at[phase, side, rows],
            send_sem=x_s.at[phase],
            recv_sem=x_r.at[phase],
            device_id={"reg": above if side == 0 else below},
            device_id_type=MESH,
        )

    def y_wait(phase, rows, part, sent):
        def wait(sides):
            ref = yrecv.at[phase, sides, rows]
            copy = pltpu.make_async_remote_copy(
                src_ref=ref,
                dst_ref=ref,
                send_sem=y_s.at[phase],
                recv_sem=y_r.at[phase, part],
                device_id={"mem": sibling},
                device_id_type=MESH,
            )
            copy.wait_send() if sent else copy.wait_recv()

        pl.when(ends[0])(lambda: wait(slice(1, 2)))
        pl.when(ends[1])(lambda: wait(slice(0, 1)))
        pl.when(jnp.logical_not(edge))(lambda: wait(slice(0, 2)))

    def x_all(phase):
        return pltpu.make_async_remote_copy(
            src_ref=xsend.at[phase],
            dst_ref=xrecv.at[phase],
            send_sem=x_s.at[phase],
            recv_sem=x_r.at[phase],
            device_id={"reg": above},
            device_id_type=MESH,
        )

    def x_wait(phase):
        x_all(phase).wait_recv()

    def center_state(phase):
        for c in range(CHUNKS):
            values = recv[phase, c].astype(F32)
            average = jnp.sum(values, axis=0, keepdims=True) * (1.0 / K)
            mean[phase, :, c * 128 : (c + 1) * 128] = jnp.broadcast_to(average, (8, 128))
            spread[phase, :, c * 128 : (c + 1) * 128] = (values - average).astype(BF16)

    def sum_row(phase):
        def weighted(weights, first_code, rows):
            w = [weights[CODE_ROW + first_code + i : CODE_ROW + first_code + i + 1, :] for i in range(3)]
            return (
                w[0] * yrecv[phase, phase, rows, :].astype(F32)
                + w[1] * own[phase, rows, :]
                + w[2] * yrecv[phase, 1 - phase, rows, :].astype(F32)
            )

        for part in range(len(PARTS)):
            rows = slice(part * 128, (part + 1) * 128)
            y_wait(phase, slice(*PARTS[part]), part, False)
            for side in range(2):
                weights = code_recv[phase, 1 - side]
                first_code = 0 if side == 0 else 6
                xsend[phase, side, rows, :] = weighted(weights, first_code, rows).astype(BF16)
                if part == len(PARTS) - 1:
                    tail = weighted(weights, first_code, slice(PACK, MSG))
                    xsend[phase, side, PACK:MSG, :] = tail_rows(tail)
                x_copy(phase, side, part).start()
        center[phase] = weighted(obs_recv[phase, :, 0:128], 3, slice(0, MSG))

    def transform(phase):
        total = center[phase] + xrecv[phase, 0].astype(F32) + xrecv[phase, 1].astype(F32)
        tail = total[PACK:MSG]
        drive = jnp.concatenate([tail[0:1] + tail[2:3], tail[1:2] + tail[3:4]], axis=1)
        row, column = square_indices(128)
        corner, cut = total[128:256], total[0:128]
        turned = cut.T
        first_block = jnp.where(row <= column, cut, turned) + jnp.where(row == column, K - 1.0, 0.0)
        last_block = jnp.where(row == column, tail[4:5] + (K - 1.0), jnp.where(row > column, cut, turned))
        system = jnp.concatenate(
            [
                jnp.concatenate([first_block, corner], axis=1),
                jnp.concatenate([corner.T, last_block], axis=1),
            ],
            axis=0,
        )
        scale = jnp.max(jnp.sum(jnp.abs(system), axis=0, keepdims=True), axis=1, keepdims=True)
        half_root = newton_root(system / scale) / jnp.sqrt(scale)
        halves = split2(half_root)
        vector = jnp.broadcast_to(drive, (16, K))
        vector = dot3(split2(vector), halves)
        vector = dot3(split2(vector), halves)[0:1]
        return (jnp.float32(K - 1.0) ** 0.5 * half_root + vector).astype(BF16)

    def apply(phase, weights):
        for c in range(0, CHUNKS, 2):
            columns = slice(c * 128, (c + 2) * 128)
            result = dot(weights, spread[phase, :, columns]) + mean[phase, 0:1, columns]
            update[phase, c] = result[:, :128].astype(BF16)
            update[phase, c + 1] = result[:, 128:].astype(BF16)

    def out_copy(phase, target):
        rows = pl.ds(pl.multiple_of(target * 16, 16), 16)
        return pltpu.make_async_remote_copy(
            src_ref=update.at[phase, :, rows, :],
            dst_ref=returned.at[phase, me],
            send_sem=out_s.at[phase],
            recv_sem=out_r.at[phase, chip],
            device_id={"mem": target},
            device_id_type=MESH,
        )

    def send_out(phase, offsets):
        for i in offsets:
            out_copy(phase, partner(*i)).start()

    def keep_own(phase):
        returned[phase, me] = update[phase, :, mine, :]

    def result_copy(slab):
        return pltpu.make_async_copy(
            ordered.at[:, :, lanes(slab)], out_hbm.at[:, :, lanes(slab)], result_s
        )

    def order_back(phase):
        def one(step, carry):
            source_chip = lax.rem(16 - slab_of(step) + 2 * chip, 8)
            def arrived(blocks):
                pltpu.make_async_remote_copy(
                    src_ref=returned.at[phase, blocks],
                    dst_ref=returned.at[phase, blocks],
                    send_sem=out_s.at[phase],
                    recv_sem=out_r.at[phase, source_chip],
                    device_id={"mem": sibling},
                    device_id_type=MESH,
                ).wait_recv()

            pl.when(source_chip != chip)(lambda: arrived(pl.ds(2 * source_chip, 2)))
            pl.when(source_chip == chip)(lambda: arrived(pl.ds(sibling, 1)))
            for c in range(CHUNKS):
                a = returned[phase, 2 * source_chip + phase, c].astype(F32)
                b = returned[phase, 2 * source_chip + 1 - phase, c].astype(F32)
                flat[pl.ds(2 * c, 16, stride=16), :] = jnp.where(first, a, pltpu.roll(b, 64, 1))
                flat[pl.ds(2 * c + 1, 16, stride=16), :] = jnp.where(first, pltpu.roll(a, 64, 1), b)
            slab = source_chip if phase == 0 else 15 - source_chip
            ordered[:, :, lanes(slab)] = flat[...].reshape(16, 16, 128).astype(BF16)
            result_copy(slab).start()
            return carry

        lax.fori_loop(0, 8, one, 0)

    with stage("adjacent"):
        pass_barrier(1, 4, adjacent_in)
        for phase in range(2):
            for side in range(2):
                code_copy(phase, side).start()
    with stage("in_wait0"):
        in_wait(0)
    with stage("observe0"):
        observe(0)
    y_start(0)

    def second_in_rest():
        for i in SENDS[EARLY:]:
            second_in(i, False)

    with stage("second_in_b"):
        pl.when(jnp.logical_not(edge))(second_in_rest)
    with stage("edge"):

        @pl.when(edge)
        def _():
            in_wait(1)
            observe(1)
            y_turn()
            y_start(1)
            second_in_rest()

    with stage("center0"):
        center_state(0)
    with stage("sum_row0"):
        codes_all().wait_recv()
        sum_row(0)
    with stage("in_wait1"):
        pl.when(jnp.logical_not(edge))(lambda: in_wait(1))
    with stage("observe1"):

        @pl.when(jnp.logical_not(edge))
        def _():
            observe(1)
            y_start(1)

    with stage("x_wait0"):
        x_wait(0)
    with stage("transform0"):
        weights = transform(0)
    with stage("apply0"):
        apply(0, weights)
    send_out(0, SENDS)
    with stage("sum_row1"):
        sum_row(1)
    with stage("center1"):
        keep_own(0)
        center_state(1)
    with stage("x_wait1"):
        x_wait(1)
    with stage("transform1"):
        weights = transform(1)
    with stage("apply1"):
        apply(1, weights)
    send_out(1, SENDS)
    keep_own(1)
    with stage("sent"):
        for phase in range(2):
            in_all(phase).wait_send()
            y_wait(phase, slice(0, MSG), 0, True)
            x_all(phase).wait_send()
        codes_all().wait_send()
        for j in range(2):
            pl.when(obs_far(j))(lambda j=j: obs_copy(j).wait_send())
    with stage("back0"):
        order_back(0)
    with stage("back1"):
        order_back(1)

    with stage("drain"):
        for phase in range(2):
            others = update.at[phase, :, pl.ds(0, K - 16), :]
            pltpu.make_async_remote_copy(
                src_ref=others,
                dst_ref=others,
                send_sem=out_s.at[phase],
                recv_sem=out_r.at[phase, chip],
                device_id={"mem": sibling},
                device_id_type=MESH,
            ).wait_send()
        pltpu.make_async_copy(ordered, out_hbm, result_s).wait()


def per_device(background, observations, obs_coef, obs_rinv, obs_site, obs_count, neighbours):
    dma = pltpu.SemaphoreType.DMA
    small = (observations, obs_coef, obs_rinv, obs_site, obs_count, neighbours)
    return pl.pallas_call(
        kernel,
        out_shape=jax.ShapeDtypeStruct(background.shape, BF16),
        in_specs=[pl.BlockSpec(memory_space=pltpu.HBM)] * 7,
        out_specs=pl.BlockSpec(memory_space=pl.ANY),
        scratch_shapes=[
            pltpu.VMEM(background.shape, BF16),
            *(pltpu.VMEM(array.shape, array.dtype) for array in small),
            pltpu.VMEM((256, 128), F32),
            pltpu.VMEM((2 * NMEM, CHUNKS, 16, 128), BF16),
            pltpu.VMEM((2, CHUNKS, K, 128), BF16),
            pltpu.VMEM((2, 16, OBS), F32),
            pltpu.VMEM((2, 16, OBS), F32),
            pltpu.VMEM((2, 2, 16, 128), F32),
            pltpu.VMEM((2, CHUNKS * 128, OBS), BF16),
            pltpu.VMEM((2, MSG, 128), F32),
            pltpu.VMEM((2, MSG, 128), BF16),
            pltpu.VMEM((2, 2, MSG, 128), BF16),
            pltpu.VMEM((2, MSG, 128), F32),
            pltpu.VMEM((2, 2, MSG, 128), BF16),
            pltpu.VMEM((2, 2, MSG, 128), BF16),
            pltpu.VMEM((2, K, CHUNKS * 128), BF16),
            pltpu.VMEM((2, 8, CHUNKS * 128), F32),
            pltpu.VMEM((2, CHUNKS, K, 128), BF16),
            pltpu.VMEM((2, NMEM, CHUNKS, 16, 128), BF16),
            pltpu.VMEM(background.shape, BF16),
            pltpu.SemaphoreType.REGULAR, pltpu.SemaphoreType.REGULAR,
            dma((2,)), dma((6,)),
            dma((2,)), dma((2,)),
            dma((2,)), dma((2,)),
            dma, dma,
            dma((2,)), dma((2, len(PARTS))),
            dma((2,)), dma((2,)),
            dma((2,)), dma((2, 8)),
            dma,
        ],
        compiler_params=pltpu.CompilerParams(
            collective_id=0, has_side_effects=True, vmem_limit_bytes=62 << 20
        ),
        name="analysis",
    )(background, *small)


def solution(mesh):
    in_specs = (
        P("mem", None, "reg"),
        P("reg", "mem", None),
        P("reg", "mem", None),
        P("reg", "mem", None),
        P("reg", "mem", None),
        P("reg", "mem"),
        P("reg", "mem", None),
    )
    out_specs = P("mem", None, "reg")
    return jax.shard_map(
        per_device, mesh=mesh, in_specs=in_specs, out_specs=out_specs, check_vma=False
    )
```

```python
import contextlib

import jax
import jax.numpy as jnp
from jax import lax
from jax.experimental import pallas as pl
from jax.experimental.pallas import tpu as pltpu
from jax.sharding import PartitionSpec as P

MESH = pl.DeviceIdType.MESH
F32 = jnp.float32
BF16 = jnp.bfloat16
NS_ITERS = 4
NMEM = 16
NREG = 32
K = 256
OBS = 384
CHUNKS = 8
PACK = 256
MSG = 272
PARTS = ((0, 128), (128, MSG))
CODE_ROW = 5
SENDS = tuple((away, core) for away in (4, 3, -3, 2, -2, 1, -1) for core in range(2)) + ((0, 0),)
EARLY = 6


def split2(x):
    high = x.astype(BF16)
    low = (x - high.astype(F32)).astype(BF16)
    return high, low


def dot(a, b):
    return jnp.dot(a, b, preferred_element_type=F32)


def dot_nt(a, b):
    return lax.dot_general(a, b, (((1,), (1,)), ((), ())), preferred_element_type=F32)


def dot3(a, b):
    return dot(a[0], b[0]) + (dot(a[0], b[1]) + dot(a[1], b[0]))


def rows_of(parts, rows):
    width = parts[0].shape[1]
    index = lax.broadcasted_iota(jnp.int32, (rows, width), 0)
    block = jnp.zeros((rows, width), F32)
    for i, part in enumerate(parts):
        block = jnp.where(index == i, part, block)
    return block


def tail_rows(tail):
    low_half, high_half = tail[0:1] + tail[2:3], tail[1:2] + tail[3:4]
    a, b = low_half.astype(BF16).astype(F32), high_half.astype(BF16).astype(F32)
    return rows_of([a, b, low_half - a, high_half - b, tail[4:5]], MSG - PACK).astype(BF16)


def square_indices(n):
    return lax.broadcasted_iota(jnp.int32, (n, n), 0), lax.broadcasted_iota(jnp.int32, (n, n), 1)


def newton_root(matrix):
    row, column = square_indices(matrix.shape[0])
    level = jnp.sum(jnp.where(row == column, matrix, 0.0), axis=0, keepdims=True)
    level = jnp.sum(level, axis=1, keepdims=True) * (1.0 / matrix.shape[0])

    def product(left, right):
        inner = dot(left[2], right[2])
        return left[0] * right[0], left[0] * right[1] + (right[0] * left[1] + inner)

    def rounded(value, rest):
        return value, rest, rest.astype(BF16)

    def middle_of(value, rest):
        return rounded(1.5 - 0.5 * value, -0.5 * rest)

    current = rounded(level, jnp.where(row == column, matrix - level, matrix))
    middle = middle_of(*current[:2])
    inverse = middle
    current = rounded(*product(current, inverse))
    for step in range(1, NS_ITERS):
        middle = middle_of(*product(inverse, current))
        if step < NS_ITERS - 1:
            current = rounded(*product(current, middle))
        inverse = rounded(*product(middle, inverse))
    return jnp.where(row == column, inverse[0] + inverse[1], inverse[1])


def stage(name):
    return contextlib.nullcontext()


def kernel(
    x_hbm, obs_hbm, coef_hbm, rinv_hbm, site_hbm, count_hbm, near_hbm, out_hbm,
    state, obs_in, coef_in, rinv_in, site_in, count_in, near_in,
    flat, packed, recv, obs_send, obs_recv, code_recv, onehot, own, gmsg, ysend, yrecv, center, xsend, xrecv, turned,
    spread, mean, update, returned, ordered,
    region_in, adjacent_in, state_s, small_s, in_s, in_r, obs_s, obs_r, code_s, code_r, y_s, y_r, x_s, x_r, turn_s, turn_r, out_s, out_r, result_s,
):
    me = lax.axis_index("mem")
    reg = lax.axis_index("reg")
    chip = me // 2
    left, right = lax.rem(me + NMEM - 1, NMEM), lax.rem(me + 1, NMEM)
    below, above = lax.rem(reg + NREG - 1, NREG), lax.rem(reg + 1, NREG)
    ends = (me == 0, me == NMEM - 1)
    edge = jnp.logical_or(*ends)

    def block_of(phase, owner):
        return owner if phase == 0 else 2 * NMEM - 1 - owner

    core = lax.rem(me, 2)
    sibling = me + 1 - 2 * core
    barrier = pltpu.get_barrier_semaphore()

    def greet(target):
        pl.semaphore_signal(barrier, inc=1, device_id={"mem": target}, device_id_type=MESH)

    pl.when(core == 1)(lambda: greet(sibling))
    for i in (4, 3, 5, 2, 6, 1, 7):
        greet(2 * lax.rem(chip + i, 8))
    for side in (below, above):
        pl.semaphore_signal(
            barrier, inc=1, device_id={"mem": 2 * chip + 1, "reg": side}, device_id_type=MESH
        )

    def pass_barrier(hearer, count, passed):
        @pl.when(core == hearer)
        def _():
            pl.semaphore_wait(barrier, count)
            pl.semaphore_signal(passed, inc=1, device_id={"mem": sibling}, device_id_type=MESH)

        pl.when(core != hearer)(lambda: pl.semaphore_wait(passed, 1))

    def slab_of(step):
        away = 4 + lax.div(step + 1, 2) * (1 - 2 * lax.rem(step, 2))
        return lax.rem(chip + away, 8)

    def lanes(slab):
        return pl.ds(pl.multiple_of(slab * 128, 128), 128)

    def state_copy(phase):
        columns = pl.ds(phase * 1024, 1024)
        return pltpu.make_async_copy(
            x_hbm.at[:, :, columns], state.at[:, :, columns], state_s.at[phase]
        )

    small = [
        pltpu.make_async_copy(source, target, small_s.at[i])
        for i, (source, target) in enumerate(
            (
                (obs_hbm, obs_in), (coef_hbm, coef_in), (rinv_hbm, rinv_in), (site_hbm, site_in),
                (count_hbm, count_in), (near_hbm, near_in),
            )
        )
    ]

    state_copy(0).start()
    for copy in small:
        copy.start()
    state_copy(1).start()

    first = lax.broadcasted_iota(jnp.int32, (16, 128), 1) < 64
    mine = pl.ds(pl.multiple_of(me * 16, 16), 16)

    def reorder(slab):
        flat[...] = state[:, :, lanes(slab)].astype(F32).reshape(256, 128)
        for c in range(CHUNKS):
            even = flat[pl.ds(2 * c, 16, stride=16), :]
            odd = flat[pl.ds(2 * c + 1, 16, stride=16), :]
            packed[2 * slab, c] = jnp.where(first, even, pltpu.roll(odd, 64, 1)).astype(BF16)
            packed[2 * slab + 1, c] = jnp.where(first, pltpu.roll(even, 64, 1), odd).astype(BF16)

    def in_copy(phase, target):
        return pltpu.make_async_remote_copy(
            src_ref=packed.at[block_of(phase, target)],
            dst_ref=recv.at[phase, :, mine, :],
            send_sem=in_s.at[phase],
            recv_sem=in_r.at[phase],
            device_id={"mem": target},
            device_id_type=MESH,
        )

    def in_all(phase):
        others = recv.at[phase, :, pl.ds(0, K - 16), :]
        return pltpu.make_async_remote_copy(
            src_ref=others,
            dst_ref=others,
            send_sem=in_s.at[phase],
            recv_sem=in_r.at[phase],
            device_id={"mem": sibling},
            device_id_type=MESH,
        )

    def in_wait(phase):
        in_all(phase).wait_recv()

    half = me // 8

    def obs_target(j):
        block = 2 * me + j
        return jnp.where(half == 0, block, 2 * NMEM - 1 - block)

    def obs_copy(j):
        return pltpu.make_async_remote_copy(
            src_ref=obs_send.at[j],
            dst_ref=obs_recv.at[half],
            send_sem=obs_s.at[j],
            recv_sem=obs_r.at[half],
            device_id={"mem": obs_target(j)},
            device_id_type=MESH,
        )

    def obs_far(j):
        return obs_target(j) != me

    def first_in(step, carry):
        slab = slab_of(step)
        reorder(slab)
        for core in range(2):
            target = 2 * slab + core
            pl.when(target != me)(lambda target=target: in_copy(0, target).start())
        return carry

    with stage("barrier"):
        state_copy(0).wait()
        pass_barrier(0, NMEM - 1, region_in)
    with stage("obs_send"):
        for copy in small:
            copy.wait()
        row = lax.broadcasted_iota(jnp.int32, (16, OBS), 0)
        code = row - CODE_ROW
        away = jnp.abs(code // 3 - 1) + jnp.abs(lax.rem(code + 15, 3) - 1)
        taper = jnp.where(away == 0, 1.0, jnp.where(away == 1, 0.5, 0.25))
        for j in range(2):
            block = jnp.where(code == 4, 1.0, 0.0)
            for i in range(5):
                block = block + jnp.where(code == near_in[0, j : j + 1, i : i + 1], taper, 0.0)
            count = jnp.broadcast_to(count_in[0:1, j : j + 1].astype(F32), (16, OBS))
            obs_send[j] = jnp.where(row == 4, count, block)
            for i, ref in enumerate((obs_in, coef_in, rinv_in)):
                obs_send[j, i : i + 1, :] = ref[0, j : j + 1, :]
            obs_send[j, 3:4, :] = site_in[0, j : j + 1, :].astype(F32)
        for j in range(2):
            pl.when(obs_far(j))(lambda j=j: obs_copy(j).start())

            @pl.when(jnp.logical_not(obs_far(j)))
            def _(j=j):
                obs_recv[half] = obs_send[j]

    def partner(away, core):
        if away == 0:
            return 2 * chip + 1 - lax.rem(me, 2)
        turned = away * (1 - 2 * lax.rem(me, 2))
        return 2 * lax.rem(chip + 8 + turned, 8) + core

    def second_in(i, wanted):
        target = partner(*i)
        at_edge = jnp.logical_or(target == 0, target == NMEM - 1)
        pl.when(at_edge if wanted else jnp.logical_not(at_edge))(lambda: in_copy(1, target).start())

    def reorder_step(slab, carry):
        reorder(slab)
        return carry

    with stage("first_in"):
        lax.fori_loop(0, 8, first_in, 0)
    with stage("second_in"):
        state_copy(1).wait()
        reorder(8)
        reorder(15)
        for i in SENDS:
            second_in(i, True)
        lax.fori_loop(9, 15, reorder_step, 0)
        recv[0, :, mine, :] = packed[me]
        recv[1, :, mine, :] = packed[block_of(1, me)]

    def code_copy(phase, side):
        if phase == 0:
            target = {"mem": right if side == 0 else left}
        else:
            target = {"reg": above if side == 0 else below}
        return pltpu.make_async_remote_copy(
            src_ref=obs_recv.at[phase, :, 0:128],
            dst_ref=code_recv.at[phase, side],
            send_sem=code_s.at[phase],
            recv_sem=code_r.at[phase],
            device_id=target,
            device_id_type=MESH,
        )

    def along_line(copy):
        for side in range(2):
            pl.when(jnp.logical_not(ends[1 - side]))(lambda side=side: copy(side).start())

    def sides_wait(ref, send_sem, recv_sem, sent):
        copy = pltpu.make_async_remote_copy(
            src_ref=ref,
            dst_ref=ref,
            send_sem=send_sem,
            recv_sem=recv_sem,
            device_id={"mem": sibling},
            device_id_type=MESH,
        )
        copy.wait_send() if sent else copy.wait_recv()

    def line_wait(ref_of, send_sem, recv_sem, sent):
        pl.when(ends[0])(lambda: sides_wait(ref_of(slice(1, 2)), send_sem, recv_sem, sent))
        pl.when(ends[1])(lambda: sides_wait(ref_of(slice(0, 1)), send_sem, recv_sem, sent))
        pl.when(jnp.logical_not(edge))(
            lambda: sides_wait(ref_of(slice(0, 2)), send_sem, recv_sem, sent)
        )

    def code_wait(phase, sent):
        if phase == 0:
            line_wait(lambda sides: code_recv.at[0, sides], code_s.at[0], code_r.at[0], sent)
        else:
            sides_wait(code_recv.at[1], code_s.at[1], code_r.at[1], sent)

    with stage("onehot"):
        for phase in range(2):
            source = block_of(phase, me) // 2

            @pl.when(source != me)
            def _(phase=phase, source=source):
                pltpu.make_async_remote_copy(
                    src_ref=obs_send.at[0],
                    dst_ref=obs_recv.at[phase],
                    send_sem=obs_s.at[0],
                    recv_sem=obs_r.at[phase],
                    device_id={"mem": source},
                    device_id_type=MESH,
                ).wait_recv()

            if phase == 0:
                along_line(lambda side: code_copy(0, side))
            site = obs_recv[phase, 3:4, :].astype(jnp.int32)
            for c in range(CHUNKS):
                place = lax.broadcasted_iota(jnp.int32, (128, OBS), 0) + c * 128
                onehot[phase, c * 128 : (c + 1) * 128, :] = jnp.where(place == site, 1.0, 0.0).astype(BF16)

    with stage("second_out"):
        for i in SENDS[:EARLY]:
            second_in(i, False)
    with stage("adjacent"):
        pass_barrier(1, 4, adjacent_in)
        for side in range(2):
            code_copy(1, side).start()

    def observe(phase):
        values = jnp.concatenate([recv[phase, c] for c in range(CHUNKS)], axis=1)
        predicted = dot(values, onehot[phase]) * obs_recv[phase, 1:2, :]
        mean_pred = jnp.sum(predicted, axis=0, keepdims=True) * (1.0 / K)
        slot = lax.broadcasted_iota(jnp.int32, (1, OBS), 1).astype(F32)
        root = jnp.where(slot < obs_recv[phase, 4:5, :], jnp.sqrt(obs_recv[phase, 2:3, :]), 0.0)
        scaled = (root * (predicted - mean_pred)).astype(BF16)
        misfit = root * (obs_recv[phase, 0:1, :] - mean_pred)
        gram = dot_nt(scaled, scaled)
        a = misfit.astype(BF16).astype(F32)
        b = (misfit - a).astype(BF16).astype(F32)
        parts = rows_of([a, b, misfit - a - b], 16).astype(BF16)
        drive = jnp.sum(dot_nt(parts, scaled), axis=0, keepdims=True)
        row, column = square_indices(128)
        upper, lower = gram[:128, :128], gram[128:, 128:]
        diagonal = jnp.sum(jnp.where(row == column, lower, 0.0), axis=0, keepdims=True)
        for i, block in enumerate((jnp.where(row <= column, upper, lower), gram[:128, 128:])):
            own[phase, i * 128 : (i + 1) * 128, :] = block
            gmsg[phase, i * 128 : (i + 1) * 128, :] = block.astype(BF16)
        zero = jnp.zeros((1, 128), F32)
        tail = rows_of([drive[:, :128], drive[:, 128:], zero, zero, diagonal], MSG - PACK)
        own[phase, PACK:MSG, :] = tail
        gmsg[phase, PACK:MSG, :] = tail_rows(tail)

    def y_copy(phase, side, part):
        rows = slice(*PARTS[part])
        return pltpu.make_async_remote_copy(
            src_ref=ysend.at[side, rows] if phase == 0 else gmsg.at[1, rows],
            dst_ref=yrecv.at[phase, side, rows],
            send_sem=y_s.at[phase],
            recv_sem=y_r.at[phase, part],
            device_id={"mem": right if side == 0 else left},
            device_id_type=MESH,
        )

    def y_wait(phase, rows, part, sent):
        line_wait(
            lambda sides: yrecv.at[phase, sides, rows], y_s.at[phase], y_r.at[phase, part], sent
        )

    def y_start():
        for part in range(len(PARTS)):
            along_line(lambda side, part=part: y_copy(1, side, part))

    def x_copy(phase, side, part):
        rows = slice(*PARTS[part])
        return pltpu.make_async_remote_copy(
            src_ref=gmsg.at[0, rows] if phase == 0 else xsend.at[side, rows],
            dst_ref=xrecv.at[phase, side, rows],
            send_sem=x_s.at[phase],
            recv_sem=x_r.at[phase],
            device_id={"reg": above if side == 0 else below},
            device_id_type=MESH,
        )

    def x_wait(phase, sent=False):
        sides_wait(xrecv.at[phase], x_s.at[phase], x_r.at[phase], sent)

    def turn_copy(side):
        return pltpu.make_async_remote_copy(
            src_ref=gmsg.at[1],
            dst_ref=turned.at[side],
            send_sem=turn_s,
            recv_sem=turn_r,
            device_id={"reg": above if side == 0 else below},
            device_id_type=MESH,
        )

    def center_state(phase):
        for c in range(CHUNKS):
            values = recv[phase, c].astype(F32)
            average = jnp.sum(values, axis=0, keepdims=True) * (1.0 / K)
            mean[phase, :, c * 128 : (c + 1) * 128] = jnp.broadcast_to(average, (8, 128))
            spread[phase, :, c * 128 : (c + 1) * 128] = (values - average).astype(BF16)

    def weighted(weights, codes, terms, rows):
        total = None
        for code, term in zip(codes, terms):
            term = weights[CODE_ROW + code : CODE_ROW + code + 1, :] * term[rows, :].astype(F32)
            total = term if total is None else total + term
        return total

    def part_sum(target, weights, codes, terms, part):
        rows = slice(part * 128, (part + 1) * 128)
        target[rows, :] = weighted(weights, codes, terms, rows).astype(BF16)
        if part == len(PARTS) - 1:
            target[PACK:MSG, :] = tail_rows(weighted(weights, codes, terms, slice(PACK, MSG)))

    def keep_turn(side):
        yrecv[1, side] = gmsg[0]

    def sum_column():
        x_wait(0)
        code_wait(0, False)
        terms = (xrecv.at[0, 0], own.at[0], xrecv.at[0, 1])
        for part in range(len(PARTS)):
            for side in range(2):
                codes = (0, 3, 6) if side == 0 else (2, 5, 8)

                @pl.when(jnp.logical_not(ends[1 - side]))
                def _(side=side, codes=codes):
                    part_sum(ysend.at[side], code_recv[0, 1 - side], codes, terms, part)
                    y_copy(0, side, part).start()

        center[0] = weighted(obs_recv[0, :, 0:128], (1, 4, 7), terms, slice(0, MSG))

    def sum_turn():
        sides_wait(turned, turn_s, turn_r, False)
        terms = (turned.at[0], own.at[1], turned.at[1])
        for side in range(2):

            @pl.when(ends[side])
            def _(side=side):
                for part in range(len(PARTS)):
                    codes = (0, 3, 6) if side == 0 else (2, 5, 8)
                    part_sum(yrecv.at[0, side], obs_recv[0, :, 0:128], codes, terms, part)

    def sum_row():
        code_wait(1, False)
        terms = (yrecv.at[1, 1], own.at[1], yrecv.at[1, 0])
        for part in range(len(PARTS)):
            y_wait(1, slice(*PARTS[part]), part, False)
            for side in range(2):
                codes = (0, 1, 2) if side == 0 else (6, 7, 8)
                part_sum(xsend.at[side], code_recv[1, 1 - side], codes, terms, part)
                x_copy(1, side, part).start()
        center[1] = weighted(obs_recv[1, :, 0:128], (3, 4, 5), terms, slice(0, MSG))

    def transform(phase):
        sides = yrecv if phase == 0 else xrecv
        total = center[phase] + sides[phase, 0].astype(F32) + sides[phase, 1].astype(F32)
        tail = total[PACK:MSG]
        drive = jnp.concatenate([tail[0:1] + tail[2:3], tail[1:2] + tail[3:4]], axis=1)
        row, column = square_indices(128)
        corner, cut = total[128:256], total[0:128]
        turned = cut.T
        first_block = jnp.where(row <= column, cut, turned) + jnp.where(row == column, K - 1.0, 0.0)
        last_block = jnp.where(row == column, tail[4:5] + (K - 1.0), jnp.where(row > column, cut, turned))
        system = jnp.concatenate(
            [
                jnp.concatenate([first_block, corner], axis=1),
                jnp.concatenate([corner.T, last_block], axis=1),
            ],
            axis=0,
        )
        scale = jnp.max(jnp.sum(jnp.abs(system), axis=0, keepdims=True), axis=1, keepdims=True)
        half_root = newton_root(system / scale) / jnp.sqrt(scale)
        halves = split2(half_root)
        vector = jnp.broadcast_to(drive, (16, K))
        vector = dot3(split2(vector), halves)
        vector = dot3(split2(vector), halves)[0:1]
        return (jnp.float32(K - 1.0) ** 0.5 * half_root + vector).astype(BF16)

    def apply(phase, weights):
        for c in range(0, CHUNKS, 2):
            columns = slice(c * 128, (c + 2) * 128)
            result = dot(weights, spread[phase, :, columns]) + mean[phase, 0:1, columns]
            update[phase, c] = result[:, :128].astype(BF16)
            update[phase, c + 1] = result[:, 128:].astype(BF16)

    def out_copy(phase, target):
        rows = pl.ds(pl.multiple_of(target * 16, 16), 16)
        return pltpu.make_async_remote_copy(
            src_ref=update.at[phase, :, rows, :],
            dst_ref=returned.at[phase, me],
            send_sem=out_s.at[phase],
            recv_sem=out_r.at[phase, chip],
            device_id={"mem": target},
            device_id_type=MESH,
        )

    def send_out(phase, offsets):
        for i in offsets:
            out_copy(phase, partner(*i)).start()

    def keep_own(phase):
        returned[phase, me] = update[phase, :, mine, :]

    def result_copy(slab):
        return pltpu.make_async_copy(
            ordered.at[:, :, lanes(slab)], out_hbm.at[:, :, lanes(slab)], result_s
        )

    def order_back(phase):
        def one(step, carry):
            source_chip = lax.rem(16 - slab_of(step) + 2 * chip, 8)
            def arrived(blocks):
                pltpu.make_async_remote_copy(
                    src_ref=returned.at[phase, blocks],
                    dst_ref=returned.at[phase, blocks],
                    send_sem=out_s.at[phase],
                    recv_sem=out_r.at[phase, source_chip],
                    device_id={"mem": sibling},
                    device_id_type=MESH,
                ).wait_recv()

            pl.when(source_chip != chip)(lambda: arrived(pl.ds(2 * source_chip, 2)))
            pl.when(source_chip == chip)(lambda: arrived(pl.ds(sibling, 1)))
            for c in range(CHUNKS):
                a = returned[phase, 2 * source_chip + phase, c].astype(F32)
                b = returned[phase, 2 * source_chip + 1 - phase, c].astype(F32)
                flat[pl.ds(2 * c, 16, stride=16), :] = jnp.where(first, a, pltpu.roll(b, 64, 1))
                flat[pl.ds(2 * c + 1, 16, stride=16), :] = jnp.where(first, pltpu.roll(a, 64, 1), b)
            slab = source_chip if phase == 0 else 15 - source_chip
            ordered[:, :, lanes(slab)] = flat[...].reshape(16, 16, 128).astype(BF16)
            result_copy(slab).start()
            return carry

        lax.fori_loop(0, 8, one, 0)

    with stage("in_wait0"):
        in_wait(0)
    with stage("observe0"):
        observe(0)
        for part in range(len(PARTS)):
            for side in range(2):
                x_copy(0, side, part).start()
        for i in SENDS[EARLY:]:
            second_in(i, False)
    with stage("edge"):

        @pl.when(edge)
        def _():
            in_wait(1)
            observe(1)
            for side in range(2):
                turn_copy(side).start()
                pl.when(ends[side])(lambda side=side: keep_turn(side))
            y_start()

    with stage("center0"):
        center_state(0)
    with stage("sum_column"):
        sum_column()
    with stage("in_wait1"):
        pl.when(jnp.logical_not(edge))(lambda: in_wait(1))
    with stage("observe1"):

        @pl.when(jnp.logical_not(edge))
        def _():
            observe(1)
            y_start()

    with stage("sum_turn"):
        pl.when(edge)(sum_turn)
    with stage("y_wait0"):
        for part in range(len(PARTS)):
            y_wait(0, slice(*PARTS[part]), part, False)
    with stage("transform0"):
        weights = transform(0)
    with stage("apply0"):
        apply(0, weights)
    send_out(0, SENDS)
    with stage("sum_row1"):
        sum_row()
    with stage("center1"):
        keep_own(0)
        center_state(1)
    with stage("x_wait1"):
        x_wait(1)
    with stage("transform1"):
        weights = transform(1)
    with stage("apply1"):
        apply(1, weights)
    send_out(1, SENDS)
    keep_own(1)
    with stage("sent"):
        for phase in range(2):
            in_all(phase).wait_send()
            y_wait(phase, slice(0, MSG), 0, True)
            x_wait(phase, True)
            code_wait(phase, True)
        pl.when(edge)(lambda: sides_wait(turned, turn_s, turn_r, True))
        for j in range(2):
            pl.when(obs_far(j))(lambda j=j: obs_copy(j).wait_send())
    with stage("back0"):
        order_back(0)
    with stage("back1"):
        order_back(1)

    with stage("drain"):
        for phase in range(2):
            others = update.at[phase, :, pl.ds(0, K - 16), :]
            pltpu.make_async_remote_copy(
                src_ref=others,
                dst_ref=others,
                send_sem=out_s.at[phase],
                recv_sem=out_r.at[phase, chip],
                device_id={"mem": sibling},
                device_id_type=MESH,
            ).wait_send()
        pltpu.make_async_copy(ordered, out_hbm, result_s).wait()


def per_device(background, observations, obs_coef, obs_rinv, obs_site, obs_count, neighbours):
    dma = pltpu.SemaphoreType.DMA
    small = (observations, obs_coef, obs_rinv, obs_site, obs_count, neighbours)
    return pl.pallas_call(
        kernel,
        out_shape=jax.ShapeDtypeStruct(background.shape, BF16),
        in_specs=[pl.BlockSpec(memory_space=pltpu.HBM)] * 7,
        out_specs=pl.BlockSpec(memory_space=pl.ANY),
        scratch_shapes=[
            pltpu.VMEM(background.shape, BF16),
            *(pltpu.VMEM(array.shape, array.dtype) for array in small),
            pltpu.VMEM((256, 128), F32),
            pltpu.VMEM((2 * NMEM, CHUNKS, 16, 128), BF16),
            pltpu.VMEM((2, CHUNKS, K, 128), BF16),
            pltpu.VMEM((2, 16, OBS), F32),
            pltpu.VMEM((2, 16, OBS), F32),
            pltpu.VMEM((2, 2, 16, 128), F32),
            pltpu.VMEM((2, CHUNKS * 128, OBS), BF16),
            pltpu.VMEM((2, MSG, 128), F32),
            pltpu.VMEM((2, MSG, 128), BF16),
            pltpu.VMEM((2, MSG, 128), BF16),
            pltpu.VMEM((2, 2, MSG, 128), BF16),
            pltpu.VMEM((2, MSG, 128), F32),
            pltpu.VMEM((2, MSG, 128), BF16),
            pltpu.VMEM((2, 2, MSG, 128), BF16),
            pltpu.VMEM((2, MSG, 128), BF16),
            pltpu.VMEM((2, K, CHUNKS * 128), BF16),
            pltpu.VMEM((2, 8, CHUNKS * 128), F32),
            pltpu.VMEM((2, CHUNKS, K, 128), BF16),
            pltpu.VMEM((2, NMEM, CHUNKS, 16, 128), BF16),
            pltpu.VMEM(background.shape, BF16),
            pltpu.SemaphoreType.REGULAR, pltpu.SemaphoreType.REGULAR,
            dma((2,)), dma((6,)),
            dma((2,)), dma((2,)),
            dma((2,)), dma((2,)),
            dma((2,)), dma((2,)),
            dma((2,)), dma((2, len(PARTS))),
            dma((2,)), dma((2,)),
            dma, dma,
            dma((2,)), dma((2, 8)),
            dma,
        ],
        compiler_params=pltpu.CompilerParams(
            collective_id=0, has_side_effects=True, vmem_limit_bytes=62 << 20
        ),
        name="analysis",
    )(background, *small)


def solution(mesh):
    in_specs = (
        P("mem", None, "reg"),
        P("reg", "mem", None),
        P("reg", "mem", None),
        P("reg", "mem", None),
        P("reg", "mem", None),
        P("reg", "mem"),
        P("reg", "mem", None),
    )
    out_specs = P("mem", None, "reg")
    return jax.shard_map(
        per_device, mesh=mesh, in_specs=in_specs, out_specs=out_specs, check_vma=False
    )
```

```python
import contextlib

import jax
import jax.numpy as jnp
from jax import lax
from jax.experimental import pallas as pl
from jax.experimental.pallas import tpu as pltpu
from jax.sharding import PartitionSpec as P

MESH = pl.DeviceIdType.MESH
F32 = jnp.float32
BF16 = jnp.bfloat16
NS_ITERS = 4
NMEM = 16
NREG = 32
K = 256
OBS = 384
CHUNKS = 8
PACK = 256
MSG = 272
PARTS = ((0, 128), (128, MSG))
CODE_ROW = 5
SENDS = tuple((away, core) for away in (4, 3, -3, 2, -2, 1, -1) for core in range(2)) + ((0, 0),)
EARLY = 6


def split2(x):
    high = x.astype(BF16)
    low = (x - high.astype(F32)).astype(BF16)
    return high, low


def dot(a, b):
    return jnp.dot(a, b, preferred_element_type=F32)


def dot_nt(a, b):
    return lax.dot_general(a, b, (((1,), (1,)), ((), ())), preferred_element_type=F32)


def dot3(a, b):
    return dot(a[0], b[0]) + (dot(a[0], b[1]) + dot(a[1], b[0]))


def rows_of(parts, rows):
    width = parts[0].shape[1]
    index = lax.broadcasted_iota(jnp.int32, (rows, width), 0)
    block = jnp.zeros((rows, width), F32)
    for i, part in enumerate(parts):
        block = jnp.where(index == i, part, block)
    return block


def tail_rows(tail):
    low_half, high_half = tail[0:1] + tail[2:3], tail[1:2] + tail[3:4]
    a, b = low_half.astype(BF16).astype(F32), high_half.astype(BF16).astype(F32)
    return rows_of([a, b, low_half - a, high_half - b, tail[4:5]], MSG - PACK).astype(BF16)


def square_indices(n):
    return lax.broadcasted_iota(jnp.int32, (n, n), 0), lax.broadcasted_iota(jnp.int32, (n, n), 1)


def newton_root(matrix):
    row, column = square_indices(matrix.shape[0])
    level = jnp.sum(jnp.where(row == column, matrix, 0.0), axis=0, keepdims=True)
    level = jnp.sum(level, axis=1, keepdims=True) * (1.0 / matrix.shape[0])

    def product(left, right):
        inner = dot(left[2], right[2])
        return left[0] * right[0], left[0] * right[1] + (right[0] * left[1] + inner)

    def rounded(value, rest):
        return value, rest, rest.astype(BF16)

    def middle_of(value, rest):
        return rounded(1.5 - 0.5 * value, -0.5 * rest)

    current = rounded(level, jnp.where(row == column, matrix - level, matrix))
    middle = middle_of(*current[:2])
    inverse = middle
    current = rounded(*product(current, inverse))
    for step in range(1, NS_ITERS):
        middle = middle_of(*product(inverse, current))
        if step < NS_ITERS - 1:
            current = rounded(*product(current, middle))
        inverse = rounded(*product(middle, inverse))
    return jnp.where(row == column, inverse[0] + inverse[1], inverse[1])


def stage(name):
    return contextlib.nullcontext()


def kernel(
    x_hbm, obs_hbm, coef_hbm, rinv_hbm, site_hbm, count_hbm, near_hbm, out_hbm,
    state, obs_in, coef_in, rinv_in, site_in, count_in, near_in,
    flat, packed, recv, obs_send, obs_recv, codes, code_recv, onehot, own, gmsg, ysend, yrecv, center, xsend, xrecv, turned,
    spread, mean, update, returned, ordered,
    region_in, adjacent_in, state_s, small_s, in_s, in_r, obs_s, obs_r, code_s, code_r, y_s, y_r, x_s, x_r, turn_s, turn_r, out_s, out_r, result_s,
):
    me = lax.axis_index("mem")
    reg = lax.axis_index("reg")
    chip = me // 2
    left, right = lax.rem(me + NMEM - 1, NMEM), lax.rem(me + 1, NMEM)
    below, above = lax.rem(reg + NREG - 1, NREG), lax.rem(reg + 1, NREG)
    ends = (me == 0, me == NMEM - 1)
    edge = jnp.logical_or(*ends)

    def block_of(phase, owner):
        return owner if phase == 0 else 2 * NMEM - 1 - owner

    core = lax.rem(me, 2)
    sibling = me + 1 - 2 * core
    barrier = pltpu.get_barrier_semaphore()

    def greet(target):
        pl.semaphore_signal(barrier, inc=1, device_id={"mem": target}, device_id_type=MESH)

    pl.when(core == 1)(lambda: greet(sibling))
    for i in (4, 3, 5, 2, 6, 1, 7):
        greet(2 * lax.rem(chip + i, 8))
    for side in (below, above):
        pl.semaphore_signal(
            barrier, inc=1, device_id={"mem": 2 * chip + 1, "reg": side}, device_id_type=MESH
        )

    def pass_barrier(hearer, count, passed):
        @pl.when(core == hearer)
        def _():
            pl.semaphore_wait(barrier, count)
            pl.semaphore_signal(passed, inc=1, device_id={"mem": sibling}, device_id_type=MESH)

        pl.when(core != hearer)(lambda: pl.semaphore_wait(passed, 1))

    def slab_of(step):
        away = 4 + lax.div(step + 1, 2) * (1 - 2 * lax.rem(step, 2))
        return lax.rem(chip + away, 8)

    def lanes(slab):
        return pl.ds(pl.multiple_of(slab * 128, 128), 128)

    def state_copy(phase):
        columns = pl.ds(phase * 1024, 1024)
        return pltpu.make_async_copy(
            x_hbm.at[:, :, columns], state.at[:, :, columns], state_s.at[phase]
        )

    small = [
        pltpu.make_async_copy(source, target, small_s.at[i])
        for i, (source, target) in enumerate(
            (
                (obs_hbm, obs_in), (coef_hbm, coef_in), (rinv_hbm, rinv_in), (site_hbm, site_in),
                (count_hbm, count_in), (near_hbm, near_in),
            )
        )
    ]

    state_copy(0).start()
    for copy in small:
        copy.start()
    state_copy(1).start()

    first = lax.broadcasted_iota(jnp.int32, (16, 128), 1) < 64
    mine = pl.ds(pl.multiple_of(me * 16, 16), 16)

    def reorder(slab):
        flat[...] = state[:, :, lanes(slab)].astype(F32).reshape(256, 128)
        for c in range(CHUNKS):
            even = flat[pl.ds(2 * c, 16, stride=16), :]
            odd = flat[pl.ds(2 * c + 1, 16, stride=16), :]
            packed[2 * slab, c] = jnp.where(first, even, pltpu.roll(odd, 64, 1)).astype(BF16)
            packed[2 * slab + 1, c] = jnp.where(first, pltpu.roll(even, 64, 1), odd).astype(BF16)

    def in_copy(phase, target):
        return pltpu.make_async_remote_copy(
            src_ref=packed.at[block_of(phase, target)],
            dst_ref=recv.at[phase, :, mine, :],
            send_sem=in_s.at[phase],
            recv_sem=in_r.at[phase],
            device_id={"mem": target},
            device_id_type=MESH,
        )

    def in_all(phase):
        others = recv.at[phase, :, pl.ds(0, K - 16), :]
        return pltpu.make_async_remote_copy(
            src_ref=others,
            dst_ref=others,
            send_sem=in_s.at[phase],
            recv_sem=in_r.at[phase],
            device_id={"mem": sibling},
            device_id_type=MESH,
        )

    def in_wait(phase):
        in_all(phase).wait_recv()

    half = me // 8

    def obs_target(j):
        block = 2 * me + j
        return jnp.where(half == 0, block, 2 * NMEM - 1 - block)

    def obs_copy(j):
        return pltpu.make_async_remote_copy(
            src_ref=obs_send.at[j],
            dst_ref=obs_recv.at[half],
            send_sem=obs_s.at[j],
            recv_sem=obs_r.at[half],
            device_id={"mem": obs_target(j)},
            device_id_type=MESH,
        )

    def obs_far(j):
        return obs_target(j) != me

    def first_in(step, carry):
        slab = slab_of(step)
        reorder(slab)
        for core in range(2):
            target = 2 * slab + core
            pl.when(target != me)(lambda target=target: in_copy(0, target).start())
        return carry

    with stage("barrier"):
        state_copy(0).wait()
        pass_barrier(0, NMEM - 1, region_in)
    with stage("obs_send"):
        for copy in small:
            copy.wait()
        row = lax.broadcasted_iota(jnp.int32, (8, OBS), 0)
        code = lax.broadcasted_iota(jnp.int32, (8, OBS), 1)
        away = jnp.abs(code // 3 - 1) + jnp.abs(lax.rem(code, 3) - 1)
        taper = jnp.where(away == 0, 1.0, jnp.where(away == 1, 0.5, 0.25))
        for j in range(2):
            block = jnp.where(code == 4, 1.0, 0.0)
            for i in range(5):
                block = block + jnp.where(code == near_in[0, j : j + 1, i : i + 1], taper, 0.0)
            count = jnp.broadcast_to(count_in[0:1, j : j + 1].astype(F32), (8, OBS))
            obs_send[j] = jnp.where(row == 4, count, block)
            for i, ref in enumerate((obs_in, coef_in, rinv_in)):
                obs_send[j, i : i + 1, :] = ref[0, j : j + 1, :]
            obs_send[j, 3:4, :] = site_in[0, j : j + 1, :].astype(F32)
        for j in range(2):
            pl.when(obs_far(j))(lambda j=j: obs_copy(j).start())

            @pl.when(jnp.logical_not(obs_far(j)))
            def _(j=j):
                obs_recv[half] = obs_send[j]

    def partner(away, core):
        if away == 0:
            return 2 * chip + 1 - lax.rem(me, 2)
        turned = away * (1 - 2 * lax.rem(me, 2))
        return 2 * lax.rem(chip + 8 + turned, 8) + core

    def second_in(i, wanted):
        target = partner(*i)
        at_edge = jnp.logical_or(target == 0, target == NMEM - 1)
        pl.when(at_edge if wanted else jnp.logical_not(at_edge))(lambda: in_copy(1, target).start())

    def reorder_step(slab, carry):
        reorder(slab)
        return carry

    with stage("first_in"):
        lax.fori_loop(0, 8, first_in, 0)
    with stage("second_in"):
        state_copy(1).wait()
        reorder(8)
        reorder(15)
        for i in SENDS:
            second_in(i, True)
        lax.fori_loop(9, 15, reorder_step, 0)
        recv[0, :, mine, :] = packed[me]
        recv[1, :, mine, :] = packed[block_of(1, me)]

    def code_copy(phase, side):
        if phase == 0:
            target = {"mem": right if side == 0 else left}
        else:
            target = {"reg": above if side == 0 else below}
        return pltpu.make_async_remote_copy(
            src_ref=codes.at[phase],
            dst_ref=code_recv.at[phase, side],
            send_sem=code_s.at[phase],
            recv_sem=code_r.at[phase],
            device_id=target,
            device_id_type=MESH,
        )

    def along_line(copy):
        for side in range(2):
            pl.when(jnp.logical_not(ends[1 - side]))(lambda side=side: copy(side).start())

    def sides_wait(ref, send_sem, recv_sem, sent):
        copy = pltpu.make_async_remote_copy(
            src_ref=ref,
            dst_ref=ref,
            send_sem=send_sem,
            recv_sem=recv_sem,
            device_id={"mem": sibling},
            device_id_type=MESH,
        )
        copy.wait_send() if sent else copy.wait_recv()

    def line_wait(ref_of, send_sem, recv_sem, sent):
        pl.when(ends[0])(lambda: sides_wait(ref_of(slice(1, 2)), send_sem, recv_sem, sent))
        pl.when(ends[1])(lambda: sides_wait(ref_of(slice(0, 1)), send_sem, recv_sem, sent))
        pl.when(jnp.logical_not(edge))(
            lambda: sides_wait(ref_of(slice(0, 2)), send_sem, recv_sem, sent)
        )

    def code_wait(phase, sent):
        if phase == 0:
            line_wait(lambda sides: code_recv.at[0, sides], code_s.at[0], code_r.at[0], sent)
        else:
            sides_wait(code_recv.at[1], code_s.at[1], code_r.at[1], sent)

    with stage("onehot"):
        for phase in range(2):
            source = block_of(phase, me) // 2

            @pl.when(source != me)
            def _(phase=phase, source=source):
                pltpu.make_async_remote_copy(
                    src_ref=obs_send.at[0],
                    dst_ref=obs_recv.at[phase],
                    send_sem=obs_s.at[0],
                    recv_sem=obs_r.at[phase],
                    device_id={"mem": source},
                    device_id_type=MESH,
                ).wait_recv()

            row, column = (lax.broadcasted_iota(jnp.int32, (16, 128), axis) for axis in range(2))
            weights = jnp.where(row - CODE_ROW == column, obs_recv[phase, 5:6, 0:128], 0.0)
            codes[phase] = jnp.broadcast_to(jnp.sum(weights, axis=1, keepdims=True), (16, 128))
            if phase == 0:
                along_line(lambda side: code_copy(0, side))
            site = obs_recv[phase, 3:4, :].astype(jnp.int32)
            for c in range(CHUNKS):
                place = lax.broadcasted_iota(jnp.int32, (128, OBS), 0) + c * 128
                onehot[phase, c * 128 : (c + 1) * 128, :] = jnp.where(place == site, 1.0, 0.0).astype(BF16)

    with stage("second_out"):
        for i in SENDS[:EARLY]:
            second_in(i, False)
    with stage("adjacent"):
        pass_barrier(1, 4, adjacent_in)
        for side in range(2):
            code_copy(1, side).start()

    def observe(phase):
        values = jnp.concatenate([recv[phase, c] for c in range(CHUNKS)], axis=1)
        predicted = dot(values, onehot[phase]) * obs_recv[phase, 1:2, :]
        mean_pred = jnp.sum(predicted, axis=0, keepdims=True) * (1.0 / K)
        slot = lax.broadcasted_iota(jnp.int32, (1, OBS), 1).astype(F32)
        root = jnp.where(slot < obs_recv[phase, 4:5, :], jnp.sqrt(obs_recv[phase, 2:3, :]), 0.0)
        scaled = (root * (predicted - mean_pred)).astype(BF16)
        misfit = root * (obs_recv[phase, 0:1, :] - mean_pred)
        gram = dot_nt(scaled, scaled)
        a = misfit.astype(BF16).astype(F32)
        b = (misfit - a).astype(BF16).astype(F32)
        parts = rows_of([a, b, misfit - a - b], 16).astype(BF16)
        drive = jnp.sum(dot_nt(parts, scaled), axis=0, keepdims=True)
        row, column = square_indices(128)
        upper, lower = gram[:128, :128], gram[128:, 128:]
        diagonal = jnp.sum(jnp.where(row == column, lower, 0.0), axis=0, keepdims=True)
        for i, block in enumerate((jnp.where(row <= column, upper, lower), gram[:128, 128:])):
            own[phase, i * 128 : (i + 1) * 128, :] = block
            gmsg[phase, i * 128 : (i + 1) * 128, :] = block.astype(BF16)
        zero = jnp.zeros((1, 128), F32)
        tail = rows_of([drive[:, :128], drive[:, 128:], zero, zero, diagonal], MSG - PACK)
        own[phase, PACK:MSG, :] = tail
        gmsg[phase, PACK:MSG, :] = tail_rows(tail)

    def y_copy(phase, side, part):
        rows = slice(*PARTS[part])
        return pltpu.make_async_remote_copy(
            src_ref=ysend.at[side, rows] if phase == 0 else gmsg.at[1, rows],
            dst_ref=yrecv.at[phase, side, rows],
            send_sem=y_s.at[phase],
            recv_sem=y_r.at[phase, part],
            device_id={"mem": right if side == 0 else left},
            device_id_type=MESH,
        )

    def y_wait(phase, rows, part, sent):
        line_wait(
            lambda sides: yrecv.at[phase, sides, rows], y_s.at[phase], y_r.at[phase, part], sent
        )

    def y_start():
        for part in range(len(PARTS)):
            along_line(lambda side, part=part: y_copy(1, side, part))

    def x_copy(phase, side, part):
        rows = slice(*PARTS[part])
        return pltpu.make_async_remote_copy(
            src_ref=gmsg.at[0, rows] if phase == 0 else xsend.at[side, rows],
            dst_ref=xrecv.at[phase, side, rows],
            send_sem=x_s.at[phase],
            recv_sem=x_r.at[phase, part],
            device_id={"reg": above if side == 0 else below},
            device_id_type=MESH,
        )

    def x_wait(phase, rows, part, sent):
        sides_wait(xrecv.at[phase, :, rows], x_s.at[phase], x_r.at[phase, part], sent)

    def turn_copy(side):
        return pltpu.make_async_remote_copy(
            src_ref=gmsg.at[1],
            dst_ref=turned.at[side],
            send_sem=turn_s,
            recv_sem=turn_r,
            device_id={"reg": above if side == 0 else below},
            device_id_type=MESH,
        )

    def center_state(phase):
        for c in range(CHUNKS):
            values = recv[phase, c].astype(F32)
            average = jnp.sum(values, axis=0, keepdims=True) * (1.0 / K)
            mean[phase, :, c * 128 : (c + 1) * 128] = jnp.broadcast_to(average, (8, 128))
            spread[phase, :, c * 128 : (c + 1) * 128] = (values - average).astype(BF16)

    def weighted(weights, seen, terms, rows):
        total = None
        for code, term in zip(seen, terms):
            term = weights[CODE_ROW + code : CODE_ROW + code + 1, :] * term[rows, :].astype(F32)
            total = term if total is None else total + term
        return total

    def part_sum(target, weights, seen, terms, part):
        rows = slice(part * 128, (part + 1) * 128)
        target[rows, :] = weighted(weights, seen, terms, rows).astype(BF16)
        if part == len(PARTS) - 1:
            target[PACK:MSG, :] = tail_rows(weighted(weights, seen, terms, slice(PACK, MSG)))

    def keep_turn(side):
        yrecv[1, side] = gmsg[0]

    def sum_column():
        code_wait(0, False)
        terms = (xrecv.at[0, 0], own.at[0], xrecv.at[0, 1])
        for part in range(len(PARTS)):
            x_wait(0, slice(*PARTS[part]), part, False)
            for side in range(2):
                seen = (0, 3, 6) if side == 0 else (2, 5, 8)

                @pl.when(jnp.logical_not(ends[1 - side]))
                def _(side=side, seen=seen):
                    part_sum(ysend.at[side], code_recv[0, 1 - side], seen, terms, part)
                    y_copy(0, side, part).start()

        center[0] = weighted(codes[0], (1, 4, 7), terms, slice(0, MSG))

    def sum_turn():
        sides_wait(turned, turn_s, turn_r, False)
        terms = (turned.at[0], own.at[1], turned.at[1])
        for side in range(2):

            @pl.when(ends[side])
            def _(side=side):
                for part in range(len(PARTS)):
                    seen = (0, 3, 6) if side == 0 else (2, 5, 8)
                    part_sum(yrecv.at[0, side], codes[0], seen, terms, part)

    def sum_row():
        code_wait(1, False)
        terms = (yrecv.at[1, 1], own.at[1], yrecv.at[1, 0])
        for part in range(len(PARTS)):
            y_wait(1, slice(*PARTS[part]), part, False)
            for side in range(2):
                seen = (0, 1, 2) if side == 0 else (6, 7, 8)
                part_sum(xsend.at[side], code_recv[1, 1 - side], seen, terms, part)
                x_copy(1, side, part).start()
        center[1] = weighted(codes[1], (3, 4, 5), terms, slice(0, MSG))

    def transform(phase):
        sides = yrecv if phase == 0 else xrecv
        total = center[phase] + sides[phase, 0].astype(F32) + sides[phase, 1].astype(F32)
        tail = total[PACK:MSG]
        drive = jnp.concatenate([tail[0:1] + tail[2:3], tail[1:2] + tail[3:4]], axis=1)
        row, column = square_indices(128)
        corner, cut = total[128:256], total[0:128]
        turned = cut.T
        first_block = jnp.where(row <= column, cut, turned) + jnp.where(row == column, K - 1.0, 0.0)
        last_block = jnp.where(row == column, tail[4:5] + (K - 1.0), jnp.where(row > column, cut, turned))
        system = jnp.concatenate(
            [
                jnp.concatenate([first_block, corner], axis=1),
                jnp.concatenate([corner.T, last_block], axis=1),
            ],
            axis=0,
        )
        scale = jnp.max(jnp.sum(jnp.abs(system), axis=0, keepdims=True), axis=1, keepdims=True)
        half_root = newton_root(system / scale) / jnp.sqrt(scale)
        halves = split2(half_root)
        vector = jnp.broadcast_to(drive, (16, K))
        vector = dot3(split2(vector), halves)
        vector = dot3(split2(vector), halves)[0:1]
        return (jnp.float32(K - 1.0) ** 0.5 * half_root + vector).astype(BF16)

    def apply(phase, weights):
        for c in range(0, CHUNKS, 2):
            columns = slice(c * 128, (c + 2) * 128)
            result = dot(weights, spread[phase, :, columns]) + mean[phase, 0:1, columns]
            update[phase, c] = result[:, :128].astype(BF16)
            update[phase, c + 1] = result[:, 128:].astype(BF16)

    def out_copy(phase, target):
        rows = pl.ds(pl.multiple_of(target * 16, 16), 16)
        return pltpu.make_async_remote_copy(
            src_ref=update.at[phase, :, rows, :],
            dst_ref=returned.at[phase, me],
            send_sem=out_s.at[phase],
            recv_sem=out_r.at[phase, chip],
            device_id={"mem": target},
            device_id_type=MESH,
        )

    def send_out(phase, offsets):
        for i in offsets:
            out_copy(phase, partner(*i)).start()

    def keep_own(phase):
        returned[phase, me] = update[phase, :, mine, :]

    def result_copy(slab):
        return pltpu.make_async_copy(
            ordered.at[:, :, lanes(slab)], out_hbm.at[:, :, lanes(slab)], result_s
        )

    def order_back(phase):
        def one(step, carry):
            source_chip = lax.rem(16 - slab_of(step) + 2 * chip, 8)
            def arrived(blocks):
                pltpu.make_async_remote_copy(
                    src_ref=returned.at[phase, blocks],
                    dst_ref=returned.at[phase, blocks],
                    send_sem=out_s.at[phase],
                    recv_sem=out_r.at[phase, source_chip],
                    device_id={"mem": sibling},
                    device_id_type=MESH,
                ).wait_recv()

            pl.when(source_chip != chip)(lambda: arrived(pl.ds(2 * source_chip, 2)))
            pl.when(source_chip == chip)(lambda: arrived(pl.ds(sibling, 1)))
            for c in range(CHUNKS):
                a = returned[phase, 2 * source_chip + phase, c].astype(F32)
                b = returned[phase, 2 * source_chip + 1 - phase, c].astype(F32)
                flat[pl.ds(2 * c, 16, stride=16), :] = jnp.where(first, a, pltpu.roll(b, 64, 1))
                flat[pl.ds(2 * c + 1, 16, stride=16), :] = jnp.where(first, pltpu.roll(a, 64, 1), b)
            slab = source_chip if phase == 0 else 15 - source_chip
            ordered[:, :, lanes(slab)] = flat[...].reshape(16, 16, 128).astype(BF16)
            result_copy(slab).start()
            return carry

        lax.fori_loop(0, 8, one, 0)

    with stage("in_wait0"):
        in_wait(0)
    with stage("observe0"):
        observe(0)
        for part in range(len(PARTS)):
            for side in range(2):
                x_copy(0, side, part).start()
        for i in SENDS[EARLY:]:
            second_in(i, False)
    with stage("edge"):

        @pl.when(edge)
        def _():
            in_wait(1)
            observe(1)
            for side in range(2):
                turn_copy(side).start()
                pl.when(ends[side])(lambda side=side: keep_turn(side))
            y_start()

    with stage("center0"):
        center_state(0)
    with stage("sum_column"):
        sum_column()
    with stage("in_wait1"):
        pl.when(jnp.logical_not(edge))(lambda: in_wait(1))
    with stage("observe1"):

        @pl.when(jnp.logical_not(edge))
        def _():
            observe(1)
            y_start()

    with stage("sum_turn"):
        pl.when(edge)(sum_turn)
    with stage("y_wait0"):
        for part in range(len(PARTS)):
            y_wait(0, slice(*PARTS[part]), part, False)
    with stage("transform0"):
        weights = transform(0)
    with stage("apply0"):
        apply(0, weights)
    send_out(0, SENDS)
    with stage("sum_row1"):
        sum_row()
    with stage("center1"):
        keep_own(0)
        center_state(1)
    with stage("x_wait1"):
        for part in range(len(PARTS)):
            x_wait(1, slice(*PARTS[part]), part, False)
    with stage("transform1"):
        weights = transform(1)
    with stage("apply1"):
        apply(1, weights)
    send_out(1, SENDS)
    keep_own(1)
    with stage("sent"):
        for phase in range(2):
            in_all(phase).wait_send()
            y_wait(phase, slice(0, MSG), 0, True)
            x_wait(phase, slice(0, MSG), 0, True)
            code_wait(phase, True)
        pl.when(edge)(lambda: sides_wait(turned, turn_s, turn_r, True))
        for j in range(2):
            pl.when(obs_far(j))(lambda j=j: obs_copy(j).wait_send())
    with stage("back0"):
        order_back(0)
    with stage("back1"):
        order_back(1)

    with stage("drain"):
        for phase in range(2):
            others = update.at[phase, :, pl.ds(0, K - 16), :]
            pltpu.make_async_remote_copy(
                src_ref=others,
                dst_ref=others,
                send_sem=out_s.at[phase],
                recv_sem=out_r.at[phase, chip],
                device_id={"mem": sibling},
                device_id_type=MESH,
            ).wait_send()
        pltpu.make_async_copy(ordered, out_hbm, result_s).wait()


def hand_over(in_ref, out_ref):
    out_ref[...] = in_ref[...]


def per_device(background, observations, obs_coef, obs_rinv, obs_site, obs_count, neighbours):
    dma = pltpu.SemaphoreType.DMA
    small = (observations, obs_coef, obs_rinv, obs_site, obs_count, neighbours)
    ordered = pl.pallas_call(
        kernel,
        out_shape=jax.ShapeDtypeStruct(background.shape, BF16),
        in_specs=[pl.BlockSpec(memory_space=pltpu.HBM)] * 7,
        out_specs=pl.BlockSpec(memory_space=pl.ANY),
        scratch_shapes=[
            pltpu.VMEM(background.shape, BF16),
            *(pltpu.VMEM(array.shape, array.dtype) for array in small),
            pltpu.VMEM((256, 128), F32),
            pltpu.VMEM((2 * NMEM, CHUNKS, 16, 128), BF16),
            pltpu.VMEM((2, CHUNKS, K, 128), BF16),
            pltpu.VMEM((2, 8, OBS), F32),
            pltpu.VMEM((2, 8, OBS), F32),
            pltpu.VMEM((2, 16, 128), F32),
            pltpu.VMEM((2, 2, 16, 128), F32),
            pltpu.VMEM((2, CHUNKS * 128, OBS), BF16),
            pltpu.VMEM((2, MSG, 128), F32),
            pltpu.VMEM((2, MSG, 128), BF16),
            pltpu.VMEM((2, MSG, 128), BF16),
            pltpu.VMEM((2, 2, MSG, 128), BF16),
            pltpu.VMEM((2, MSG, 128), F32),
            pltpu.VMEM((2, MSG, 128), BF16),
            pltpu.VMEM((2, 2, MSG, 128), BF16),
            pltpu.VMEM((2, MSG, 128), BF16),
            pltpu.VMEM((2, K, CHUNKS * 128), BF16),
            pltpu.VMEM((2, 8, CHUNKS * 128), F32),
            pltpu.VMEM((2, CHUNKS, K, 128), BF16),
            pltpu.VMEM((2, NMEM, CHUNKS, 16, 128), BF16),
            pltpu.VMEM(background.shape, BF16),
            pltpu.SemaphoreType.REGULAR, pltpu.SemaphoreType.REGULAR,
            dma((2,)), dma((6,)),
            dma((2,)), dma((2,)),
            dma((2,)), dma((2,)),
            dma((2,)), dma((2,)),
            dma((2,)), dma((2, len(PARTS))),
            dma((2,)), dma((2, len(PARTS))),
            dma, dma,
            dma((2,)), dma((2, 8)),
            dma,
        ],
        compiler_params=pltpu.CompilerParams(
            collective_id=0, has_side_effects=True, vmem_limit_bytes=62 << 20
        ),
        name="analysis",
    )(background, *small)
    half = pl.BlockSpec((8, 16, background.shape[2]), lambda i: (i, 0, 0))
    return pl.pallas_call(
        hand_over,
        grid=(2,),
        out_shape=jax.ShapeDtypeStruct(background.shape, BF16),
        in_specs=[half],
        out_specs=half,
        compiler_params=pltpu.CompilerParams(vmem_limit_bytes=60 << 20),
        name="hand_over",
    )(ordered)


def solution(mesh):
    in_specs = (
        P("mem", None, "reg"),
        P("reg", "mem", None),
        P("reg", "mem", None),
        P("reg", "mem", None),
        P("reg", "mem", None),
        P("reg", "mem"),
        P("reg", "mem", None),
    )
    out_specs = P("mem", None, "reg")
    return jax.shard_map(
        per_device, mesh=mesh, in_specs=in_specs, out_specs=out_specs, check_vma=False
    )
```

```python
import contextlib

import jax
import jax.numpy as jnp
from jax import lax
from jax.experimental import pallas as pl
from jax.experimental.pallas import tpu as pltpu
from jax.sharding import PartitionSpec as P

MESH = pl.DeviceIdType.MESH
F32 = jnp.float32
BF16 = jnp.bfloat16
NS_ITERS = 4
NMEM = 16
NREG = 32
K = 256
OBS = 384
CHUNKS = 8
PACK = 256
MSG = 272
PARTS = ((0, 128), (128, MSG))
CODE_ROW = 5
SENDS = tuple((away, core) for away in (4, 3, -3, 2, -2, 1, -1) for core in range(2)) + ((0, 0),)
EARLY = 6


def dot(a, b):
    return jnp.dot(a, b, preferred_element_type=F32)


def dot_nt(a, b):
    return lax.dot_general(a, b, (((1,), (1,)), ((), ())), preferred_element_type=F32)


def rows_of(parts, rows):
    width = parts[0].shape[1]
    index = lax.broadcasted_iota(jnp.int32, (rows, width), 0)
    block = jnp.zeros((rows, width), F32)
    for i, part in enumerate(parts):
        block = jnp.where(index == i, part, block)
    return block


def tail_rows(tail):
    low_half, high_half = tail[0:1] + tail[2:3], tail[1:2] + tail[3:4]
    a, b = low_half.astype(BF16).astype(F32), high_half.astype(BF16).astype(F32)
    return rows_of([a, b, low_half - a, high_half - b, tail[4:5]], MSG - PACK).astype(BF16)


def square_indices(n):
    return lax.broadcasted_iota(jnp.int32, (n, n), 0), lax.broadcasted_iota(jnp.int32, (n, n), 1)


def newton_root(matrix):
    row, column = square_indices(matrix.shape[0])
    level = jnp.sum(jnp.where(row == column, matrix, 0.0), axis=0, keepdims=True)
    level = jnp.sum(level, axis=1, keepdims=True) * (1.0 / matrix.shape[0])

    def product(left, right):
        inner = dot(left[2], right[2])
        return left[0] * right[0], left[0] * right[1] + (right[0] * left[1] + inner)

    def rounded(value, rest):
        return value, rest, rest.astype(BF16)

    def middle_of(value, rest):
        return rounded(1.5 - 0.5 * value, -0.5 * rest)

    current = rounded(level, jnp.where(row == column, matrix - level, matrix))
    middle = middle_of(*current[:2])
    inverse = middle
    current = rounded(*product(current, inverse))
    for step in range(1, NS_ITERS):
        middle = middle_of(*product(inverse, current))
        if step < NS_ITERS - 1:
            current = rounded(*product(current, middle))
        inverse = rounded(*product(middle, inverse))
    return inverse


def stage(name):
    return contextlib.nullcontext()


def kernel(
    x_hbm, obs_hbm, coef_hbm, rinv_hbm, site_hbm, count_hbm, near_hbm, out_hbm,
    state, obs_in, coef_in, rinv_in, site_in, count_in, near_in,
    flat, packed, recv, obs_send, obs_recv, codes, code_recv, onehot, own, gmsg, ysend, yrecv, center, xsend, xrecv, turned,
    spread, mean, update, returned, ordered,
    region_in, adjacent_in, state_s, small_s, in_s, in_r, obs_s, obs_r, code_s, code_r, y_s, y_r, x_s, x_r, turn_s, turn_r, out_s, out_r, result_s,
):
    me = lax.axis_index("mem")
    reg = lax.axis_index("reg")
    chip = me // 2
    left, right = lax.rem(me + NMEM - 1, NMEM), lax.rem(me + 1, NMEM)
    below, above = lax.rem(reg + NREG - 1, NREG), lax.rem(reg + 1, NREG)
    ends = (me == 0, me == NMEM - 1)
    edge = jnp.logical_or(*ends)

    def block_of(phase, owner):
        return owner if phase == 0 else 2 * NMEM - 1 - owner

    core = lax.rem(me, 2)
    sibling = me + 1 - 2 * core
    barrier = pltpu.get_barrier_semaphore()

    def greet(target):
        pl.semaphore_signal(barrier, inc=1, device_id={"mem": target}, device_id_type=MESH)

    pl.when(core == 1)(lambda: greet(sibling))
    for i in (4, 3, 5, 2, 6, 1, 7):
        greet(2 * lax.rem(chip + i, 8))
    for side in (below, above):
        pl.semaphore_signal(
            barrier, inc=1, device_id={"mem": 2 * chip + 1, "reg": side}, device_id_type=MESH
        )

    def pass_barrier(hearer, count, passed):
        @pl.when(core == hearer)
        def _():
            pl.semaphore_wait(barrier, count)
            pl.semaphore_signal(passed, inc=1, device_id={"mem": sibling}, device_id_type=MESH)

        pl.when(core != hearer)(lambda: pl.semaphore_wait(passed, 1))

    def slab_of(step):
        away = 4 + lax.div(step + 1, 2) * (1 - 2 * lax.rem(step, 2))
        return lax.rem(chip + away, 8)

    def lanes(slab):
        return pl.ds(pl.multiple_of(slab * 128, 128), 128)

    def state_copy(phase):
        columns = pl.ds(phase * 1024, 1024)
        return pltpu.make_async_copy(
            x_hbm.at[:, :, columns], state.at[:, :, columns], state_s.at[phase]
        )

    small = [
        pltpu.make_async_copy(source, target, small_s.at[i])
        for i, (source, target) in enumerate(
            (
                (obs_hbm, obs_in), (coef_hbm, coef_in), (rinv_hbm, rinv_in), (site_hbm, site_in),
                (count_hbm, count_in), (near_hbm, near_in),
            )
        )
    ]

    state_copy(0).start()
    for copy in small:
        copy.start()
    state_copy(1).start()

    first = lax.broadcasted_iota(jnp.int32, (16, 128), 1) < 64
    mine = pl.ds(pl.multiple_of(me * 16, 16), 16)

    def reorder(slab):
        flat[...] = state[:, :, lanes(slab)].astype(F32).reshape(256, 128)
        for c in range(CHUNKS):
            even = flat[pl.ds(2 * c, 16, stride=16), :]
            odd = flat[pl.ds(2 * c + 1, 16, stride=16), :]
            packed[2 * slab, c] = jnp.where(first, even, pltpu.roll(odd, 64, 1)).astype(BF16)
            packed[2 * slab + 1, c] = jnp.where(first, pltpu.roll(even, 64, 1), odd).astype(BF16)

    def in_copy(phase, target):
        return pltpu.make_async_remote_copy(
            src_ref=packed.at[block_of(phase, target)],
            dst_ref=recv.at[phase, :, mine, :],
            send_sem=in_s.at[phase],
            recv_sem=in_r.at[phase],
            device_id={"mem": target},
            device_id_type=MESH,
        )

    def in_all(phase):
        others = recv.at[phase, :, pl.ds(0, K - 16), :]
        return pltpu.make_async_remote_copy(
            src_ref=others,
            dst_ref=others,
            send_sem=in_s.at[phase],
            recv_sem=in_r.at[phase],
            device_id={"mem": sibling},
            device_id_type=MESH,
        )

    def in_wait(phase):
        in_all(phase).wait_recv()

    half = me // 8

    def obs_target(j):
        block = 2 * me + j
        return jnp.where(half == 0, block, 2 * NMEM - 1 - block)

    def obs_copy(j):
        return pltpu.make_async_remote_copy(
            src_ref=obs_send.at[j],
            dst_ref=obs_recv.at[half],
            send_sem=obs_s.at[j],
            recv_sem=obs_r.at[half],
            device_id={"mem": obs_target(j)},
            device_id_type=MESH,
        )

    def obs_far(j):
        return obs_target(j) != me

    def first_in(step, carry):
        slab = slab_of(step)
        reorder(slab)
        for core in range(2):
            target = 2 * slab + core
            pl.when(target != me)(lambda target=target: in_copy(0, target).start())
        return carry

    with stage("barrier"):
        state_copy(0).wait()
        pass_barrier(0, NMEM - 1, region_in)
    with stage("obs_send"):
        for copy in small:
            copy.wait()
        row = lax.broadcasted_iota(jnp.int32, (8, OBS), 0)
        code = lax.broadcasted_iota(jnp.int32, (8, OBS), 1)
        away = jnp.abs(code // 3 - 1) + jnp.abs(lax.rem(code, 3) - 1)
        taper = jnp.where(away == 0, 1.0, jnp.where(away == 1, 0.5, 0.25))
        for j in range(2):
            block = jnp.where(code == 4, 1.0, 0.0)
            for i in range(5):
                block = block + jnp.where(code == near_in[0, j : j + 1, i : i + 1], taper, 0.0)
            count = jnp.broadcast_to(count_in[0:1, j : j + 1].astype(F32), (8, OBS))
            obs_send[j] = jnp.where(row == 4, count, block)
            for i, ref in enumerate((obs_in, coef_in, rinv_in)):
                obs_send[j, i : i + 1, :] = ref[0, j : j + 1, :]
            obs_send[j, 3:4, :] = site_in[0, j : j + 1, :].astype(F32)
        for j in range(2):
            pl.when(obs_far(j))(lambda j=j: obs_copy(j).start())

            @pl.when(jnp.logical_not(obs_far(j)))
            def _(j=j):
                obs_recv[half] = obs_send[j]

    def partner(away, core):
        if away == 0:
            return 2 * chip + 1 - lax.rem(me, 2)
        turned = away * (1 - 2 * lax.rem(me, 2))
        return 2 * lax.rem(chip + 8 + turned, 8) + core

    def second_in(i, wanted):
        target = partner(*i)
        at_edge = jnp.logical_or(target == 0, target == NMEM - 1)
        pl.when(at_edge if wanted else jnp.logical_not(at_edge))(lambda: in_copy(1, target).start())

    def reorder_step(slab, carry):
        reorder(slab)
        return carry

    with stage("first_in"):
        lax.fori_loop(0, 8, first_in, 0)
    with stage("second_in"):
        state_copy(1).wait()
        reorder(8)
        reorder(15)
        for i in SENDS:
            second_in(i, True)
        lax.fori_loop(9, 15, reorder_step, 0)
        recv[0, :, mine, :] = packed[me]
        recv[1, :, mine, :] = packed[block_of(1, me)]

    def code_copy(phase, side):
        if phase == 0:
            target = {"mem": right if side == 0 else left}
        else:
            target = {"reg": above if side == 0 else below}
        return pltpu.make_async_remote_copy(
            src_ref=codes.at[phase],
            dst_ref=code_recv.at[phase, side],
            send_sem=code_s.at[phase],
            recv_sem=code_r.at[phase],
            device_id=target,
            device_id_type=MESH,
        )

    def along_line(copy):
        for side in range(2):
            pl.when(jnp.logical_not(ends[1 - side]))(lambda side=side: copy(side).start())

    def sides_wait(ref, send_sem, recv_sem, sent):
        copy = pltpu.make_async_remote_copy(
            src_ref=ref,
            dst_ref=ref,
            send_sem=send_sem,
            recv_sem=recv_sem,
            device_id={"mem": sibling},
            device_id_type=MESH,
        )
        copy.wait_send() if sent else copy.wait_recv()

    def line_wait(ref_of, send_sem, recv_sem, sent):
        pl.when(ends[0])(lambda: sides_wait(ref_of(slice(1, 2)), send_sem, recv_sem, sent))
        pl.when(ends[1])(lambda: sides_wait(ref_of(slice(0, 1)), send_sem, recv_sem, sent))
        pl.when(jnp.logical_not(edge))(
            lambda: sides_wait(ref_of(slice(0, 2)), send_sem, recv_sem, sent)
        )

    def code_wait(phase, sent):
        if phase == 0:
            line_wait(lambda sides: code_recv.at[0, sides], code_s.at[0], code_r.at[0], sent)
        else:
            sides_wait(code_recv.at[1], code_s.at[1], code_r.at[1], sent)

    with stage("onehot"):
        for phase in range(2):
            source = block_of(phase, me) // 2

            @pl.when(source != me)
            def _(phase=phase, source=source):
                pltpu.make_async_remote_copy(
                    src_ref=obs_send.at[0],
                    dst_ref=obs_recv.at[phase],
                    send_sem=obs_s.at[0],
                    recv_sem=obs_r.at[phase],
                    device_id={"mem": source},
                    device_id_type=MESH,
                ).wait_recv()

            row, column = (lax.broadcasted_iota(jnp.int32, (16, 128), axis) for axis in range(2))
            weights = jnp.where(row - CODE_ROW == column, obs_recv[phase, 5:6, 0:128], 0.0)
            codes[phase] = jnp.broadcast_to(jnp.sum(weights, axis=1, keepdims=True), (16, 128))
            if phase == 0:
                along_line(lambda side: code_copy(0, side))
            site = obs_recv[phase, 3:4, :].astype(jnp.int32)
            for c in range(CHUNKS):
                place = lax.broadcasted_iota(jnp.int32, (128, OBS), 0) + c * 128
                onehot[phase, c * 128 : (c + 1) * 128, :] = jnp.where(place == site, 1.0, 0.0).astype(BF16)

    with stage("second_out"):
        for i in SENDS[:EARLY]:
            second_in(i, False)
    with stage("adjacent"):
        pass_barrier(1, 4, adjacent_in)
        for side in range(2):
            code_copy(1, side).start()

    def observe(phase, part_done):
        values = jnp.concatenate([recv[phase, c] for c in range(CHUNKS)], axis=1)
        predicted = dot(values, onehot[phase]) * obs_recv[phase, 1:2, :]
        mean_pred = jnp.sum(predicted, axis=0, keepdims=True) * (1.0 / K)
        slot = lax.broadcasted_iota(jnp.int32, (1, OBS), 1).astype(F32)
        root = jnp.where(slot < obs_recv[phase, 4:5, :], jnp.sqrt(obs_recv[phase, 2:3, :]), 0.0)
        scaled = (root * (predicted - mean_pred)).astype(BF16)
        misfit = root * (obs_recv[phase, 0:1, :] - mean_pred)
        gram = dot_nt(scaled, scaled)
        row, column = square_indices(128)
        upper, lower = gram[:128, :128], gram[128:, 128:]
        cut = jnp.where(row <= column, upper, lower)
        own[phase, 0:128, :] = cut
        gmsg[phase, 0:128, :] = cut.astype(BF16)
        part_done(0)
        diagonal = jnp.sum(jnp.where(row == column, lower, 0.0), axis=0, keepdims=True)
        a = misfit.astype(BF16).astype(F32)
        b = (misfit - a).astype(BF16).astype(F32)
        parts = rows_of([a, b, misfit - a - b], 16).astype(BF16)
        drive = jnp.sum(dot_nt(parts, scaled), axis=0, keepdims=True)
        own[phase, 128:256, :] = gram[:128, 128:]
        gmsg[phase, 128:256, :] = gram[:128, 128:].astype(BF16)
        zero = jnp.zeros((1, 128), F32)
        tail = rows_of([drive[:, :128], drive[:, 128:], zero, zero, diagonal], MSG - PACK)
        own[phase, PACK:MSG, :] = tail
        gmsg[phase, PACK:MSG, :] = tail_rows(tail)
        part_done(1)

    def y_copy(phase, side, part):
        rows = slice(*PARTS[part])
        return pltpu.make_async_remote_copy(
            src_ref=ysend.at[side, rows] if phase == 0 else gmsg.at[1, rows],
            dst_ref=yrecv.at[phase, side, rows],
            send_sem=y_s.at[phase],
            recv_sem=y_r.at[phase, part],
            device_id={"mem": right if side == 0 else left},
            device_id_type=MESH,
        )

    def y_wait(phase, rows, part, sent):
        line_wait(
            lambda sides: yrecv.at[phase, sides, rows], y_s.at[phase], y_r.at[phase, part], sent
        )

    def y_start(part):
        along_line(lambda side: y_copy(1, side, part))

    def x_start(part):
        for side in range(2):
            x_copy(0, side, part).start()

    def x_copy(phase, side, part):
        rows = slice(*PARTS[part])
        return pltpu.make_async_remote_copy(
            src_ref=gmsg.at[0, rows] if phase == 0 else xsend.at[side, rows],
            dst_ref=xrecv.at[phase, side, rows],
            send_sem=x_s.at[phase],
            recv_sem=x_r.at[phase, part],
            device_id={"reg": above if side == 0 else below},
            device_id_type=MESH,
        )

    def x_wait(phase, rows, part, sent):
        sides_wait(xrecv.at[phase, :, rows], x_s.at[phase], x_r.at[phase, part], sent)

    def turn_copy(side):
        return pltpu.make_async_remote_copy(
            src_ref=gmsg.at[1],
            dst_ref=turned.at[side],
            send_sem=turn_s,
            recv_sem=turn_r,
            device_id={"reg": above if side == 0 else below},
            device_id_type=MESH,
        )

    def center_state(phase):
        for c in range(CHUNKS):
            values = recv[phase, c].astype(F32)
            average = jnp.sum(values, axis=0, keepdims=True) * (1.0 / K)
            mean[phase, :, c * 128 : (c + 1) * 128] = jnp.broadcast_to(average, (8, 128))
            spread[phase, :, c * 128 : (c + 1) * 128] = (values - average).astype(BF16)

    def weighted(weights, seen, terms, rows):
        total = None
        for code, term in zip(seen, terms):
            term = weights[CODE_ROW + code : CODE_ROW + code + 1, :] * term[rows, :].astype(F32)
            total = term if total is None else total + term
        return total

    def part_sum(target, weights, seen, terms, part):
        rows = slice(part * 128, (part + 1) * 128)
        target[rows, :] = weighted(weights, seen, terms, rows).astype(BF16)
        if part == len(PARTS) - 1:
            target[PACK:MSG, :] = tail_rows(weighted(weights, seen, terms, slice(PACK, MSG)))

    def keep_turn(side):
        yrecv[1, side] = gmsg[0]

    def sum_column():
        code_wait(0, False)
        terms = (xrecv.at[0, 0], own.at[0], xrecv.at[0, 1])
        for part in range(len(PARTS)):
            x_wait(0, slice(*PARTS[part]), part, False)
            for side in range(2):
                seen = (0, 3, 6) if side == 0 else (2, 5, 8)

                @pl.when(jnp.logical_not(ends[1 - side]))
                def _(side=side, seen=seen):
                    part_sum(ysend.at[side], code_recv[0, 1 - side], seen, terms, part)
                    y_copy(0, side, part).start()

        center[0] = weighted(codes[0], (1, 4, 7), terms, slice(0, MSG))

    def sum_turn():
        sides_wait(turned, turn_s, turn_r, False)
        terms = (turned.at[0], own.at[1], turned.at[1])
        for side in range(2):

            @pl.when(ends[side])
            def _(side=side):
                for part in range(len(PARTS)):
                    seen = (0, 3, 6) if side == 0 else (2, 5, 8)
                    part_sum(yrecv.at[0, side], codes[0], seen, terms, part)

    def sum_row():
        code_wait(1, False)
        terms = (yrecv.at[1, 1], own.at[1], yrecv.at[1, 0])
        for part in range(len(PARTS)):
            y_wait(1, slice(*PARTS[part]), part, False)
            for side in range(2):
                seen = (0, 1, 2) if side == 0 else (6, 7, 8)
                part_sum(xsend.at[side], code_recv[1, 1 - side], seen, terms, part)
                x_copy(1, side, part).start()
        center[1] = weighted(codes[1], (3, 4, 5), terms, slice(0, MSG))

    def transform(phase):
        sides = yrecv if phase == 0 else xrecv
        total = center[phase] + sides[phase, 0].astype(F32) + sides[phase, 1].astype(F32)
        tail = total[PACK:MSG]
        drive = jnp.concatenate([tail[0:1] + tail[2:3], tail[1:2] + tail[3:4]], axis=1)
        row, column = square_indices(128)
        corner, cut = total[128:256], total[0:128]
        turned = cut.T
        first_block = jnp.where(row <= column, cut, turned) + jnp.where(row == column, K - 1.0, 0.0)
        last_block = jnp.where(row == column, tail[4:5] + (K - 1.0), jnp.where(row > column, cut, turned))
        system = jnp.concatenate(
            [
                jnp.concatenate([first_block, corner], axis=1),
                jnp.concatenate([corner.T, last_block], axis=1),
            ],
            axis=0,
        )
        scale = jnp.max(jnp.sum(jnp.abs(system), axis=0, keepdims=True), axis=1, keepdims=True)
        level, rest, rounded_rest = newton_root(system * (1.0 / scale))
        row, column = square_indices(K)
        root = jnp.where(row == column, level + rest, rest)
        high_row = lax.broadcasted_iota(jnp.int32, (16, K), 0) == 0
        low_row = lax.broadcasted_iota(jnp.int32, (16, K), 0) == 1
        vector = drive * (1.0 / scale)
        for _ in range(2):
            high = vector.astype(BF16).astype(F32)
            parts = jnp.where(high_row, high, jnp.where(low_row, vector - high, 0.0)).astype(BF16)
            vector = level * vector + jnp.sum(dot(parts, rounded_rest), axis=0, keepdims=True)
        return (root * (jnp.float32(K - 1.0) ** 0.5 / jnp.sqrt(scale)) + vector).astype(BF16)

    def apply(phase, weights):
        for c in range(0, CHUNKS, 2):
            columns = slice(c * 128, (c + 2) * 128)
            result = dot(weights, spread[phase, :, columns]) + mean[phase, 0:1, columns]
            update[phase, c] = result[:, :128].astype(BF16)
            update[phase, c + 1] = result[:, 128:].astype(BF16)

    def out_copy(phase, target):
        rows = pl.ds(pl.multiple_of(target * 16, 16), 16)
        return pltpu.make_async_remote_copy(
            src_ref=update.at[phase, :, rows, :],
            dst_ref=returned.at[phase, me],
            send_sem=out_s.at[phase],
            recv_sem=out_r.at[phase, chip],
            device_id={"mem": target},
            device_id_type=MESH,
        )

    def send_out(phase, offsets):
        for i in offsets:
            out_copy(phase, partner(*i)).start()

    def keep_own(phase):
        returned[phase, me] = update[phase, :, mine, :]

    def result_copy(slab):
        return pltpu.make_async_copy(
            ordered.at[:, :, lanes(slab)], out_hbm.at[:, :, lanes(slab)], result_s
        )

    def order_back(phase):
        def one(step, carry):
            source_chip = lax.rem(16 - slab_of(step) + 2 * chip, 8)
            def arrived(blocks):
                pltpu.make_async_remote_copy(
                    src_ref=returned.at[phase, blocks],
                    dst_ref=returned.at[phase, blocks],
                    send_sem=out_s.at[phase],
                    recv_sem=out_r.at[phase, source_chip],
                    device_id={"mem": sibling},
                    device_id_type=MESH,
                ).wait_recv()

            pl.when(source_chip != chip)(lambda: arrived(pl.ds(2 * source_chip, 2)))
            pl.when(source_chip == chip)(lambda: arrived(pl.ds(sibling, 1)))
            for c in range(CHUNKS):
                a = returned[phase, 2 * source_chip + phase, c].astype(F32)
                b = returned[phase, 2 * source_chip + 1 - phase, c].astype(F32)
                flat[pl.ds(2 * c, 16, stride=16), :] = jnp.where(first, a, pltpu.roll(b, 64, 1))
                flat[pl.ds(2 * c + 1, 16, stride=16), :] = jnp.where(first, pltpu.roll(a, 64, 1), b)
            slab = source_chip if phase == 0 else 15 - source_chip
            ordered[:, :, lanes(slab)] = flat[...].reshape(16, 16, 128).astype(BF16)
            result_copy(slab).start()
            return carry

        lax.fori_loop(0, 8, one, 0)

    with stage("in_wait0"):
        in_wait(0)
    with stage("observe0"):
        observe(0, x_start)
        for i in SENDS[EARLY:]:
            second_in(i, False)
    with stage("edge"):

        @pl.when(edge)
        def _():
            in_wait(1)
            observe(1, y_start)
            for side in range(2):
                turn_copy(side).start()
                pl.when(ends[side])(lambda side=side: keep_turn(side))

    with stage("center0"):
        center_state(0)
    with stage("sum_column"):
        sum_column()
    with stage("in_wait1"):
        pl.when(jnp.logical_not(edge))(lambda: in_wait(1))
    with stage("observe1"):

        @pl.when(jnp.logical_not(edge))
        def _():
            observe(1, y_start)

    with stage("sum_turn"):
        pl.when(edge)(sum_turn)
    with stage("y_wait0"):
        for part in range(len(PARTS)):
            y_wait(0, slice(*PARTS[part]), part, False)
    with stage("transform0"):
        weights = transform(0)
    with stage("apply0"):
        apply(0, weights)
    send_out(0, SENDS)
    with stage("sum_row1"):
        sum_row()
    with stage("center1"):
        keep_own(0)
        center_state(1)
    with stage("x_wait1"):
        for part in range(len(PARTS)):
            x_wait(1, slice(*PARTS[part]), part, False)
    with stage("transform1"):
        weights = transform(1)
    with stage("apply1"):
        apply(1, weights)
    send_out(1, SENDS)
    keep_own(1)
    with stage("sent"):
        for phase in range(2):
            in_all(phase).wait_send()
            y_wait(phase, slice(0, MSG), 0, True)
            x_wait(phase, slice(0, MSG), 0, True)
            code_wait(phase, True)
        pl.when(edge)(lambda: sides_wait(turned, turn_s, turn_r, True))
        for j in range(2):
            pl.when(obs_far(j))(lambda j=j: obs_copy(j).wait_send())
    with stage("back0"):
        order_back(0)
    with stage("back1"):
        order_back(1)

    with stage("drain"):
        for phase in range(2):
            others = update.at[phase, :, pl.ds(0, K - 16), :]
            pltpu.make_async_remote_copy(
                src_ref=others,
                dst_ref=others,
                send_sem=out_s.at[phase],
                recv_sem=out_r.at[phase, chip],
                device_id={"mem": sibling},
                device_id_type=MESH,
            ).wait_send()
        pltpu.make_async_copy(ordered, out_hbm, result_s).wait()


def hand_over(in_ref, out_ref):
    out_ref[...] = in_ref[...]


def per_device(background, observations, obs_coef, obs_rinv, obs_site, obs_count, neighbours):
    dma = pltpu.SemaphoreType.DMA
    small = (observations, obs_coef, obs_rinv, obs_site, obs_count, neighbours)
    ordered = pl.pallas_call(
        kernel,
        out_shape=jax.ShapeDtypeStruct(background.shape, BF16),
        in_specs=[pl.BlockSpec(memory_space=pltpu.HBM)] * 7,
        out_specs=pl.BlockSpec(memory_space=pl.ANY),
        scratch_shapes=[
            pltpu.VMEM(background.shape, BF16),
            *(pltpu.VMEM(array.shape, array.dtype) for array in small),
            pltpu.VMEM((256, 128), F32),
            pltpu.VMEM((2 * NMEM, CHUNKS, 16, 128), BF16),
            pltpu.VMEM((2, CHUNKS, K, 128), BF16),
            pltpu.VMEM((2, 8, OBS), F32),
            pltpu.VMEM((2, 8, OBS), F32),
            pltpu.VMEM((2, 16, 128), F32),
            pltpu.VMEM((2, 2, 16, 128), F32),
            pltpu.VMEM((2, CHUNKS * 128, OBS), BF16),
            pltpu.VMEM((2, MSG, 128), F32),
            pltpu.VMEM((2, MSG, 128), BF16),
            pltpu.VMEM((2, MSG, 128), BF16),
            pltpu.VMEM((2, 2, MSG, 128), BF16),
            pltpu.VMEM((2, MSG, 128), F32),
            pltpu.VMEM((2, MSG, 128), BF16),
            pltpu.VMEM((2, 2, MSG, 128), BF16),
            pltpu.VMEM((2, MSG, 128), BF16),
            pltpu.VMEM((2, K, CHUNKS * 128), BF16),
            pltpu.VMEM((2, 8, CHUNKS * 128), F32),
            pltpu.VMEM((2, CHUNKS, K, 128), BF16),
            pltpu.VMEM((2, NMEM, CHUNKS, 16, 128), BF16),
            pltpu.VMEM(background.shape, BF16),
            pltpu.SemaphoreType.REGULAR, pltpu.SemaphoreType.REGULAR,
            dma((2,)), dma((6,)),
            dma((2,)), dma((2,)),
            dma((2,)), dma((2,)),
            dma((2,)), dma((2,)),
            dma((2,)), dma((2, len(PARTS))),
            dma((2,)), dma((2, len(PARTS))),
            dma, dma,
            dma((2,)), dma((2, 8)),
            dma,
        ],
        compiler_params=pltpu.CompilerParams(
            collective_id=0, has_side_effects=True, vmem_limit_bytes=62 << 20
        ),
        name="analysis",
    )(background, *small)
    half = pl.BlockSpec((8, 16, background.shape[2]), lambda i: (i, 0, 0))
    return pl.pallas_call(
        hand_over,
        grid=(2,),
        out_shape=jax.ShapeDtypeStruct(background.shape, BF16),
        in_specs=[half],
        out_specs=half,
        compiler_params=pltpu.CompilerParams(vmem_limit_bytes=60 << 20),
        name="hand_over",
    )(ordered)


def solution(mesh):
    in_specs = (
        P("mem", None, "reg"),
        P("reg", "mem", None),
        P("reg", "mem", None),
        P("reg", "mem", None),
        P("reg", "mem", None),
        P("reg", "mem"),
        P("reg", "mem", None),
    )
    out_specs = P("mem", None, "reg")
    return jax.shard_map(
        per_device, mesh=mesh, in_specs=in_specs, out_specs=out_specs, check_vma=False
    )
```

```python
import contextlib

import jax
import jax.numpy as jnp
from jax import lax
from jax.experimental import pallas as pl
from jax.experimental.pallas import tpu as pltpu
from jax.sharding import PartitionSpec as P

MESH = pl.DeviceIdType.MESH
F32 = jnp.float32
BF16 = jnp.bfloat16
NS_ITERS = 4
NMEM = 16
NREG = 32
K = 256
OBS = 384
CHUNKS = 8
PACK = 256
MSG = 272
PARTS = ((0, 128), (128, MSG))
CODE_ROW = 5
SENDS = tuple((away, core) for away in (4, 3, -3, 2, -2, 1, -1) for core in range(2)) + ((0, 0),)
EARLY = 6


def dot(a, b):
    return jnp.dot(a, b, preferred_element_type=F32)


def dot_nt(a, b):
    return lax.dot_general(a, b, (((1,), (1,)), ((), ())), preferred_element_type=F32)


def rows_of(parts, rows):
    width = parts[0].shape[1]
    index = lax.broadcasted_iota(jnp.int32, (rows, width), 0)
    block = jnp.zeros((rows, width), F32)
    for i, part in enumerate(parts):
        block = jnp.where(index == i, part, block)
    return block


def tail_rows(tail):
    low_half, high_half = tail[0:1] + tail[2:3], tail[1:2] + tail[3:4]
    a, b = low_half.astype(BF16).astype(F32), high_half.astype(BF16).astype(F32)
    return rows_of([a, b, low_half - a, high_half - b, tail[4:5]], MSG - PACK).astype(BF16)


def square_indices(n):
    return lax.broadcasted_iota(jnp.int32, (n, n), 0), lax.broadcasted_iota(jnp.int32, (n, n), 1)


def newton_root(matrix):
    row, column = square_indices(matrix.shape[0])
    level = jnp.sum(jnp.where(row == column, matrix, 0.0), axis=0, keepdims=True)
    level = jnp.sum(level, axis=1, keepdims=True) * (1.0 / matrix.shape[0])

    def product(left, right):
        inner = dot(left[2], right[2])
        return left[0] * right[0], left[0] * right[1] + (right[0] * left[1] + inner)

    def rounded(value, rest):
        return value, rest, rest.astype(BF16)

    def middle_of(value, rest):
        return rounded(1.5 - 0.5 * value, -0.5 * rest)

    current = rounded(level, jnp.where(row == column, matrix - level, matrix))
    middle = middle_of(*current[:2])
    inverse = middle
    current = rounded(*product(current, inverse))
    for step in range(1, NS_ITERS):
        middle = middle_of(*product(inverse, current))
        if step < NS_ITERS - 1:
            current = rounded(*product(current, middle))
        inverse = rounded(*product(middle, inverse))
    return inverse


def stage(name):
    return contextlib.nullcontext()


def kernel(
    x_hbm, obs_hbm, coef_hbm, rinv_hbm, site_hbm, count_hbm, near_hbm, out_hbm,
    state, obs_in, coef_in, rinv_in, site_in, count_in, near_in,
    flat, packed, recv, obs_send, obs_recv, codes, code_recv, onehot, own, gmsg, ysend, yrecv, center, xsend, xrecv, turned,
    spread, mean, update, returned, ordered,
    region_in, adjacent_in, state_s, small_s, in_s, in_r, obs_s, obs_r, code_s, code_r, y_s, y_r, x_s, x_r, turn_s, turn_r, out_s, out_r, result_s,
):
    me = lax.axis_index("mem")
    reg = lax.axis_index("reg")
    chip = me // 2
    left, right = lax.rem(me + NMEM - 1, NMEM), lax.rem(me + 1, NMEM)
    below, above = lax.rem(reg + NREG - 1, NREG), lax.rem(reg + 1, NREG)
    ends = (me == 0, me == NMEM - 1)
    edge = jnp.logical_or(*ends)

    def block_of(phase, owner):
        return owner if phase == 0 else 2 * NMEM - 1 - owner

    core = lax.rem(me, 2)
    sibling = me + 1 - 2 * core
    barrier = pltpu.get_barrier_semaphore()

    def greet(target):
        pl.semaphore_signal(barrier, inc=1, device_id={"mem": target}, device_id_type=MESH)

    pl.when(core == 1)(lambda: greet(sibling))
    for i in (4, 3, 5, 2, 6, 1, 7):
        greet(2 * lax.rem(chip + i, 8))
    for side in (below, above):
        pl.semaphore_signal(
            barrier, inc=1, device_id={"mem": 2 * chip + 1, "reg": side}, device_id_type=MESH
        )

    def pass_barrier(hearer, count, passed):
        @pl.when(core == hearer)
        def _():
            pl.semaphore_wait(barrier, count)
            pl.semaphore_signal(passed, inc=1, device_id={"mem": sibling}, device_id_type=MESH)

        pl.when(core != hearer)(lambda: pl.semaphore_wait(passed, 1))

    def slab_of(step):
        away = 4 + lax.div(step + 1, 2) * (1 - 2 * lax.rem(step, 2)) * (1 - 2 * lax.rem(me, 2))
        return lax.rem(chip + away, 8)

    def lanes(slab):
        return pl.ds(pl.multiple_of(slab * 128, 128), 128)

    def state_copy(phase):
        columns = pl.ds(phase * 1024, 1024)
        return pltpu.make_async_copy(
            x_hbm.at[:, :, columns], state.at[:, :, columns], state_s.at[phase]
        )

    small = [
        pltpu.make_async_copy(source, target, small_s.at[i])
        for i, (source, target) in enumerate(
            (
                (obs_hbm, obs_in), (coef_hbm, coef_in), (rinv_hbm, rinv_in), (site_hbm, site_in),
                (count_hbm, count_in), (near_hbm, near_in),
            )
        )
    ]

    state_copy(0).start()
    for copy in small:
        copy.start()
    state_copy(1).start()

    first = lax.broadcasted_iota(jnp.int32, (16, 128), 1) < 64
    mine = pl.ds(pl.multiple_of(me * 16, 16), 16)

    def reorder(slab):
        flat[...] = state[:, :, lanes(slab)].astype(F32).reshape(256, 128)
        for c in range(CHUNKS):
            even = flat[pl.ds(2 * c, 16, stride=16), :]
            odd = flat[pl.ds(2 * c + 1, 16, stride=16), :]
            packed[2 * slab, c] = jnp.where(first, even, pltpu.roll(odd, 64, 1)).astype(BF16)
            packed[2 * slab + 1, c] = jnp.where(first, pltpu.roll(even, 64, 1), odd).astype(BF16)

    def in_copy(phase, target):
        return pltpu.make_async_remote_copy(
            src_ref=packed.at[block_of(phase, target)],
            dst_ref=recv.at[phase, :, mine, :],
            send_sem=in_s.at[phase],
            recv_sem=in_r.at[phase],
            device_id={"mem": target},
            device_id_type=MESH,
        )

    def in_all(phase):
        others = recv.at[phase, :, pl.ds(0, K - 16), :]
        return pltpu.make_async_remote_copy(
            src_ref=others,
            dst_ref=others,
            send_sem=in_s.at[phase],
            recv_sem=in_r.at[phase],
            device_id={"mem": sibling},
            device_id_type=MESH,
        )

    def in_wait(phase):
        in_all(phase).wait_recv()

    half = me // 8

    def obs_target(j):
        block = 2 * me + j
        return jnp.where(half == 0, block, 2 * NMEM - 1 - block)

    def obs_copy(j):
        return pltpu.make_async_remote_copy(
            src_ref=obs_send.at[j],
            dst_ref=obs_recv.at[half],
            send_sem=obs_s.at[j],
            recv_sem=obs_r.at[half],
            device_id={"mem": obs_target(j)},
            device_id_type=MESH,
        )

    def obs_far(j):
        return obs_target(j) != me

    def first_in(step, carry):
        slab = slab_of(step)
        reorder(slab)
        for core in range(2):
            target = 2 * slab + core
            pl.when(target != me)(lambda target=target: in_copy(0, target).start())
        return carry

    with stage("barrier"):
        state_copy(0).wait()
        pass_barrier(0, NMEM - 1, region_in)
    with stage("obs_send"):
        for copy in small:
            copy.wait()
        row = lax.broadcasted_iota(jnp.int32, (8, OBS), 0)
        code = lax.broadcasted_iota(jnp.int32, (8, OBS), 1)
        away = jnp.abs(code // 3 - 1) + jnp.abs(lax.rem(code, 3) - 1)
        taper = jnp.where(away == 0, 1.0, jnp.where(away == 1, 0.5, 0.25))
        for j in range(2):
            block = jnp.where(code == 4, 1.0, 0.0)
            for i in range(5):
                block = block + jnp.where(code == near_in[0, j : j + 1, i : i + 1], taper, 0.0)
            count = jnp.broadcast_to(count_in[0:1, j : j + 1].astype(F32), (8, OBS))
            obs_send[j] = jnp.where(row == 4, count, block)
            for i, ref in enumerate((obs_in, coef_in, rinv_in)):
                obs_send[j, i : i + 1, :] = ref[0, j : j + 1, :]
            obs_send[j, 3:4, :] = site_in[0, j : j + 1, :].astype(F32)
        for j in range(2):
            pl.when(obs_far(j))(lambda j=j: obs_copy(j).start())

            @pl.when(jnp.logical_not(obs_far(j)))
            def _(j=j):
                obs_recv[half] = obs_send[j]

    def partner(away, core):
        if away == 0:
            return 2 * chip + 1 - lax.rem(me, 2)
        turned = away * (1 - 2 * lax.rem(me, 2))
        return 2 * lax.rem(chip + 8 + turned, 8) + core

    def second_in(i, wanted):
        target = partner(*i)
        at_edge = jnp.logical_or(target == 0, target == NMEM - 1)
        pl.when(at_edge if wanted else jnp.logical_not(at_edge))(lambda: in_copy(1, target).start())

    def reorder_step(slab, carry):
        reorder(slab)
        return carry

    with stage("first_in"):
        lax.fori_loop(0, 8, first_in, 0)
    with stage("second_in"):
        state_copy(1).wait()
        reorder(8)
        reorder(15)
        for i in SENDS:
            second_in(i, True)
        lax.fori_loop(9, 15, reorder_step, 0)
        recv[0, :, mine, :] = packed[me]
        recv[1, :, mine, :] = packed[block_of(1, me)]

    def code_copy(phase, side):
        if phase == 0:
            target = {"mem": right if side == 0 else left}
        else:
            target = {"reg": above if side == 0 else below}
        return pltpu.make_async_remote_copy(
            src_ref=codes.at[phase],
            dst_ref=code_recv.at[phase, side],
            send_sem=code_s.at[phase],
            recv_sem=code_r.at[phase],
            device_id=target,
            device_id_type=MESH,
        )

    def along_line(copy):
        for side in range(2):
            pl.when(jnp.logical_not(ends[1 - side]))(lambda side=side: copy(side).start())

    def sides_wait(ref, send_sem, recv_sem, sent):
        copy = pltpu.make_async_remote_copy(
            src_ref=ref,
            dst_ref=ref,
            send_sem=send_sem,
            recv_sem=recv_sem,
            device_id={"mem": sibling},
            device_id_type=MESH,
        )
        copy.wait_send() if sent else copy.wait_recv()

    def line_wait(ref_of, send_sem, recv_sem, sent):
        pl.when(ends[0])(lambda: sides_wait(ref_of(slice(1, 2)), send_sem, recv_sem, sent))
        pl.when(ends[1])(lambda: sides_wait(ref_of(slice(0, 1)), send_sem, recv_sem, sent))
        pl.when(jnp.logical_not(edge))(
            lambda: sides_wait(ref_of(slice(0, 2)), send_sem, recv_sem, sent)
        )

    def code_wait(phase, sent):
        if phase == 0:
            line_wait(lambda sides: code_recv.at[0, sides], code_s.at[0], code_r.at[0], sent)
        else:
            sides_wait(code_recv.at[1], code_s.at[1], code_r.at[1], sent)

    with stage("onehot"):
        for phase in range(2):
            source = block_of(phase, me) // 2

            @pl.when(source != me)
            def _(phase=phase, source=source):
                pltpu.make_async_remote_copy(
                    src_ref=obs_send.at[0],
                    dst_ref=obs_recv.at[phase],
                    send_sem=obs_s.at[0],
                    recv_sem=obs_r.at[phase],
                    device_id={"mem": source},
                    device_id_type=MESH,
                ).wait_recv()

            row, column = (lax.broadcasted_iota(jnp.int32, (16, 128), axis) for axis in range(2))
            weights = jnp.where(row - CODE_ROW == column, obs_recv[phase, 5:6, 0:128], 0.0)
            codes[phase] = jnp.broadcast_to(jnp.sum(weights, axis=1, keepdims=True), (16, 128))
            if phase == 0:
                along_line(lambda side: code_copy(0, side))
            site = obs_recv[phase, 3:4, :].astype(jnp.int32)
            for c in range(CHUNKS):
                place = lax.broadcasted_iota(jnp.int32, (128, OBS), 0) + c * 128
                onehot[phase, c * 128 : (c + 1) * 128, :] = jnp.where(place == site, 1.0, 0.0).astype(BF16)

    with stage("second_out"):
        for i in SENDS[:EARLY]:
            second_in(i, False)
    with stage("adjacent"):
        pass_barrier(1, 4, adjacent_in)
        for side in range(2):
            code_copy(1, side).start()

    def observe(phase, part_done):
        values = jnp.concatenate([recv[phase, c] for c in range(CHUNKS)], axis=1)
        predicted = dot(values, onehot[phase]) * obs_recv[phase, 1:2, :]
        mean_pred = jnp.sum(predicted, axis=0, keepdims=True) * (1.0 / K)
        slot = lax.broadcasted_iota(jnp.int32, (1, OBS), 1).astype(F32)
        root = jnp.where(slot < obs_recv[phase, 4:5, :], jnp.sqrt(obs_recv[phase, 2:3, :]), 0.0)
        scaled = (root * (predicted - mean_pred)).astype(BF16)
        misfit = root * (obs_recv[phase, 0:1, :] - mean_pred)
        gram = dot_nt(scaled, scaled)
        row, column = square_indices(128)
        upper, lower = gram[:128, :128], gram[128:, 128:]
        cut = jnp.where(row <= column, upper, lower)
        own[phase, 0:128, :] = cut
        gmsg[phase, 0:128, :] = cut.astype(BF16)
        part_done(0)
        diagonal = jnp.sum(jnp.where(row == column, lower, 0.0), axis=0, keepdims=True)
        a = misfit.astype(BF16).astype(F32)
        b = (misfit - a).astype(BF16).astype(F32)
        parts = rows_of([a, b, misfit - a - b], 16).astype(BF16)
        drive = jnp.sum(dot_nt(parts, scaled), axis=0, keepdims=True)
        own[phase, 128:256, :] = gram[:128, 128:]
        gmsg[phase, 128:256, :] = gram[:128, 128:].astype(BF16)
        zero = jnp.zeros((1, 128), F32)
        tail = rows_of([drive[:, :128], drive[:, 128:], zero, zero, diagonal], MSG - PACK)
        own[phase, PACK:MSG, :] = tail
        gmsg[phase, PACK:MSG, :] = tail_rows(tail)
        part_done(1)

    def y_copy(phase, side, part):
        rows = slice(*PARTS[part])
        return pltpu.make_async_remote_copy(
            src_ref=ysend.at[side, rows] if phase == 0 else gmsg.at[1, rows],
            dst_ref=yrecv.at[phase, side, rows],
            send_sem=y_s.at[phase],
            recv_sem=y_r.at[phase, part],
            device_id={"mem": right if side == 0 else left},
            device_id_type=MESH,
        )

    def y_wait(phase, rows, part, sent):
        line_wait(
            lambda sides: yrecv.at[phase, sides, rows], y_s.at[phase], y_r.at[phase, part], sent
        )

    def y_start(part):
        along_line(lambda side: y_copy(1, side, part))

    def x_start(part):
        for side in range(2):
            x_copy(0, side, part).start()

    def x_copy(phase, side, part):
        rows = slice(*PARTS[part])
        return pltpu.make_async_remote_copy(
            src_ref=gmsg.at[0, rows] if phase == 0 else xsend.at[side, rows],
            dst_ref=xrecv.at[phase, side, rows],
            send_sem=x_s.at[phase],
            recv_sem=x_r.at[phase, part],
            device_id={"reg": above if side == 0 else below},
            device_id_type=MESH,
        )

    def x_wait(phase, rows, part, sent):
        sides_wait(xrecv.at[phase, :, rows], x_s.at[phase], x_r.at[phase, part], sent)

    def turn_copy(side):
        return pltpu.make_async_remote_copy(
            src_ref=gmsg.at[1],
            dst_ref=turned.at[side],
            send_sem=turn_s,
            recv_sem=turn_r,
            device_id={"reg": above if side == 0 else below},
            device_id_type=MESH,
        )

    def center_state(phase):
        for c in range(CHUNKS):
            values = recv[phase, c].astype(F32)
            average = jnp.sum(values, axis=0, keepdims=True) * (1.0 / K)
            mean[phase, :, c * 128 : (c + 1) * 128] = jnp.broadcast_to(average, (8, 128))
            spread[phase, :, c * 128 : (c + 1) * 128] = (values - average).astype(BF16)

    def weighted(weights, seen, terms, rows):
        total = None
        for code, term in zip(seen, terms):
            term = weights[CODE_ROW + code : CODE_ROW + code + 1, :] * term[rows, :].astype(F32)
            total = term if total is None else total + term
        return total

    def part_sum(target, weights, seen, terms, part):
        rows = slice(part * 128, (part + 1) * 128)
        target[rows, :] = weighted(weights, seen, terms, rows).astype(BF16)
        if part == len(PARTS) - 1:
            target[PACK:MSG, :] = tail_rows(weighted(weights, seen, terms, slice(PACK, MSG)))

    def keep_turn(side):
        yrecv[1, side] = gmsg[0]

    def sum_column():
        code_wait(0, False)
        terms = (xrecv.at[0, 0], own.at[0], xrecv.at[0, 1])
        for part in range(len(PARTS)):
            x_wait(0, slice(*PARTS[part]), part, False)
            for side in range(2):
                seen = (0, 3, 6) if side == 0 else (2, 5, 8)

                @pl.when(jnp.logical_not(ends[1 - side]))
                def _(side=side, seen=seen):
                    part_sum(ysend.at[side], code_recv[0, 1 - side], seen, terms, part)
                    y_copy(0, side, part).start()

        center[0] = weighted(codes[0], (1, 4, 7), terms, slice(0, MSG))

    def sum_turn():
        sides_wait(turned, turn_s, turn_r, False)
        terms = (turned.at[0], own.at[1], turned.at[1])
        for side in range(2):

            @pl.when(ends[side])
            def _(side=side):
                for part in range(len(PARTS)):
                    seen = (0, 3, 6) if side == 0 else (2, 5, 8)
                    part_sum(yrecv.at[0, side], codes[0], seen, terms, part)

    def sum_row():
        code_wait(1, False)
        terms = (yrecv.at[1, 1], own.at[1], yrecv.at[1, 0])
        for part in range(len(PARTS)):
            y_wait(1, slice(*PARTS[part]), part, False)
            for side in range(2):
                seen = (0, 1, 2) if side == 0 else (6, 7, 8)
                part_sum(xsend.at[side], code_recv[1, 1 - side], seen, terms, part)
                x_copy(1, side, part).start()
        center[1] = weighted(codes[1], (3, 4, 5), terms, slice(0, MSG))

    def transform(phase):
        sides = yrecv if phase == 0 else xrecv
        total = center[phase] + sides[phase, 0].astype(F32) + sides[phase, 1].astype(F32)
        tail = total[PACK:MSG]
        drive = jnp.concatenate([tail[0:1] + tail[2:3], tail[1:2] + tail[3:4]], axis=1)
        row, column = square_indices(128)
        corner, cut = total[128:256], total[0:128]
        turned = cut.T
        first_block = jnp.where(row <= column, cut, turned) + jnp.where(row == column, K - 1.0, 0.0)
        last_block = jnp.where(row == column, tail[4:5] + (K - 1.0), jnp.where(row > column, cut, turned))
        system = jnp.concatenate(
            [
                jnp.concatenate([first_block, corner], axis=1),
                jnp.concatenate([corner.T, last_block], axis=1),
            ],
            axis=0,
        )
        scale = jnp.max(jnp.sum(jnp.abs(system), axis=0, keepdims=True), axis=1, keepdims=True)
        level, rest, rounded_rest = newton_root(system * (1.0 / scale))
        row, column = square_indices(K)
        root = jnp.where(row == column, level + rest, rest)
        high_row = lax.broadcasted_iota(jnp.int32, (16, K), 0) == 0
        low_row = lax.broadcasted_iota(jnp.int32, (16, K), 0) == 1
        vector = drive * (1.0 / scale)
        for _ in range(2):
            high = vector.astype(BF16).astype(F32)
            parts = jnp.where(high_row, high, jnp.where(low_row, vector - high, 0.0)).astype(BF16)
            vector = level * vector + jnp.sum(dot(parts, rounded_rest), axis=0, keepdims=True)
        return (root * (jnp.float32(K - 1.0) ** 0.5 / jnp.sqrt(scale)) + vector).astype(BF16)

    def apply(phase, weights):
        for c in range(0, CHUNKS, 2):
            columns = slice(c * 128, (c + 2) * 128)
            result = dot(weights, spread[phase, :, columns]) + mean[phase, 0:1, columns]
            update[phase, c] = result[:, :128].astype(BF16)
            update[phase, c + 1] = result[:, 128:].astype(BF16)

    def out_copy(phase, target):
        rows = pl.ds(pl.multiple_of(target * 16, 16), 16)
        return pltpu.make_async_remote_copy(
            src_ref=update.at[phase, :, rows, :],
            dst_ref=returned.at[phase, me],
            send_sem=out_s.at[phase],
            recv_sem=out_r.at[8 if phase == 0 else chip],
            device_id={"mem": target},
            device_id_type=MESH,
        )

    def send_out(phase, offsets):
        for i in offsets:
            out_copy(phase, partner(*i)).start()

    def keep_own(phase):
        returned[phase, me] = update[phase, :, mine, :]

    def result_copy(slab):
        return pltpu.make_async_copy(
            ordered.at[:, :, lanes(slab)], out_hbm.at[:, :, lanes(slab)], result_s
        )

    def order_back(phase):
        def arrived(blocks, index):
            blocks = returned.at[phase, blocks]
            sides_wait(blocks, out_s.at[phase], out_r.at[index], False)

        if phase == 0:
            arrived(slice(0, NMEM - 1), 8)

        def one(step, carry):
            source_chip = lax.rem(16 - slab_of(step) + 2 * chip, 8)
            if phase == 1:
                pl.when(source_chip != chip)(lambda: arrived(pl.ds(2 * source_chip, 2), source_chip))
                pl.when(source_chip == chip)(lambda: arrived(pl.ds(sibling, 1), source_chip))
            for c in range(CHUNKS):
                a = returned[phase, 2 * source_chip + phase, c].astype(F32)
                b = returned[phase, 2 * source_chip + 1 - phase, c].astype(F32)
                flat[pl.ds(2 * c, 16, stride=16), :] = jnp.where(first, a, pltpu.roll(b, 64, 1))
                flat[pl.ds(2 * c + 1, 16, stride=16), :] = jnp.where(first, pltpu.roll(a, 64, 1), b)
            slab = source_chip if phase == 0 else 15 - source_chip
            ordered[:, :, lanes(slab)] = flat[...].reshape(16, 16, 128).astype(BF16)
            result_copy(slab).start()
            return carry

        lax.fori_loop(0, 8, one, 0)

    with stage("in_wait0"):
        in_wait(0)
    with stage("observe0"):
        observe(0, x_start)
        for i in SENDS[EARLY:]:
            second_in(i, False)
    with stage("edge"):

        @pl.when(edge)
        def _():
            in_wait(1)
            observe(1, y_start)
            for side in range(2):
                turn_copy(side).start()
                pl.when(ends[side])(lambda side=side: keep_turn(side))

    with stage("center0"):
        center_state(0)
    with stage("sum_column"):
        sum_column()
    with stage("in_wait1"):
        pl.when(jnp.logical_not(edge))(lambda: in_wait(1))
    with stage("observe1"):

        @pl.when(jnp.logical_not(edge))
        def _():
            observe(1, y_start)

    with stage("sum_turn"):
        pl.when(edge)(sum_turn)
    with stage("y_wait0"):
        for part in range(len(PARTS)):
            y_wait(0, slice(*PARTS[part]), part, False)
    with stage("transform0"):
        weights = transform(0)
    with stage("apply0"):
        apply(0, weights)
    send_out(0, SENDS)
    with stage("sum_row1"):
        sum_row()
    with stage("center1"):
        keep_own(0)
        center_state(1)
    with stage("x_wait1"):
        for part in range(len(PARTS)):
            x_wait(1, slice(*PARTS[part]), part, False)
    with stage("transform1"):
        weights = transform(1)
    with stage("apply1"):
        apply(1, weights)
    send_out(1, SENDS)
    keep_own(1)
    with stage("sent"):
        for phase in range(2):
            in_all(phase).wait_send()
            y_wait(phase, slice(0, MSG), 0, True)
            x_wait(phase, slice(0, MSG), 0, True)
            code_wait(phase, True)
        pl.when(edge)(lambda: sides_wait(turned, turn_s, turn_r, True))
        for j in range(2):
            pl.when(obs_far(j))(lambda j=j: obs_copy(j).wait_send())
    with stage("back0"):
        order_back(0)
    with stage("back1"):
        order_back(1)

    with stage("drain"):
        for phase in range(2):
            others = update.at[phase, :, pl.ds(0, K - 16), :]
            pltpu.make_async_remote_copy(
                src_ref=others,
                dst_ref=others,
                send_sem=out_s.at[phase],
                recv_sem=out_r.at[chip],
                device_id={"mem": sibling},
                device_id_type=MESH,
            ).wait_send()
        pltpu.make_async_copy(ordered, out_hbm, result_s).wait()


def hand_over(in_ref, out_ref):
    out_ref[...] = in_ref[...]


def per_device(background, observations, obs_coef, obs_rinv, obs_site, obs_count, neighbours):
    dma = pltpu.SemaphoreType.DMA
    small = (observations, obs_coef, obs_rinv, obs_site, obs_count, neighbours)
    ordered = pl.pallas_call(
        kernel,
        out_shape=jax.ShapeDtypeStruct(background.shape, BF16),
        in_specs=[pl.BlockSpec(memory_space=pltpu.HBM)] * 7,
        out_specs=pl.BlockSpec(memory_space=pl.ANY),
        scratch_shapes=[
            pltpu.VMEM(background.shape, BF16),
            *(pltpu.VMEM(array.shape, array.dtype) for array in small),
            pltpu.VMEM((256, 128), F32),
            pltpu.VMEM((2 * NMEM, CHUNKS, 16, 128), BF16),
            pltpu.VMEM((2, CHUNKS, K, 128), BF16),
            pltpu.VMEM((2, 8, OBS), F32),
            pltpu.VMEM((2, 8, OBS), F32),
            pltpu.VMEM((2, 16, 128), F32),
            pltpu.VMEM((2, 2, 16, 128), F32),
            pltpu.VMEM((2, CHUNKS * 128, OBS), BF16),
            pltpu.VMEM((2, MSG, 128), F32),
            pltpu.VMEM((2, MSG, 128), BF16),
            pltpu.VMEM((2, MSG, 128), BF16),
            pltpu.VMEM((2, 2, MSG, 128), BF16),
            pltpu.VMEM((2, MSG, 128), F32),
            pltpu.VMEM((2, MSG, 128), BF16),
            pltpu.VMEM((2, 2, MSG, 128), BF16),
            pltpu.VMEM((2, MSG, 128), BF16),
            pltpu.VMEM((2, K, CHUNKS * 128), BF16),
            pltpu.VMEM((2, 8, CHUNKS * 128), F32),
            pltpu.VMEM((2, CHUNKS, K, 128), BF16),
            pltpu.VMEM((2, NMEM, CHUNKS, 16, 128), BF16),
            pltpu.VMEM(background.shape, BF16),
            pltpu.SemaphoreType.REGULAR, pltpu.SemaphoreType.REGULAR,
            dma((2,)), dma((6,)),
            dma((2,)), dma((2,)),
            dma((2,)), dma((2,)),
            dma((2,)), dma((2,)),
            dma((2,)), dma((2, len(PARTS))),
            dma((2,)), dma((2, len(PARTS))),
            dma, dma,
            dma((2,)), dma((9,)),
            dma,
        ],
        compiler_params=pltpu.CompilerParams(
            collective_id=0, has_side_effects=True, vmem_limit_bytes=62 << 20
        ),
        name="analysis",
    )(background, *small)
    half = pl.BlockSpec((8, 16, background.shape[2]), lambda i: (i, 0, 0))
    return pl.pallas_call(
        hand_over,
        grid=(2,),
        out_shape=jax.ShapeDtypeStruct(background.shape, BF16),
        in_specs=[half],
        out_specs=half,
        compiler_params=pltpu.CompilerParams(vmem_limit_bytes=60 << 20),
        name="hand_over",
    )(ordered)


def solution(mesh):
    in_specs = (
        P("mem", None, "reg"),
        P("reg", "mem", None),
        P("reg", "mem", None),
        P("reg", "mem", None),
        P("reg", "mem", None),
        P("reg", "mem"),
        P("reg", "mem", None),
    )
    out_specs = P("mem", None, "reg")
    return jax.shard_map(
        per_device, mesh=mesh, in_specs=in_specs, out_specs=out_specs, check_vma=False
    )
```

```python
import contextlib

import jax
import jax.numpy as jnp
from jax import lax
from jax.experimental import pallas as pl
from jax.experimental.pallas import tpu as pltpu
from jax.sharding import PartitionSpec as P

MESH = pl.DeviceIdType.MESH
F32 = jnp.float32
BF16 = jnp.bfloat16
NS_ITERS = 4
NMEM = 16
NREG = 32
K = 256
OBS = 384
CHUNKS = 8
PACK = 256
MSG = 272
PARTS = ((0, 128), (128, MSG))
CODE_ROW = 5
SENDS = tuple((away, core) for away in (4, 3, -3, 2, -2, 1, -1) for core in range(2)) + ((0, 0),)
EARLY = 10


def dot(a, b):
    return jnp.dot(a, b, preferred_element_type=F32)


def dot_nt(a, b):
    return lax.dot_general(a, b, (((1,), (1,)), ((), ())), preferred_element_type=F32)


def rows_of(parts, rows):
    width = parts[0].shape[1]
    index = lax.broadcasted_iota(jnp.int32, (rows, width), 0)
    block = jnp.zeros((rows, width), F32)
    for i, part in enumerate(parts):
        block = jnp.where(index == i, part, block)
    return block


def tail_rows(tail):
    low_half, high_half = tail[0:1] + tail[2:3], tail[1:2] + tail[3:4]
    a, b = low_half.astype(BF16).astype(F32), high_half.astype(BF16).astype(F32)
    return rows_of([a, b, low_half - a, high_half - b, tail[4:5]], MSG - PACK).astype(BF16)


def square_indices(n):
    return lax.broadcasted_iota(jnp.int32, (n, n), 0), lax.broadcasted_iota(jnp.int32, (n, n), 1)


def newton_root(matrix):
    row, column = square_indices(matrix.shape[0])
    level = jnp.sum(jnp.where(row == column, matrix, 0.0), axis=0, keepdims=True)
    level = jnp.sum(level, axis=1, keepdims=True) * (1.0 / matrix.shape[0])

    def product(left, right):
        inner = dot(left[2], right[2])
        return left[0] * right[0], left[0] * right[1] + (right[0] * left[1] + inner)

    def rounded(value, rest):
        return value, rest, rest.astype(BF16)

    def middle_of(value, rest):
        return rounded(1.5 - 0.5 * value, -0.5 * rest)

    current = rounded(level, jnp.where(row == column, matrix - level, matrix))
    middle = middle_of(*current[:2])
    inverse = middle
    current = rounded(*product(current, inverse))
    for step in range(1, NS_ITERS):
        middle = middle_of(*product(inverse, current))
        if step < NS_ITERS - 1:
            current = rounded(*product(current, middle))
        inverse = rounded(*product(middle, inverse))
    return inverse


def stage(name):
    return contextlib.nullcontext()


def kernel(
    x_hbm, obs_hbm, coef_hbm, rinv_hbm, site_hbm, count_hbm, near_hbm, out_hbm,
    state, obs_in, coef_in, rinv_in, site_in, count_in, near_in,
    flat, packed, recv, obs_send, obs_recv, codes, code_recv, onehot, own, gmsg, ysend, yrecv, center, xsend, xrecv, turned,
    spread, mean, update, returned, ordered,
    region_in, adjacent_in, state_s, small_s, in_s, in_r, obs_s, obs_r, code_s, code_r, y_s, y_r, x_s, x_r, turn_s, turn_r, out_s, out_r, result_s,
):
    me = lax.axis_index("mem")
    reg = lax.axis_index("reg")
    chip = me // 2
    left, right = lax.rem(me + NMEM - 1, NMEM), lax.rem(me + 1, NMEM)
    below, above = lax.rem(reg + NREG - 1, NREG), lax.rem(reg + 1, NREG)
    ends = (me == 0, me == NMEM - 1)
    edge = jnp.logical_or(*ends)

    def block_of(phase, owner):
        return owner if phase == 0 else 2 * NMEM - 1 - owner

    core = lax.rem(me, 2)
    sibling = me + 1 - 2 * core
    barrier = pltpu.get_barrier_semaphore()

    def greet(target):
        pl.semaphore_signal(barrier, inc=1, device_id={"mem": target}, device_id_type=MESH)

    pl.when(core == 1)(lambda: greet(sibling))
    for i in (4, 3, 5, 2, 6, 1, 7):
        greet(2 * lax.rem(chip + i, 8))
    for side in (below, above):
        pl.semaphore_signal(
            barrier, inc=1, device_id={"mem": 2 * chip + 1, "reg": side}, device_id_type=MESH
        )

    def pass_barrier(hearer, count, passed):
        @pl.when(core == hearer)
        def _():
            pl.semaphore_wait(barrier, count)
            pl.semaphore_signal(passed, inc=1, device_id={"mem": sibling}, device_id_type=MESH)

        pl.when(core != hearer)(lambda: pl.semaphore_wait(passed, 1))

    def slab_of(step):
        away = 4 + lax.div(step + 1, 2) * (1 - 2 * lax.rem(step, 2)) * (1 - 2 * lax.rem(me, 2))
        return lax.rem(chip + away, 8)

    def lanes(slab):
        return pl.ds(pl.multiple_of(slab * 128, 128), 128)

    def state_copy(phase):
        columns = pl.ds(phase * 1024, 1024)
        return pltpu.make_async_copy(
            x_hbm.at[:, :, columns], state.at[:, :, columns], state_s.at[phase]
        )

    small = [
        pltpu.make_async_copy(source, target, small_s.at[i])
        for i, (source, target) in enumerate(
            (
                (obs_hbm, obs_in), (coef_hbm, coef_in), (rinv_hbm, rinv_in), (site_hbm, site_in),
                (count_hbm, count_in), (near_hbm, near_in),
            )
        )
    ]

    state_copy(0).start()
    for copy in small:
        copy.start()
    state_copy(1).start()

    first = lax.broadcasted_iota(jnp.int32, (16, 128), 1) < 64
    mine = pl.ds(pl.multiple_of(me * 16, 16), 16)

    def reorder(slab):
        flat[...] = state[:, :, lanes(slab)].astype(F32).reshape(256, 128)
        for c in range(CHUNKS):
            even = flat[pl.ds(2 * c, 16, stride=16), :]
            odd = flat[pl.ds(2 * c + 1, 16, stride=16), :]
            packed[2 * slab, c] = jnp.where(first, even, pltpu.roll(odd, 64, 1)).astype(BF16)
            packed[2 * slab + 1, c] = jnp.where(first, pltpu.roll(even, 64, 1), odd).astype(BF16)

    def in_copy(phase, target):
        return pltpu.make_async_remote_copy(
            src_ref=packed.at[block_of(phase, target)],
            dst_ref=recv.at[phase, :, mine, :],
            send_sem=in_s.at[phase],
            recv_sem=in_r.at[phase],
            device_id={"mem": target},
            device_id_type=MESH,
        )

    def in_all(phase):
        others = recv.at[phase, :, pl.ds(0, K - 16), :]
        return pltpu.make_async_remote_copy(
            src_ref=others,
            dst_ref=others,
            send_sem=in_s.at[phase],
            recv_sem=in_r.at[phase],
            device_id={"mem": sibling},
            device_id_type=MESH,
        )

    def in_wait(phase):
        in_all(phase).wait_recv()

    half = me // 8

    def obs_target(j):
        block = 2 * me + j
        return jnp.where(half == 0, block, 2 * NMEM - 1 - block)

    def obs_copy(j):
        return pltpu.make_async_remote_copy(
            src_ref=obs_send.at[j],
            dst_ref=obs_recv.at[half],
            send_sem=obs_s.at[j],
            recv_sem=obs_r.at[half],
            device_id={"mem": obs_target(j)},
            device_id_type=MESH,
        )

    def obs_far(j):
        return obs_target(j) != me

    def first_in(step, carry):
        slab = slab_of(step)
        reorder(slab)
        for core in range(2):
            target = 2 * slab + core
            pl.when(target != me)(lambda target=target: in_copy(0, target).start())
        return carry

    with stage("barrier"):
        state_copy(0).wait()
        pass_barrier(0, NMEM - 1, region_in)
    with stage("obs_send"):
        for copy in small:
            copy.wait()
        row = lax.broadcasted_iota(jnp.int32, (8, OBS), 0)
        code = lax.broadcasted_iota(jnp.int32, (8, OBS), 1)
        away = jnp.abs(code // 3 - 1) + jnp.abs(lax.rem(code, 3) - 1)
        taper = jnp.where(away == 0, 1.0, jnp.where(away == 1, 0.5, 0.25))
        for j in range(2):
            block = jnp.where(code == 4, 1.0, 0.0)
            for i in range(5):
                block = block + jnp.where(code == near_in[0, j : j + 1, i : i + 1], taper, 0.0)
            count = jnp.broadcast_to(count_in[0:1, j : j + 1].astype(F32), (8, OBS))
            obs_send[j] = jnp.where(row == 4, count, block)
            for i, ref in enumerate((obs_in, coef_in, rinv_in)):
                obs_send[j, i : i + 1, :] = ref[0, j : j + 1, :]
            obs_send[j, 3:4, :] = site_in[0, j : j + 1, :].astype(F32)
        for j in range(2):
            pl.when(obs_far(j))(lambda j=j: obs_copy(j).start())

            @pl.when(jnp.logical_not(obs_far(j)))
            def _(j=j):
                obs_recv[half] = obs_send[j]

    def partner(away, core):
        if away == 0:
            return 2 * chip + 1 - lax.rem(me, 2)
        turned = away * (1 - 2 * lax.rem(me, 2))
        return 2 * lax.rem(chip + 8 + turned, 8) + core

    def second_in(i, wanted):
        target = partner(*i)
        at_edge = jnp.logical_or(target == 0, target == NMEM - 1)
        pl.when(at_edge if wanted else jnp.logical_not(at_edge))(lambda: in_copy(1, target).start())

    def reorder_step(slab, carry):
        reorder(slab)
        return carry

    with stage("first_in"):
        lax.fori_loop(0, 8, first_in, 0)
    with stage("second_in"):
        state_copy(1).wait()
        reorder(8)
        reorder(15)
        for i in SENDS:
            second_in(i, True)
        lax.fori_loop(9, 15, reorder_step, 0)
        recv[0, :, mine, :] = packed[me]
        recv[1, :, mine, :] = packed[block_of(1, me)]

    def code_copy(phase, side):
        if phase == 0:
            target = {"mem": right if side == 0 else left}
        else:
            target = {"reg": above if side == 0 else below}
        return pltpu.make_async_remote_copy(
            src_ref=codes.at[phase],
            dst_ref=code_recv.at[phase, side],
            send_sem=code_s.at[phase],
            recv_sem=code_r.at[phase],
            device_id=target,
            device_id_type=MESH,
        )

    def along_line(copy):
        for side in range(2):
            pl.when(jnp.logical_not(ends[1 - side]))(lambda side=side: copy(side).start())

    def sides_wait(ref, send_sem, recv_sem, sent):
        copy = pltpu.make_async_remote_copy(
            src_ref=ref,
            dst_ref=ref,
            send_sem=send_sem,
            recv_sem=recv_sem,
            device_id={"mem": sibling},
            device_id_type=MESH,
        )
        copy.wait_send() if sent else copy.wait_recv()

    def line_wait(ref_of, send_sem, recv_sem, sent):
        pl.when(ends[0])(lambda: sides_wait(ref_of(slice(1, 2)), send_sem, recv_sem, sent))
        pl.when(ends[1])(lambda: sides_wait(ref_of(slice(0, 1)), send_sem, recv_sem, sent))
        pl.when(jnp.logical_not(edge))(
            lambda: sides_wait(ref_of(slice(0, 2)), send_sem, recv_sem, sent)
        )

    def code_wait(phase, sent):
        if phase == 0:
            line_wait(lambda sides: code_recv.at[0, sides], code_s.at[0], code_r.at[0], sent)
        else:
            sides_wait(code_recv.at[1], code_s.at[1], code_r.at[1], sent)

    with stage("onehot"):
        for phase in range(2):
            source = block_of(phase, me) // 2

            @pl.when(source != me)
            def _(phase=phase, source=source):
                pltpu.make_async_remote_copy(
                    src_ref=obs_send.at[0],
                    dst_ref=obs_recv.at[phase],
                    send_sem=obs_s.at[0],
                    recv_sem=obs_r.at[phase],
                    device_id={"mem": source},
                    device_id_type=MESH,
                ).wait_recv()

            row, column = (lax.broadcasted_iota(jnp.int32, (16, 128), axis) for axis in range(2))
            weights = jnp.where(row - CODE_ROW == column, obs_recv[phase, 5:6, 0:128], 0.0)
            codes[phase] = jnp.broadcast_to(jnp.sum(weights, axis=1, keepdims=True), (16, 128))
            if phase == 0:
                along_line(lambda side: code_copy(0, side))
            site = obs_recv[phase, 3:4, :].astype(jnp.int32)
            for c in range(CHUNKS):
                place = lax.broadcasted_iota(jnp.int32, (128, OBS), 0) + c * 128
                onehot[phase, c * 128 : (c + 1) * 128, :] = jnp.where(place == site, 1.0, 0.0).astype(BF16)

    with stage("second_out"):
        for i in SENDS[:EARLY]:
            second_in(i, False)
    with stage("adjacent"):
        pass_barrier(1, 4, adjacent_in)
        for side in range(2):
            code_copy(1, side).start()

    def observe(phase, part_done):
        values = jnp.concatenate([recv[phase, c] for c in range(CHUNKS)], axis=1)
        predicted = dot(values, onehot[phase]) * obs_recv[phase, 1:2, :]
        mean_pred = jnp.sum(predicted, axis=0, keepdims=True) * (1.0 / K)
        slot = lax.broadcasted_iota(jnp.int32, (1, OBS), 1).astype(F32)
        root = jnp.where(slot < obs_recv[phase, 4:5, :], jnp.sqrt(obs_recv[phase, 2:3, :]), 0.0)
        scaled = (root * (predicted - mean_pred)).astype(BF16)
        misfit = root * (obs_recv[phase, 0:1, :] - mean_pred)
        gram = dot_nt(scaled, scaled)
        row, column = square_indices(128)
        upper, lower = gram[:128, :128], gram[128:, 128:]
        cut = jnp.where(row <= column, upper, lower)
        own[phase, 0:128, :] = cut
        gmsg[phase, 0:128, :] = cut.astype(BF16)
        part_done(0)
        diagonal = jnp.sum(jnp.where(row == column, lower, 0.0), axis=0, keepdims=True)
        a = misfit.astype(BF16).astype(F32)
        b = (misfit - a).astype(BF16).astype(F32)
        parts = rows_of([a, b, misfit - a - b], 16).astype(BF16)
        drive = jnp.sum(dot_nt(parts, scaled), axis=0, keepdims=True)
        own[phase, 128:256, :] = gram[:128, 128:]
        gmsg[phase, 128:256, :] = gram[:128, 128:].astype(BF16)
        zero = jnp.zeros((1, 128), F32)
        tail = rows_of([drive[:, :128], drive[:, 128:], zero, zero, diagonal], MSG - PACK)
        own[phase, PACK:MSG, :] = tail
        gmsg[phase, PACK:MSG, :] = tail_rows(tail)
        part_done(1)

    def y_copy(phase, side, part):
        rows = slice(*PARTS[part])
        return pltpu.make_async_remote_copy(
            src_ref=ysend.at[side, rows] if phase == 0 else gmsg.at[1, rows],
            dst_ref=yrecv.at[phase, side, rows],
            send_sem=y_s.at[phase],
            recv_sem=y_r.at[phase, part],
            device_id={"mem": right if side == 0 else left},
            device_id_type=MESH,
        )

    def y_wait(phase, rows, part, sent):
        line_wait(
            lambda sides: yrecv.at[phase, sides, rows], y_s.at[phase], y_r.at[phase, part], sent
        )

    def y_start(part):
        along_line(lambda side: y_copy(1, side, part))

    def x_start(part):
        for side in range(2):
            x_copy(0, side, part).start()

    def x_copy(phase, side, part):
        rows = slice(*PARTS[part])
        return pltpu.make_async_remote_copy(
            src_ref=gmsg.at[0, rows] if phase == 0 else xsend.at[side, rows],
            dst_ref=xrecv.at[phase, side, rows],
            send_sem=x_s.at[phase],
            recv_sem=x_r.at[part if phase == 0 else 2],
            device_id={"reg": above if side == 0 else below},
            device_id_type=MESH,
        )

    def x_wait(phase, rows, part, sent):
        sides_wait(xrecv.at[phase, :, rows], x_s.at[phase], x_r.at[part if phase == 0 else 2], sent)

    def turn_copy(side):
        return pltpu.make_async_remote_copy(
            src_ref=gmsg.at[1],
            dst_ref=turned.at[side],
            send_sem=turn_s,
            recv_sem=turn_r,
            device_id={"reg": above if side == 0 else below},
            device_id_type=MESH,
        )

    def center_state(phase):
        for c in range(CHUNKS):
            values = recv[phase, c].astype(F32)
            average = jnp.sum(values, axis=0, keepdims=True) * (1.0 / K)
            mean[phase, :, c * 128 : (c + 1) * 128] = jnp.broadcast_to(average, (8, 128))
            spread[phase, :, c * 128 : (c + 1) * 128] = (values - average).astype(BF16)

    def weighted(weights, seen, terms, rows):
        total = None
        for code, term in zip(seen, terms):
            term = weights[CODE_ROW + code : CODE_ROW + code + 1, :] * term[rows, :].astype(F32)
            total = term if total is None else total + term
        return total

    def part_sum(target, weights, seen, terms, part):
        rows = slice(part * 128, (part + 1) * 128)
        target[rows, :] = weighted(weights, seen, terms, rows).astype(BF16)
        if part == len(PARTS) - 1:
            target[PACK:MSG, :] = tail_rows(weighted(weights, seen, terms, slice(PACK, MSG)))

    def keep_turn(side):
        yrecv[1, side] = gmsg[0]

    def sum_column():
        code_wait(0, False)
        terms = (xrecv.at[0, 0], own.at[0], xrecv.at[0, 1])
        for part in range(len(PARTS)):
            x_wait(0, slice(*PARTS[part]), part, False)
            for side in range(2):
                seen = (0, 3, 6) if side == 0 else (2, 5, 8)

                @pl.when(jnp.logical_not(ends[1 - side]))
                def _(side=side, seen=seen):
                    part_sum(ysend.at[side], code_recv[0, 1 - side], seen, terms, part)
                    y_copy(0, side, part).start()

        center[0] = weighted(codes[0], (1, 4, 7), terms, slice(0, MSG))

    def sum_turn():
        sides_wait(turned, turn_s, turn_r, False)
        terms = (turned.at[0], own.at[1], turned.at[1])
        for side in range(2):

            @pl.when(ends[side])
            def _(side=side):
                for part in range(len(PARTS)):
                    seen = (0, 3, 6) if side == 0 else (2, 5, 8)
                    part_sum(yrecv.at[0, side], codes[0], seen, terms, part)

    def sum_row():
        code_wait(1, False)
        terms = (yrecv.at[1, 1], own.at[1], yrecv.at[1, 0])
        for part in range(len(PARTS)):
            y_wait(1, slice(*PARTS[part]), part, False)
            for side in range(2):
                seen = (0, 1, 2) if side == 0 else (6, 7, 8)
                part_sum(xsend.at[side], code_recv[1, 1 - side], seen, terms, part)
                x_copy(1, side, part).start()
        center[1] = weighted(codes[1], (3, 4, 5), terms, slice(0, MSG))

    def transform(phase):
        sides = yrecv if phase == 0 else xrecv
        total = center[phase] + sides[phase, 0].astype(F32) + sides[phase, 1].astype(F32)
        tail = total[PACK:MSG]
        drive = jnp.concatenate([tail[0:1] + tail[2:3], tail[1:2] + tail[3:4]], axis=1)
        row, column = square_indices(128)
        corner, cut = total[128:256], total[0:128]
        turned = cut.T
        first_block = jnp.where(row <= column, cut, turned) + jnp.where(row == column, K - 1.0, 0.0)
        last_block = jnp.where(row == column, tail[4:5] + (K - 1.0), jnp.where(row > column, cut, turned))
        system = jnp.concatenate(
            [
                jnp.concatenate([first_block, corner], axis=1),
                jnp.concatenate([corner.T, last_block], axis=1),
            ],
            axis=0,
        )
        scale = jnp.max(jnp.sum(jnp.abs(system), axis=0, keepdims=True), axis=1, keepdims=True)
        level, rest, rounded_rest = newton_root(system * (1.0 / scale))
        row, column = square_indices(K)
        root = jnp.where(row == column, level + rest, rest)
        high_row = lax.broadcasted_iota(jnp.int32, (16, K), 0) == 0
        low_row = lax.broadcasted_iota(jnp.int32, (16, K), 0) == 1
        vector = drive * (1.0 / scale)
        for _ in range(2):
            high = vector.astype(BF16).astype(F32)
            parts = jnp.where(high_row, high, jnp.where(low_row, vector - high, 0.0)).astype(BF16)
            vector = level * vector + jnp.sum(dot(parts, rounded_rest), axis=0, keepdims=True)
        return (root * (jnp.float32(K - 1.0) ** 0.5 / jnp.sqrt(scale)) + vector).astype(BF16)

    def apply(phase, weights):
        for c in range(0, CHUNKS, 2):
            columns = slice(c * 128, (c + 2) * 128)
            result = dot(weights, spread[phase, :, columns]) + mean[phase, 0:1, columns]
            update[phase, c] = result[:, :128].astype(BF16)
            update[phase, c + 1] = result[:, 128:].astype(BF16)

    def out_copy(phase, target):
        rows = pl.ds(pl.multiple_of(target * 16, 16), 16)
        return pltpu.make_async_remote_copy(
            src_ref=update.at[phase, :, rows, :],
            dst_ref=returned.at[phase, me],
            send_sem=out_s.at[phase],
            recv_sem=out_r.at[8 if phase == 0 else chip],
            device_id={"mem": target},
            device_id_type=MESH,
        )

    def send_out(phase, offsets):
        for i in offsets:
            out_copy(phase, partner(*i)).start()

    def keep_own(phase):
        returned[phase, me] = update[phase, :, mine, :]

    def result_copy(slab):
        return pltpu.make_async_copy(
            ordered.at[:, :, lanes(slab)], out_hbm.at[:, :, lanes(slab)], result_s
        )

    def order_back(phase):
        def arrived(blocks, index):
            blocks = returned.at[phase, blocks]
            sides_wait(blocks, out_s.at[phase], out_r.at[index], False)

        if phase == 0:
            arrived(slice(0, NMEM - 1), 8)

        def one(step, carry):
            source_chip = lax.rem(16 - slab_of(step) + 2 * chip, 8)
            if phase == 1:
                pl.when(source_chip != chip)(lambda: arrived(pl.ds(2 * source_chip, 2), source_chip))
                pl.when(source_chip == chip)(lambda: arrived(pl.ds(sibling, 1), source_chip))
            for c in range(CHUNKS):
                a = returned[phase, 2 * source_chip + phase, c].astype(F32)
                b = returned[phase, 2 * source_chip + 1 - phase, c].astype(F32)
                flat[pl.ds(2 * c, 16, stride=16), :] = jnp.where(first, a, pltpu.roll(b, 64, 1))
                flat[pl.ds(2 * c + 1, 16, stride=16), :] = jnp.where(first, pltpu.roll(a, 64, 1), b)
            slab = source_chip if phase == 0 else 15 - source_chip
            ordered[:, :, lanes(slab)] = flat[...].reshape(16, 16, 128).astype(BF16)
            result_copy(slab).start()
            return carry

        lax.fori_loop(0, 8, one, 0)

    with stage("in_wait0"):
        in_wait(0)
    with stage("observe0"):
        observe(0, x_start)
        for i in SENDS[EARLY:]:
            second_in(i, False)
    with stage("edge"):

        @pl.when(edge)
        def _():
            in_wait(1)
            observe(1, y_start)
            for side in range(2):
                turn_copy(side).start()
                pl.when(ends[side])(lambda side=side: keep_turn(side))

    with stage("center0"):
        center_state(0)
    with stage("sum_column"):
        sum_column()
    with stage("in_wait1"):
        pl.when(jnp.logical_not(edge))(lambda: in_wait(1))
    with stage("observe1"):

        @pl.when(jnp.logical_not(edge))
        def _():
            observe(1, y_start)

    with stage("sum_turn"):
        pl.when(edge)(sum_turn)
    with stage("y_wait0"):
        for part in range(len(PARTS)):
            y_wait(0, slice(*PARTS[part]), part, False)
    with stage("transform0"):
        weights = transform(0)
    with stage("apply0"):
        apply(0, weights)
    send_out(0, SENDS)
    with stage("sum_row1"):
        sum_row()
    with stage("center1"):
        keep_own(0)
        center_state(1)
    with stage("x_wait1"):
        x_wait(1, slice(0, MSG), 0, False)
    with stage("transform1"):
        weights = transform(1)
    with stage("apply1"):
        apply(1, weights)
    send_out(1, SENDS)
    keep_own(1)
    with stage("sent"):
        for phase in range(2):
            in_all(phase).wait_send()
            y_wait(phase, slice(0, MSG), 0, True)
            x_wait(phase, slice(0, MSG), 0, True)
            code_wait(phase, True)
        pl.when(edge)(lambda: sides_wait(turned, turn_s, turn_r, True))
        for j in range(2):
            pl.when(obs_far(j))(lambda j=j: obs_copy(j).wait_send())
    with stage("back0"):
        order_back(0)
    with stage("back1"):
        order_back(1)

    with stage("drain"):
        for phase in range(2):
            others = update.at[phase, :, pl.ds(0, K - 16), :]
            pltpu.make_async_remote_copy(
                src_ref=others,
                dst_ref=others,
                send_sem=out_s.at[phase],
                recv_sem=out_r.at[chip],
                device_id={"mem": sibling},
                device_id_type=MESH,
            ).wait_send()
        pltpu.make_async_copy(ordered, out_hbm, result_s).wait()


def hand_over(in_ref, out_ref):
    out_ref[...] = in_ref[...]


def per_device(background, observations, obs_coef, obs_rinv, obs_site, obs_count, neighbours):
    dma = pltpu.SemaphoreType.DMA
    small = (observations, obs_coef, obs_rinv, obs_site, obs_count, neighbours)
    ordered = pl.pallas_call(
        kernel,
        out_shape=jax.ShapeDtypeStruct(background.shape, BF16),
        in_specs=[pl.BlockSpec(memory_space=pltpu.HBM)] * 7,
        out_specs=pl.BlockSpec(memory_space=pl.ANY),
        scratch_shapes=[
            pltpu.VMEM(background.shape, BF16),
            *(pltpu.VMEM(array.shape, array.dtype) for array in small),
            pltpu.VMEM((256, 128), F32),
            pltpu.VMEM((2 * NMEM, CHUNKS, 16, 128), BF16),
            pltpu.VMEM((2, CHUNKS, K, 128), BF16),
            pltpu.VMEM((2, 8, OBS), F32),
            pltpu.VMEM((2, 8, OBS), F32),
            pltpu.VMEM((2, 16, 128), F32),
            pltpu.VMEM((2, 2, 16, 128), F32),
            pltpu.VMEM((2, CHUNKS * 128, OBS), BF16),
            pltpu.VMEM((2, MSG, 128), F32),
            pltpu.VMEM((2, MSG, 128), BF16),
            pltpu.VMEM((2, MSG, 128), BF16),
            pltpu.VMEM((2, 2, MSG, 128), BF16),
            pltpu.VMEM((2, MSG, 128), F32),
            pltpu.VMEM((2, MSG, 128), BF16),
            pltpu.VMEM((2, 2, MSG, 128), BF16),
            pltpu.VMEM((2, MSG, 128), BF16),
            pltpu.VMEM((2, K, CHUNKS * 128), BF16),
            pltpu.VMEM((2, 8, CHUNKS * 128), F32),
            pltpu.VMEM((2, CHUNKS, K, 128), BF16),
            pltpu.VMEM((2, NMEM, CHUNKS, 16, 128), BF16),
            pltpu.VMEM(background.shape, BF16),
            pltpu.SemaphoreType.REGULAR, pltpu.SemaphoreType.REGULAR,
            dma((2,)), dma((6,)),
            dma((2,)), dma((2,)),
            dma((2,)), dma((2,)),
            dma((2,)), dma((2,)),
            dma((2,)), dma((2, len(PARTS))),
            dma((2,)), dma((3,)),
            dma, dma,
            dma((2,)), dma((9,)),
            dma,
        ],
        compiler_params=pltpu.CompilerParams(
            collective_id=0, has_side_effects=True, vmem_limit_bytes=62 << 20
        ),
        name="analysis",
    )(background, *small)
    half = pl.BlockSpec((8, 16, background.shape[2]), lambda i: (i, 0, 0))
    return pl.pallas_call(
        hand_over,
        grid=(2,),
        out_shape=jax.ShapeDtypeStruct(background.shape, BF16),
        in_specs=[half],
        out_specs=half,
        compiler_params=pltpu.CompilerParams(vmem_limit_bytes=60 << 20),
        name="hand_over",
    )(ordered)


def solution(mesh):
    in_specs = (
        P("mem", None, "reg"),
        P("reg", "mem", None),
        P("reg", "mem", None),
        P("reg", "mem", None),
        P("reg", "mem", None),
        P("reg", "mem"),
        P("reg", "mem", None),
    )
    out_specs = P("mem", None, "reg")
    return jax.shard_map(
        per_device, mesh=mesh, in_specs=in_specs, out_specs=out_specs, check_vma=False
    )
```
